512 devices in a mesh: ctx: 64 (over y, z), head: 8 (over x, core).
Axes of the slice: x: 4, y: 8, z: 8, core: 2. Of those that a mesh axis runs over, the one named last changes fastest.
Arguments:
- g_conv: bfloat16 [1536, 16384], P('head', 'ctx'), may hold values from -6 to 6
- pre: bfloat16 [2, 1536, 16384], P(None, 'head', 'ctx'), may hold values from -6 to 6
- kernel: float32 [31, 1536], P(None, 'head'), may hold values from -1 to 1
- w_point: bfloat16 [2, 1536, 1536], P(None, 'head'), may hold values from -0.15625 to 0.15625
- g_out: bfloat16 [1536, 16384], P('head', 'ctx'), may hold values from -6 to 6
- w_out: bfloat16 [1536, 1536], P('head'), may hold values from -0.15625 to 0.15625
- queries: bfloat16 [16384, 1536], P('ctx', 'head'), may hold values from -24 to 24
- keys: bfloat16 [16384, 1536], P('ctx', 'head'), may hold values from -24 to 24
- values: bfloat16 [16384, 1536], P('ctx', 'head'), may hold values from -6 to 6
- block_mask: int32 [128, 4, 2], P('ctx'), may hold values from 0 to 1
- counts: int32 [64], P('ctx'), may hold values from 1 to 256, 12288 in all
Outputs:
- stream_grad: bfloat16 [16384, 1536], P('ctx', 'head')
- grad_queries: bfloat16 [16384, 1536], P('ctx', 'head')
- grad_keys: bfloat16 [16384, 1536], P('ctx', 'head')
- grad_values: bfloat16 [16384, 1536], P('ctx', 'head')
The draws below stay inside these ranges and needn't reach their ends.
Inputs may be any that keep to these rules, and one draw needn't show every extreme that they name: `counts`: the largest count equals 256.
All inputs are finite; a program needn't handle non-finite values. No bound on the sum of `counts` on one device may be relied on, other than what follows from the above.
Results may differ from the reference program's by a relative error of at most 0.02.
Values may be sent and summed in bfloat16 or wider, within the bound.
No kernel may reach another device: no remote copies, remote signals or barrier semaphores. Data moves between devices by JAX's collectives and lax.ppermute only.
A program may use at most 64 MiB of HBM per device.

```python
import math
import jax
import jax.numpy as jnp
import numpy as np
from jax import lax

D = 1536
HEADS = 24
HEAD_DIM = 64
KW = 31
LINKS = 4
FRAMES_DEV = 256
HALF = 15
SPANS = 64
FRAMES = 16384
BLOCKS_DEV = 2
NBLOCKS = 128
N_CTX = 64
N_HEAD = 8


def draw_queries(key, part):
    key = jax.random.fold_in(key, 11)
    own_part = jax.random.normal(key, (FRAMES, D), jnp.float32)
    result = own_part
    return jnp.clip(result, -24.0, 24.0).astype(jnp.bfloat16)


def draw_keys(key, part):
    key = jax.random.fold_in(key, 12)
    own_part = jax.random.normal(key, (FRAMES, D), jnp.float32)
    result = own_part
    return jnp.clip(result, -24.0, 24.0).astype(jnp.bfloat16)


def draw_block_mask(key, part):
    key = jax.random.fold_in(key, 21)
    first_key, second_key = jax.random.split(key)
    span_total = NBLOCKS // BLOCKS_DEV
    density = jax.random.randint(first_key, (span_total, 1, 1, 1), 1, 9)
    samples = jax.random.randint(second_key, (span_total, BLOCKS_DEV, LINKS, BLOCKS_DEV), 0, 8)
    return (samples < density).astype(jnp.int32).reshape(NBLOCKS, LINKS, BLOCKS_DEV)


def with_spikes(values, rng, source, target, blocks, factor):
    owner, partner = [(jnp.arange(values.shape[axis_at]) // (values.shape[axis_at] // blocks)).reshape([-1 if axis == axis_at else 1 for axis in range(values.ndim)]) for axis_at in (source, target)]
    chosen = jax.random.permutation(rng, blocks)[partner]
    strong = (owner == chosen) | (owner == (partner + blocks // 2) % blocks)
    return jnp.where(strong, factor * values, values)


def block_scale(key, shape, cuts, smallest, largest):
    level = 1.0
    for axis_at, parts in cuts:
        steps = jax.random.uniform(jax.random.fold_in(jax.random.fold_in(key, 6), axis_at), (parts,), jnp.float32, smallest / len(cuts), largest / len(cuts))
        level = level * jnp.repeat(jnp.exp(steps), shape[axis_at] // parts).reshape((-1,) + (1,) * (len(shape) - 1 - axis_at))
    return level


def profile(count, total, limit, skew):
    loads = [(1 << 20) // math.isqrt(grade ** skew) + 1 for grade in range(2, count + 1)]
    surplus, given = total - limit - (count - 1), [1] * (count - 1)
    while surplus > 0:
        free = [i for i in range(count - 1) if given[i] < limit]
        mass, remaining = sum([loads[i] for i in free]), surplus
        for i in free:
            addition = min(limit - given[i], max(1, remaining * loads[i] // mass), surplus)
            given[i] = given[i] + addition
            surplus = surplus - addition
    return np.array([limit] + given)


def ragged_sizes(stream_key, count, total, most, skew):
    if count == 2:
        one = jax.random.randint(stream_key, (), max(1, total - most), min(most, total - 1) + 1)
        return jnp.stack([one, total - one])
    tallies = jnp.asarray(profile(count, total, most, skew), jnp.int32)
    couples = (count - 1) // 2
    donor, sink = tallies[1:1 + 2 * couples:2], tallies[2:2 + 2 * couples:2]
    margin = jnp.minimum(donor - 1, most - sink)
    passed = jax.random.randint(jax.random.fold_in(stream_key, 1), (couples,), 0, 1 << 20) % (margin + 1)
    tallies = tallies.at[1:1 + 2 * couples:2].set(donor - passed).at[2:2 + 2 * couples:2].set(sink + passed)
    return tallies[jax.random.permutation(jax.random.fold_in(stream_key, 2), count)]


def gaussian(rng, extent, deviation, limit, shards=(), kind=jnp.bfloat16):
    values = jax.random.normal(rng, extent, jnp.float32) * deviation
    if len(shards) > 0:
        values = block_scale(rng, extent, shards, -0.22, 0.18) * values
    return jnp.clip(values, min=-limit, max=limit).astype(kind)


def bell_draw_with(key, shape, deviation, limit, cuts, heavy, held_as=jnp.bfloat16):
    values = deviation * jax.random.normal(key, shape, jnp.float32)
    if cuts:
        values = values * block_scale(key, shape, cuts, -0.22, 0.18)
    return jnp.clip(with_spikes(values, jax.random.fold_in(key, 3), *heavy), -limit, limit).astype(held_as)


def setup_inputs(seed: int = 0) -> dict:
    streams_of = jax.random.split(jax.random.key(seed), 12)
    g_conv = gaussian(streams_of[0], (D, FRAMES), 1.0, 6.0, ((0, 8), (1, 64)))
    pre = gaussian(streams_of[1], (2, D, FRAMES), 1.0, 6.0, ((1, 8), (2, 64)))
    kernel = gaussian(streams_of[2], (KW, D), KW ** -0.5, 1.0, ((1, 8),), jnp.float32)
    w_point = bell_draw_with(streams_of[3], (2, D, D), (2 * D) ** -0.5, 0.15625, ((1, 8),), (1, 2, 8, 2.0))
    g_out = gaussian(streams_of[4], (D, FRAMES), 1.0, 6.0, ((0, 8), (1, 64)))
    w_out = gaussian(streams_of[5], (D, D), D ** -0.5, 0.15625, ((0, 8),))
    queries = draw_queries(jax.random.fold_in(streams_of[11], 71), 0)
    keys = draw_keys(jax.random.fold_in(streams_of[11], 71), 0)
    values = gaussian(streams_of[8], (FRAMES, D), 1.0, 6.0, ((0, 64), (1, 8)))
    block_mask = draw_block_mask(jax.random.fold_in(streams_of[11], 71), 0)
    counts = ragged_sizes(streams_of[10], SPANS, FRAMES * 3 // 4, FRAMES_DEV, 2).astype(jnp.int32)
    return {"g_conv": g_conv, "pre": pre, "kernel": kernel, "w_point": w_point, "g_out": g_out, "w_out": w_out, "queries": queries, "keys": keys, "values": values, "block_mask": block_mask, "counts": counts}


def link_allowed(query_valid, key_valid, link_mask, is_local):
    blocks = link_mask > 0
    if is_local:
        blocks = blocks | jnp.eye(blocks.shape[0], dtype=bool)
    block_count = blocks.shape[0]
    width = query_valid.shape[0] // block_count
    element = jnp.broadcast_to(blocks[:, None, :, None], (block_count, width, block_count, width))
    element = element.reshape(block_count * width, block_count * width)
    return element & query_valid[:, None] & key_valid[None, :]

def reference(g_conv, pre, kernel, w_point, g_out, w_out, queries, keys, values, block_mask, counts):
    width = g_conv.shape[0]
    frames = g_conv.shape[1]
    padded = jnp.pad(g_conv.astype(jnp.float32), ((0, 0), (HALF, HALF)))
    conv_grad = jnp.zeros((width, frames), jnp.float32)
    for tap_index in range(KW):
        first_row = 2 * HALF - tap_index
        conv_grad = conv_grad + kernel[tap_index].astype(jnp.float32)[:, None] * padded[:, first_row:first_row + frames]
    pre_wide = pre.astype(jnp.float32)
    gate = jax.nn.sigmoid(pre_wide[1])
    grad_value = conv_grad * gate
    grad_gate = conv_grad * pre_wide[0] * gate * (1.0 - gate)
    pre_grad = jnp.stack([grad_value, grad_gate], axis=0).astype(jnp.bfloat16)
    group_width = width // N_HEAD
    grouped_pre = pre_grad.reshape(2, N_HEAD, group_width, frames)
    grouped_weight = w_point.reshape(2, N_HEAD, group_width, width)
    point_grad = jnp.zeros((frames, width), jnp.float32)
    for group_index in range(N_HEAD):
        left = grouped_pre[:, group_index].reshape(2 * group_width, frames)
        right = grouped_weight[:, group_index].reshape(2 * group_width, width)
        partial_sum = lax.dot_general(left, right, (((0,), (0,)), ((), ())), preferred_element_type=jnp.float32)
        partial_sum = lax.optimization_barrier(partial_sum.astype(jnp.bfloat16))
        point_grad = point_grad + partial_sum.astype(jnp.float32)
    stream_grad = (g_out.astype(jnp.float32).T + point_grad).astype(jnp.bfloat16)
    frame_index = jnp.arange(frames, dtype=jnp.int32)
    valid = frame_index % FRAMES_DEV < counts[frame_index // FRAMES_DEV]
    head_grad = jnp.dot(stream_grad, w_out.T, preferred_element_type=jnp.float32)
    head_grad = jnp.where(valid[:, None], head_grad, 0.0).astype(jnp.bfloat16)
    span_count = N_CTX
    offsets = [0, 1, -1, span_count // 2]
    score_scale = 1.0 / math.sqrt(HEAD_DIM)

    def split(array):
        return array.reshape(span_count, FRAMES_DEV, HEADS, HEAD_DIM).astype(jnp.float32)
    query_spans = split(queries)
    key_spans = split(keys)
    value_spans = split(values)
    grad_spans = split(head_grad)
    valid_spans = valid.reshape(span_count, FRAMES_DEV)
    mask_spans = block_mask.reshape(span_count, BLOCKS_DEV, LINKS, BLOCKS_DEV)

    def span_stats(index):
        query_here = query_spans[index]
        grad_here = grad_spans[index]
        allowed_list = []
        key_list = []
        value_list = []
        for link_index in range(LINKS):
            other = (index - offsets[link_index]) % span_count
            key_list.append(key_spans[other])
            value_list.append(value_spans[other])
            allowed_list.append(link_allowed(valid_spans[index], valid_spans[other], mask_spans[index][:, link_index, :], link_index == 0))
        key_all = jnp.concatenate(key_list, axis=0)
        value_all = jnp.concatenate(value_list, axis=0)
        allowed = jnp.concatenate(allowed_list, axis=1)
        scores = jnp.einsum('qhd,khd->hqk', query_here, key_all) * score_scale
        row_max = lax.optimization_barrier(jnp.max(jnp.where(allowed[None], scores, -1e+30), axis=-1))
        expo = jnp.where(allowed[None], jnp.exp(scores - row_max[..., None]), 0.0)
        row_sum = lax.optimization_barrier(jnp.sum(expo, axis=-1)) + (1.0 - valid_spans[index].astype(jnp.float32))[None, :]
        probs = expo / row_sum[..., None]
        dprob = jnp.einsum('qhd,khd->hqk', grad_here, value_all)
        row_delta = lax.optimization_barrier(jnp.sum(probs * dprob, axis=-1))
        dscore = (probs * (dprob - row_delta[..., None])).astype(jnp.bfloat16)
        grad_query = jnp.einsum('hqk,khd->qhd', dscore.astype(jnp.float32), key_all) * score_scale
        return (grad_query, row_max, row_sum, row_delta)
    span_ids = jnp.arange(span_count, dtype=jnp.int32)
    grad_query, row_max, row_sum, row_delta = lax.map(span_stats, span_ids)
    key_total = jnp.zeros((span_count, FRAMES_DEV, HEADS, HEAD_DIM), jnp.float32)
    value_total = jnp.zeros((span_count, FRAMES_DEV, HEADS, HEAD_DIM), jnp.float32)
    for link_index in range(LINKS):
        offset = offsets[link_index]

        def span_terms(index):
            other = (index - offset) % span_count
            allowed = link_allowed(valid_spans[index], valid_spans[other], mask_spans[index][:, link_index, :], link_index == 0)
            scores = jnp.einsum('qhd,khd->hqk', query_spans[index], key_spans[other]) * score_scale
            probs = jnp.where(allowed[None], jnp.exp(scores - row_max[index][..., None]) / row_sum[index][..., None], 0.0)
            dprob = jnp.einsum('qhd,khd->hqk', grad_spans[index], value_spans[other])
            dscore = (probs * (dprob - row_delta[index][..., None])).astype(jnp.bfloat16)
            probs_low = probs.astype(jnp.bfloat16)
            key_term = jnp.einsum('hqk,qhd->khd', dscore.astype(jnp.float32), query_spans[index]) * score_scale
            value_term = jnp.einsum('hqk,qhd->khd', probs_low.astype(jnp.float32), grad_spans[index])
            return (key_term, value_term)
        key_term, value_term = lax.map(span_terms, span_ids)
        key_total = key_total + jnp.roll(key_term, -offset, axis=0)
        value_total = value_total + jnp.roll(value_term, -offset, axis=0)
    grad_queries = grad_query.reshape(frames, width).astype(jnp.bfloat16)
    grad_keys = key_total.reshape(frames, width).astype(jnp.bfloat16)
    grad_values = value_total.reshape(frames, width).astype(jnp.bfloat16)
    return (stream_grad, grad_queries, grad_keys, grad_values)
```

```python
import functools
import math

import jax
import jax.numpy as jnp
from jax import lax
from jax.experimental import pallas as pl
from jax.experimental.pallas import tpu as pltpu
from jax.sharding import PartitionSpec as P

HEAD_DIM = 64
KW = 31
LINKS = 4
HALF = 15
LANES = 128
META = 16
NEG = -1e30
SCALE = 1.0 / math.sqrt(HEAD_DIM)
SCALE2 = SCALE * math.log2(math.e)
MIRROR = (0, 2, 1, 3)
VMEM = pl.BlockSpec(memory_space=pltpu.VMEM)
HBM = pl.BlockSpec(memory_space=pltpu.HBM)
SMEM = pl.BlockSpec(memory_space=pltpu.SMEM)
F32 = jnp.float32
BF16 = jnp.bfloat16


def call(body, out_shapes, args, specs, flops, moved, exps=0, scratch=()):
    return pl.pallas_call(
        body,
        out_shape=out_shapes,
        in_specs=specs,
        out_specs=jax.tree.map(lambda _: VMEM, out_shapes),
        scratch_shapes=list(scratch),
        compiler_params=pltpu.CompilerParams(vmem_limit_bytes=24 * 1024 * 1024),
        cost_estimate=pl.CostEstimate(flops=flops, bytes_accessed=moved, transcendentals=exps),
    )(*args)


def dot_tn(a, b):
    return lax.dot_general(a, b, (((0,), (0,)), ((), ())), preferred_element_type=F32)


def dot_nt(a, b):
    return lax.dot_general(a, b, (((1,), (1,)), ((), ())), preferred_element_type=F32)


def dot_nn(a, b):
    return lax.dot_general(a, b, (((1,), (0,)), ((), ())), preferred_element_type=F32)


def prep_body(
    mask_ref,
    count_ref,
    keys_ref,
    values_ref,
    queries_ref,
    g_ref,
    pre_ref,
    taps_ref,
    w_ref,
    out_ref,
    conv_ref,
    gate_ref,
    taps_out,
    w_out,
    x_ref,
    g_low,
    pre_low,
    taps_low,
    w_low,
    sems,
):
    columns, rows = keys_ref.shape
    copies = [
        pltpu.make_async_copy(g_ref, g_low, sems.at[0]),
        pltpu.make_async_copy(taps_ref, taps_low, sems.at[1]),
        pltpu.make_async_copy(pre_ref, pre_low, sems.at[2]),
        pltpu.make_async_copy(w_ref, w_low, sems.at[3]),
        pltpu.make_async_copy(keys_ref, out_ref.at[pl.ds(0, columns)], sems.at[4]),
        pltpu.make_async_copy(values_ref, out_ref.at[pl.ds(columns, columns)], sems.at[5]),
        pltpu.make_async_copy(queries_ref, out_ref.at[pl.ds(2 * columns, columns)], sems.at[6]),
    ]
    for copy in copies:
        copy.start()
    row = lax.broadcasted_iota(jnp.int32, (META, rows), 0)
    first = lax.broadcasted_iota(jnp.int32, (META, rows), 1) < rows // 2
    meta = jnp.where(row == 0, count_ref[0].astype(F32), 0.0)
    for j in range(LINKS):
        for kb in range(2):
            picked = []
            for qb in range(2):
                bit = (mask_ref[qb, j, kb] > 0).astype(F32)
                if j == 0 and qb == kb:
                    bit = jnp.maximum(bit, 1.0)
                picked.append(bit)
            meta = jnp.where(row == 1 + 2 * j + kb, jnp.where(first, picked[0], picked[1]), meta)
    out_ref[3 * columns :, :] = meta.astype(BF16)
    copies[0].wait()
    x_ref[:, 0:LANES] = jnp.zeros((columns, LANES), F32)
    x_ref[:, LANES : LANES + rows] = g_low[...].astype(F32)
    x_ref[:, LANES + rows :] = jnp.zeros((columns, LANES), F32)
    copies[1].wait()
    taps = jnp.concatenate([taps_low[...], jnp.zeros((LANES - KW, columns), F32)], axis=0)
    taps_out[...] = taps.T
    copies[2].wait()
    step = 32

    def block(i, carry):
        at = pl.ds(pl.multiple_of(i * step, step), step)
        x = x_ref[at, :]
        wide = x.shape[1]
        moved = [pltpu.roll(x, (16 - 8 * a) % wide, 1)[:, LANES:] for a in range(4)]
        acc = jnp.zeros((step, wide - LANES), F32)
        for b in range(8):
            part = 0.0
            for a in range(4):
                k = 31 - 8 * a - b
                if k < KW:
                    part = part + taps_out[at, k : k + 1] * moved[a]
            acc = acc + (pltpu.roll(part, wide - LANES - b, 1) if b else part)
        conv_ref[at, :] = acc[:, :rows]
        value = pre_low[0, at, :].astype(F32)
        gate = jax.nn.sigmoid(pre_low[1, at, :].astype(F32))
        gate_ref[0, at, :] = gate
        gate_ref[1, at, :] = value * gate * (1.0 - gate)
        return carry

    lax.fori_loop(0, columns // step, block, 0)
    copies[3].wait()
    model = w_ref.shape[1]
    for at in range(0, model, LANES):
        w_out[at : at + LANES, :] = w_low[:, at : at + LANES].T
    for copy in copies[4:]:
        copy.wait()


def meta_of(ref, columns):
    return ref[3 * columns : 3 * columns + META, :].astype(F32)


def limits(query_meta, key_count, link):
    lane = lax.broadcasted_iota(jnp.int32, query_meta[0:1].shape, 1).astype(F32)
    valid = lane < query_meta[0:1]
    return [
        jnp.where(valid & (query_meta[1 + 2 * link + kb : 2 + 2 * link + kb] > 0.5), key_count, 0.0)
        for kb in range(2)
    ]


def masked(scores, limit_rows):
    rows = scores.shape[0]
    half = rows // 2
    parts = []
    for kb in range(2):
        index = lax.broadcasted_iota(jnp.int32, (half, scores.shape[1]), 0).astype(F32) + kb * half
        parts.append(
            jnp.where(index < limit_rows[kb], scores[kb * half : (kb + 1) * half], NEG)
        )
    return jnp.concatenate(parts, axis=0)


def conv_body(columns, before_ref, after_ref, conv_ref, gate_ref, taps_ref, w_ref, out_ref, low_ref):
    rows = conv_ref.shape[1]
    step = 64
    for at in range(0, columns, step):
        here = slice(at, at + step)
        lane = lax.broadcasted_iota(jnp.int32, (step, LANES), 1)
        before = jnp.where(lane >= LANES - HALF, before_ref[here, rows - LANES :].astype(F32), 0.0)
        after = jnp.where(lane < HALF, after_ref[here, :LANES].astype(F32), 0.0)
        left = jnp.zeros((step, LANES), F32)
        right = jnp.zeros((step, LANES), F32)
        for m in range(1, HALF + 1):
            left = left + taps_ref[here, HALF + m : HALF + m + 1] * pltpu.roll(before, m, 1)
            right = right + taps_ref[here, HALF - m : HALF - m + 1] * pltpu.roll(after, LANES - m, 1)
        left = jnp.where(lane < HALF, left, 0.0)
        right = jnp.where(lane >= LANES - HALF, right, 0.0)
        grad = conv_ref[here, :] + jnp.concatenate([left, right], axis=1)
        low_ref[here, :] = (grad * gate_ref[0, here, :]).astype(BF16)
        low_ref[columns + at : columns + at + step, :] = (grad * gate_ref[1, here, :]).astype(BF16)
    model = w_ref.shape[0]
    chunk = 256 if model % 256 == 0 else LANES
    low = low_ref[...]
    for at in range(0, model, chunk):
        out_ref[at : at + chunk, :] = dot_nn(w_ref[at : at + chunk, :], low).astype(BF16)


def softmax_of(refs, own_meta, columns, links, h, top):
    lo, hi = h * HEAD_DIM, (h + 1) * HEAD_DIM
    query = refs[0][2 * columns + lo : 2 * columns + hi, :]
    scores = []
    for ref, link in zip(refs[1:], links):
        limit = limits(own_meta, meta_of(ref, columns)[0:1], link)
        scores.append(masked(dot_tn(ref[lo:hi, :], query) * SCALE2, limit))
    top = functools.reduce(jnp.maximum, [jnp.max(s, axis=0, keepdims=True) for s in scores], top)
    total = jnp.zeros_like(top)
    mixed = jnp.zeros((HEAD_DIM, top.shape[1]), F32)
    for ref, score in zip(refs[1:], scores):
        expo = jnp.exp2(score - top)
        total = total + jnp.sum(expo, axis=0, keepdims=True)
        mixed = mixed + dot_nn(ref[columns + lo : columns + hi, :], expo.astype(BF16))
    return top, total, mixed


def softmax_body(columns, own_ref, one_ref, two_ref, out_ref):
    own_meta = meta_of(own_ref, columns)
    heads = columns // HEAD_DIM
    start = jnp.full(own_meta[0:1].shape, NEG, F32)
    out_ref[columns:, :] = jnp.zeros((8, own_ref.shape[1]), F32)
    for h in range(heads):
        top, total, mixed = softmax_of(
            (own_ref, own_ref, one_ref, two_ref), own_meta, columns, (0, 1, 2), h, start
        )
        out_ref[h * HEAD_DIM : (h + 1) * HEAD_DIM, :] = mixed
        out_ref[columns + h : columns + h + 1, :] = top
        out_ref[columns + heads + h : columns + heads + h + 1, :] = total


def pieces(value, count):
    found = []
    for _ in range(count):
        low = value.astype(BF16).astype(F32)
        found.append(low)
        value = value - low
    return found


def grad_body(columns, w_ref, stream_ref, own_ref, far_ref, soft_ref, out_ref):
    head_grad = dot_nn(w_ref[...], stream_ref[...])
    own_meta = meta_of(own_ref, columns)
    heads = columns // HEAD_DIM
    lane = lax.broadcasted_iota(jnp.int32, own_meta[0:1].shape, 1).astype(F32)
    valid = lane < own_meta[0:1]
    low = jnp.where(valid, head_grad, 0.0).astype(BF16)
    out_ref[0:columns, :] = low
    rows = []
    for h in range(heads):
        lo, hi = h * HEAD_DIM, (h + 1) * HEAD_DIM
        old_top = soft_ref[columns + h : columns + h + 1, :]
        top, total, mixed = softmax_of((own_ref, far_ref), own_meta, columns, (3,), h, old_top)
        factor = jnp.exp2(old_top - top)
        total = total + factor * soft_ref[columns + heads + h : columns + heads + h + 1, :]
        mixed = (mixed + factor * soft_ref[lo:hi, :]) / total
        delta = jnp.sum(low[lo:hi].astype(F32) * mixed, axis=0, keepdims=True)
        rows += pieces(jnp.where(valid, top + jnp.log2(total), -NEG), 3)
        rows += pieces(jnp.where(valid, delta, 0.0), 2)
    index = lax.broadcasted_iota(jnp.int32, (META, own_meta.shape[1]), 0)
    meta = jnp.zeros((META, own_meta.shape[1]), F32)
    for i, row in enumerate(rows):
        meta = jnp.where(index == i, row, meta)
    out_ref[columns:, :] = meta.astype(BF16)


def stats_of(ref, columns, h):
    meta = ref[columns : columns + META, :].astype(F32)
    at = 5 * h
    lse = (meta[at : at + 1] + meta[at + 1 : at + 2]) + meta[at + 2 : at + 3]
    delta = meta[at + 3 : at + 4] + meta[at + 4 : at + 5]
    return lse, delta


def tile(key, value, query, grad, lse, delta, limit):
    probs = jnp.exp2(masked(dot_tn(key, query) * SCALE2 - lse, limit))
    dscore = (probs * (dot_tn(value, grad) - delta)).astype(BF16)
    return probs.astype(BF16), dscore


def local_body(columns, own_ref, one_ref, two_ref, far_ref, grad_ref, query_out, acc_out):
    refs = (own_ref, one_ref, two_ref, far_ref)
    own_meta = meta_of(own_ref, columns)
    limit = [limits(own_meta, meta_of(refs[j], columns)[0:1], j) for j in range(LINKS)]
    for h in range(columns // HEAD_DIM):
        lo, hi = h * HEAD_DIM, (h + 1) * HEAD_DIM
        query = own_ref[2 * columns + lo : 2 * columns + hi, :]
        grad = grad_ref[lo:hi, :]
        lse, delta = stats_of(grad_ref, columns, h)
        total = jnp.zeros((HEAD_DIM, own_ref.shape[1]), F32)
        for j in range(LINKS):
            key = refs[j][lo:hi, :]
            value = refs[j][columns + lo : columns + hi, :]
            probs, dscore = tile(key, value, query, grad, lse, delta, limit[j])
            total = total + dot_nn(key, dscore)
            if j == 0:
                acc_out[lo:hi, :] = dot_nt(query, dscore)
                acc_out[columns + lo : columns + hi, :] = dot_nt(grad, probs)
        query_out[lo:hi, :] = (total * SCALE).astype(BF16)


def remote_terms(columns, links, own_ref, span_refs, grad_refs, h):
    lo, hi = h * HEAD_DIM, (h + 1) * HEAD_DIM
    key = own_ref[lo:hi, :]
    value = own_ref[columns + lo : columns + hi, :]
    count = meta_of(own_ref, columns)[0:1]
    key_term = value_term = 0.0
    for link, span_ref, grad_ref in zip(links, span_refs, grad_refs):
        query = span_ref[2 * columns + lo : 2 * columns + hi, :]
        grad = grad_ref[lo:hi, :]
        lse, delta = stats_of(grad_ref, columns, h)
        limit = limits(meta_of(span_ref, columns), count, link)
        probs, dscore = tile(key, value, query, grad, lse, delta, limit)
        key_term = key_term + dot_nt(query, dscore)
        value_term = value_term + dot_nt(grad, probs)
    return key_term, value_term


def near_body(columns, own_ref, one_ref, two_ref, grad_one_ref, grad_two_ref, acc_ref, acc_out):
    for h in range(columns // HEAD_DIM):
        lo, hi = h * HEAD_DIM, (h + 1) * HEAD_DIM
        key_term, value_term = remote_terms(
            columns,
            (MIRROR[1], MIRROR[2]),
            own_ref,
            (one_ref, two_ref),
            (grad_one_ref, grad_two_ref),
            h,
        )
        acc_out[lo:hi, :] = acc_ref[lo:hi, :] + key_term
        acc_out[columns + lo : columns + hi, :] = acc_ref[columns + lo : columns + hi, :] + value_term


def far_body(columns, own_ref, far_ref, grad_far_ref, acc_ref, key_out, value_out):
    for h in range(columns // HEAD_DIM):
        lo, hi = h * HEAD_DIM, (h + 1) * HEAD_DIM
        key_term, value_term = remote_terms(
            columns, (MIRROR[3],), own_ref, (far_ref,), (grad_far_ref,), h
        )
        key_out[lo:hi, :] = ((acc_ref[lo:hi, :] + key_term) * SCALE).astype(BF16)
        value_out[lo:hi, :] = (acc_ref[columns + lo : columns + hi, :] + value_term).astype(BF16)


def shifted(value, steps):
    count = lax.axis_size("ctx")
    pairs = [(source, (source + steps) % count) for source in range(count)]
    return lax.ppermute(value, "ctx", pairs)


def per_device(
    g_conv, pre, kernel, w_point, g_out, w_out, queries, keys, values, block_mask, counts
):
    columns, row_count = g_conv.shape
    model = w_point.shape[2]
    groups = lax.axis_size("head")
    spans = lax.axis_size("ctx")
    shape = jax.ShapeDtypeStruct
    queries, keys, values = (queries.T, keys.T, values.T)
    message = 3 * columns + META
    square = 2 * columns * row_count * row_count

    up = [(i, i + 1) for i in range(spans - 1)]
    before = lax.ppermute(g_conv, "ctx", up)
    after = lax.ppermute(g_conv, "ctx", [(j, i) for i, j in up])
    flat = (columns, row_count)
    own, conv, gate, taps, w_turned = call(
        prep_body,
        (
            shape((message, row_count), BF16),
            shape(flat, F32),
            shape((2,) + flat, F32),
            shape((columns, LANES), F32),
            shape((model, 2 * columns), BF16),
        ),
        (
            block_mask,
            counts,
            keys,
            values,
            queries,
            g_conv,
            pre,
            kernel,
            w_point.reshape(2 * columns, model),
        ),
        [SMEM] * 2 + [HBM] * 7,
        2 * KW * columns * row_count,
        8 * columns * model + 8 * message * row_count,
        columns * row_count,
        (
            pltpu.VMEM((columns, row_count + 2 * LANES), F32),
            pltpu.VMEM(flat, BF16),
            pltpu.VMEM((2,) + flat, BF16),
            pltpu.VMEM((KW, columns), F32),
            pltpu.VMEM((2 * columns, model), BF16),
            pltpu.SemaphoreType.DMA((7,)),
        ),
    )
    offsets = [0, 1, -1, spans // 2]
    far = shifted(own, offsets[3])
    point_grad = call(
        functools.partial(conv_body, columns),
        shape((model, row_count), BF16),
        (before, after, conv, gate, taps, w_turned),
        [VMEM] * 6,
        4 * columns * model * row_count,
        4 * columns * model,
        0,
        (pltpu.VMEM((2 * columns, row_count), BF16),),
    )
    parts = lax.all_to_all(
        point_grad.reshape(groups, columns, row_count), "head", 0, 0, tiled=False
    )
    later, _ = lax.optimization_barrier((own, point_grad))
    one, two = [shifted(later, offset) for offset in offsets[1:3]]
    soft = call(
        functools.partial(softmax_body, columns),
        shape((columns + 8, row_count), F32),
        (own, one, two),
        [VMEM] * 3,
        6 * square,
        6 * message * row_count,
        3 * columns // HEAD_DIM * row_count * row_count,
    )
    piece = jnp.sum(parts.astype(F32), axis=0)
    stream_grad = (g_out.astype(F32) + piece).astype(BF16)
    stream_full = lax.all_gather(stream_grad, "head", axis=0, tiled=True)
    grad = call(
        functools.partial(grad_body, columns),
        shape((columns + META, row_count), BF16),
        (w_out, stream_full, own, far, soft),
        [VMEM] * 5,
        2 * columns * model * row_count + 2 * square,
        2 * model * (columns + row_count),
        columns // HEAD_DIM * row_count * row_count,
    )
    grad_one, grad_two, grad_far = [shifted(grad, offset) for offset in offsets[1:]]
    grad_queries, acc = call(
        functools.partial(local_body, columns),
        (shape((columns, row_count), BF16), shape((2 * columns, row_count), F32)),
        (own, one, two, far, grad),
        [VMEM] * 5,
        3 * LINKS * square,
        8 * message * row_count,
        LINKS * columns // HEAD_DIM * row_count * row_count,
    )
    acc = call(
        functools.partial(near_body, columns),
        shape((2 * columns, row_count), F32),
        (own, one, two, grad_one, grad_two, acc),
        [VMEM] * 6,
        8 * square,
        8 * message * row_count,
        2 * columns // HEAD_DIM * row_count * row_count,
    )
    grad_keys, grad_values = call(
        functools.partial(far_body, columns),
        (shape((columns, row_count), BF16), shape((columns, row_count), BF16)),
        (own, far, grad_far, acc),
        [VMEM] * 4,
        4 * square,
        8 * message * row_count,
        columns // HEAD_DIM * row_count * row_count,
    )
    return (stream_grad.T, grad_queries.T, grad_keys.T, grad_values.T)


def solution(mesh):
    in_specs = (
        P("head", "ctx"),
        P(None, "head", "ctx"),
        P(None, "head"),
        P(None, "head", None),
        P("head", "ctx"),
        P("head", None),
        P("ctx", "head"),
        P("ctx", "head"),
        P("ctx", "head"),
        P("ctx", None, None),
        P("ctx"),
    )
    out_specs = (P("ctx", "head"), P("ctx", "head"), P("ctx", "head"), P("ctx", "head"))
    return jax.shard_map(
        per_device, mesh=mesh, in_specs=in_specs, out_specs=out_specs, check_vma=False
    )
```

```python
import functools
import math

import jax
import jax.numpy as jnp
from jax import lax
from jax.experimental import pallas as pl
from jax.experimental.pallas import tpu as pltpu
from jax.sharding import PartitionSpec as P

HEAD_DIM = 64
KW = 31
LINKS = 4
HALF = 15
LANES = 128
META = 16
BIG = 58
NEG = -1e30
SCALE = 1.0 / math.sqrt(HEAD_DIM)
SCALE2 = SCALE * math.log2(math.e)
MIRROR = (0, 2, 1, 3)
VMEM = pl.BlockSpec(memory_space=pltpu.VMEM)
HBM = pl.BlockSpec(memory_space=pltpu.HBM)
SMEM = pl.BlockSpec(memory_space=pltpu.SMEM)
F32 = jnp.float32
BF16 = jnp.bfloat16


def call(body, out_shapes, args, specs, flops, moved, exps=0, scratch=(), mib=24):
    return pl.pallas_call(
        body,
        out_shape=out_shapes,
        in_specs=specs,
        out_specs=jax.tree.map(lambda _: VMEM, out_shapes),
        scratch_shapes=list(scratch),
        compiler_params=pltpu.CompilerParams(vmem_limit_bytes=mib * 1024 * 1024),
        cost_estimate=pl.CostEstimate(flops=flops, bytes_accessed=moved, transcendentals=exps),
    )(*args)


def dot_tn(a, b):
    return lax.dot_general(a, b, (((0,), (0,)), ((), ())), preferred_element_type=F32)


def dot_nt(a, b):
    return lax.dot_general(a, b, (((1,), (1,)), ((), ())), preferred_element_type=F32)


def dot_nn(a, b):
    return lax.dot_general(a, b, (((1,), (0,)), ((), ())), preferred_element_type=F32)


def pack_body(mask_ref, count_ref, keys_ref, values_ref, queries_ref, out_ref, sems):
    columns, rows = keys_ref.shape
    copies = [
        pltpu.make_async_copy(ref, out_ref.at[pl.ds(i * columns, columns)], sems.at[i])
        for i, ref in enumerate((keys_ref, values_ref, queries_ref))
    ]
    for copy in copies:
        copy.start()
    row = lax.broadcasted_iota(jnp.int32, (META, rows), 0)
    first = lax.broadcasted_iota(jnp.int32, (META, rows), 1) < rows // 2
    meta = jnp.where(row == 0, count_ref[0].astype(F32), 0.0)
    for j in range(LINKS):
        for kb in range(2):
            picked = []
            for qb in range(2):
                bit = (mask_ref[qb, j, kb] > 0).astype(F32)
                if j == 0 and qb == kb:
                    bit = jnp.maximum(bit, 1.0)
                picked.append(bit)
            meta = jnp.where(row == 1 + 2 * j + kb, jnp.where(first, picked[0], picked[1]), meta)
    out_ref[3 * columns :, :] = meta.astype(BF16)
    for copy in copies:
        copy.wait()


def own_conv_body(
    g_ref, pre_ref, taps_ref, conv_ref, gate_ref, taps_out, x_ref, g_low, pre_low, taps_low, sems
):
    columns, rows = g_ref.shape
    copies = [
        pltpu.make_async_copy(g_ref, g_low, sems.at[0]),
        pltpu.make_async_copy(taps_ref, taps_low, sems.at[1]),
        pltpu.make_async_copy(pre_ref, pre_low, sems.at[2]),
    ]
    for copy in copies:
        copy.start()
    x_ref[:, 0:LANES] = jnp.zeros((columns, LANES), F32)
    x_ref[:, LANES + rows :] = jnp.zeros((columns, LANES), F32)
    for copy in copies:
        copy.wait()
    x_ref[:, LANES : LANES + rows] = g_low[...].astype(F32)
    taps = jnp.concatenate([taps_low[...], jnp.zeros((LANES - KW, columns), F32)], axis=0)
    taps_out[...] = taps.T
    step = 32

    def block(i, carry):
        at = pl.ds(pl.multiple_of(i * step, step), step)
        x = x_ref[at, :]
        wide = x.shape[1]
        moved = [pltpu.roll(x, (16 - 8 * a) % wide, 1)[:, LANES:] for a in range(4)]
        acc = jnp.zeros((step, wide - LANES), F32)
        for b in range(8):
            part = 0.0
            for a in range(4):
                k = 31 - 8 * a - b
                if k < KW:
                    part = part + taps_out[at, k : k + 1] * moved[a]
            acc = acc + (pltpu.roll(part, wide - LANES - b, 1) if b else part)
        conv_ref[at, :] = acc[:, :rows]
        value = pre_low[0, at, :].astype(F32)
        gate = jax.nn.sigmoid(pre_low[1, at, :].astype(F32))
        gate_ref[0, at, :] = gate
        gate_ref[1, at, :] = value * gate * (1.0 - gate)
        return carry

    lax.fori_loop(0, columns // step, block, 0)


def meta_of(ref, columns):
    return ref[3 * columns : 3 * columns + META, :].astype(F32)


def limits(query_meta, key_count, link):
    lane = lax.broadcasted_iota(jnp.int32, query_meta[0:1].shape, 1).astype(F32)
    valid = lane < query_meta[0:1]
    return [
        jnp.where(valid & (query_meta[1 + 2 * link + kb : 2 + 2 * link + kb] > 0.5), key_count, 0.0)
        for kb in range(2)
    ]


def masked(scores, limit_rows):
    rows = scores.shape[0]
    half = rows // 2
    parts = []
    for kb in range(2):
        index = lax.broadcasted_iota(jnp.int32, (half, scores.shape[1]), 0).astype(F32) + kb * half
        parts.append(
            jnp.where(index < limit_rows[kb], scores[kb * half : (kb + 1) * half], NEG)
        )
    return jnp.concatenate(parts, axis=0)


def edge_body(
    columns,
    before_ref,
    after_ref,
    conv_ref,
    gate_ref,
    taps_ref,
    w_ref,
    out_ref,
    low_ref,
    w_low,
    sem,
):
    copy = pltpu.make_async_copy(w_ref, w_low, sem)
    copy.start()
    rows = conv_ref.shape[1]
    step = 64
    for at in range(0, columns, step):
        here = slice(at, at + step)
        lane = lax.broadcasted_iota(jnp.int32, (step, LANES), 1)
        before = jnp.where(lane >= LANES - HALF, before_ref[here, rows - LANES :].astype(F32), 0.0)
        after = jnp.where(lane < HALF, after_ref[here, :LANES].astype(F32), 0.0)
        left = jnp.zeros((step, LANES), F32)
        right = jnp.zeros((step, LANES), F32)
        for m in range(1, HALF + 1):
            left = left + taps_ref[here, HALF + m : HALF + m + 1] * pltpu.roll(before, m, 1)
            right = right + taps_ref[here, HALF - m : HALF - m + 1] * pltpu.roll(after, LANES - m, 1)
        left = jnp.where(lane < HALF, left, 0.0)
        right = jnp.where(lane >= LANES - HALF, right, 0.0)
        grad = conv_ref[here, :] + jnp.concatenate([left, right], axis=1)
        low_ref[here, :] = (grad * gate_ref[0, here, :]).astype(BF16)
        low_ref[columns + at : columns + at + step, :] = (grad * gate_ref[1, here, :]).astype(BF16)
    copy.wait()
    model = w_ref.shape[1]
    chunk = 256 if model % 256 == 0 else LANES
    low = low_ref[...]
    for at in range(0, model, chunk):
        out_ref[at : at + chunk, :] = dot_tn(w_low[:, at : at + chunk], low).astype(BF16)


def softmax_of(refs, own_meta, columns, links, h, top):
    lo, hi = h * HEAD_DIM, (h + 1) * HEAD_DIM
    query = refs[0][2 * columns + lo : 2 * columns + hi, :]
    scores = []
    for ref, link in zip(refs[1:], links):
        limit = limits(own_meta, meta_of(ref, columns)[0:1], link)
        scores.append(masked(dot_tn(ref[lo:hi, :], query) * SCALE2, limit))
    top = functools.reduce(jnp.maximum, [jnp.max(s, axis=0, keepdims=True) for s in scores], top)
    total = jnp.zeros_like(top)
    mixed = jnp.zeros((HEAD_DIM, top.shape[1]), F32)
    for ref, score in zip(refs[1:], scores):
        expo = jnp.exp2(score - top)
        total = total + jnp.sum(expo, axis=0, keepdims=True)
        mixed = mixed + dot_nn(ref[columns + lo : columns + hi, :], expo.astype(BF16))
    return top, total, mixed


def softmax_body(columns, own_ref, one_ref, two_ref, out_ref):
    own_meta = meta_of(own_ref, columns)
    heads = columns // HEAD_DIM
    start = jnp.full(own_meta[0:1].shape, NEG, F32)
    out_ref[columns:, :] = jnp.zeros((8, own_ref.shape[1]), F32)
    for h in range(heads):
        top, total, mixed = softmax_of(
            (own_ref, own_ref, one_ref, two_ref), own_meta, columns, (0, 1, 2), h, start
        )
        out_ref[h * HEAD_DIM : (h + 1) * HEAD_DIM, :] = mixed
        out_ref[columns + h : columns + h + 1, :] = top
        out_ref[columns + heads + h : columns + heads + h + 1, :] = total


def pieces(value, count):
    found = []
    for _ in range(count):
        low = value.astype(BF16).astype(F32)
        found.append(low)
        value = value - low
    return found


def grad_body(columns, w_ref, stream_ref, own_ref, far_ref, soft_ref, out_ref):
    head_grad = dot_nn(w_ref[...], stream_ref[...])
    own_meta = meta_of(own_ref, columns)
    heads = columns // HEAD_DIM
    lane = lax.broadcasted_iota(jnp.int32, own_meta[0:1].shape, 1).astype(F32)
    valid = lane < own_meta[0:1]
    low = jnp.where(valid, head_grad, 0.0).astype(BF16)
    out_ref[0:columns, :] = low
    rows = []
    for h in range(heads):
        lo, hi = h * HEAD_DIM, (h + 1) * HEAD_DIM
        old_top = soft_ref[columns + h : columns + h + 1, :]
        top, total, mixed = softmax_of((own_ref, far_ref), own_meta, columns, (3,), h, old_top)
        factor = jnp.exp2(old_top - top)
        total = total + factor * soft_ref[columns + heads + h : columns + heads + h + 1, :]
        mixed = (mixed + factor * soft_ref[lo:hi, :]) / total
        delta = jnp.sum(low[lo:hi].astype(F32) * mixed, axis=0, keepdims=True)
        rows += pieces(jnp.where(valid, top + jnp.log2(total), -NEG), 3)
        rows += pieces(jnp.where(valid, delta, 0.0), 2)
    index = lax.broadcasted_iota(jnp.int32, (META, own_meta.shape[1]), 0)
    meta = jnp.zeros((META, own_meta.shape[1]), F32)
    for i, row in enumerate(rows):
        meta = jnp.where(index == i, row, meta)
    out_ref[columns:, :] = meta.astype(BF16)


def stats_of(ref, columns, h):
    meta = ref[columns : columns + META, :].astype(F32)
    at = 5 * h
    lse = (meta[at : at + 1] + meta[at + 1 : at + 2]) + meta[at + 2 : at + 3]
    delta = meta[at + 3 : at + 4] + meta[at + 4 : at + 5]
    return lse, delta


def tile(key, value, query, grad, lse, delta, limit):
    probs = jnp.exp2(masked(dot_tn(key, query) * SCALE2 - lse, limit))
    dscore = (probs * (dot_tn(value, grad) - delta)).astype(BF16)
    return probs.astype(BF16), dscore


def local_body(columns, own_ref, one_ref, two_ref, far_ref, grad_ref, query_out, acc_out):
    refs = (own_ref, one_ref, two_ref, far_ref)
    own_meta = meta_of(own_ref, columns)
    limit = [limits(own_meta, meta_of(refs[j], columns)[0:1], j) for j in range(LINKS)]
    for h in range(columns // HEAD_DIM):
        lo, hi = h * HEAD_DIM, (h + 1) * HEAD_DIM
        query = own_ref[2 * columns + lo : 2 * columns + hi, :]
        grad = grad_ref[lo:hi, :]
        lse, delta = stats_of(grad_ref, columns, h)
        total = jnp.zeros((HEAD_DIM, own_ref.shape[1]), F32)
        for j in range(LINKS):
            key = refs[j][lo:hi, :]
            value = refs[j][columns + lo : columns + hi, :]
            probs, dscore = tile(key, value, query, grad, lse, delta, limit[j])
            total = total + dot_nn(key, dscore)
            if j == 0:
                acc_out[lo:hi, :] = dot_nt(query, dscore)
                acc_out[columns + lo : columns + hi, :] = dot_nt(grad, probs)
        query_out[lo:hi, :] = (total * SCALE).astype(BF16)


def remote_terms(columns, links, own_ref, span_refs, grad_refs, h):
    lo, hi = h * HEAD_DIM, (h + 1) * HEAD_DIM
    key = own_ref[lo:hi, :]
    value = own_ref[columns + lo : columns + hi, :]
    count = meta_of(own_ref, columns)[0:1]
    key_term = value_term = 0.0
    for link, span_ref, grad_ref in zip(links, span_refs, grad_refs):
        query = span_ref[2 * columns + lo : 2 * columns + hi, :]
        grad = grad_ref[lo:hi, :]
        lse, delta = stats_of(grad_ref, columns, h)
        limit = limits(meta_of(span_ref, columns), count, link)
        probs, dscore = tile(key, value, query, grad, lse, delta, limit)
        key_term = key_term + dot_nt(query, dscore)
        value_term = value_term + dot_nt(grad, probs)
    return key_term, value_term


def near_body(columns, own_ref, one_ref, two_ref, grad_one_ref, grad_two_ref, acc_ref, acc_out):
    for h in range(columns // HEAD_DIM):
        lo, hi = h * HEAD_DIM, (h + 1) * HEAD_DIM
        key_term, value_term = remote_terms(
            columns,
            (MIRROR[1], MIRROR[2]),
            own_ref,
            (one_ref, two_ref),
            (grad_one_ref, grad_two_ref),
            h,
        )
        acc_out[lo:hi, :] = acc_ref[lo:hi, :] + key_term
        acc_out[columns + lo : columns + hi, :] = acc_ref[columns + lo : columns + hi, :] + value_term


def far_body(columns, own_ref, far_ref, grad_far_ref, acc_ref, key_out, value_out):
    for h in range(columns // HEAD_DIM):
        lo, hi = h * HEAD_DIM, (h + 1) * HEAD_DIM
        key_term, value_term = remote_terms(
            columns, (MIRROR[3],), own_ref, (far_ref,), (grad_far_ref,), h
        )
        key_out[lo:hi, :] = ((acc_ref[lo:hi, :] + key_term) * SCALE).astype(BF16)
        value_out[lo:hi, :] = (acc_ref[columns + lo : columns + hi, :] + value_term).astype(BF16)


def shifted(value, steps):
    count = lax.axis_size("ctx")
    pairs = [(source, (source + steps) % count) for source in range(count)]
    return lax.ppermute(value, "ctx", pairs)


def per_device(
    g_conv, pre, kernel, w_point, g_out, w_out, queries, keys, values, block_mask, counts
):
    columns, row_count = g_conv.shape
    model = w_point.shape[2]
    groups = lax.axis_size("head")
    spans = lax.axis_size("ctx")
    shape = jax.ShapeDtypeStruct
    queries, keys, values = (queries.T, keys.T, values.T)
    message = 3 * columns + META
    square = 2 * columns * row_count * row_count

    up = [(i, i + 1) for i in range(spans - 1)]
    before = lax.ppermute(g_conv, "ctx", up)
    after = lax.ppermute(g_conv, "ctx", [(j, i) for i, j in up])
    flat = (columns, row_count)
    own = call(
        pack_body,
        shape((message, row_count), BF16),
        (block_mask, counts, keys, values, queries),
        [SMEM] * 2 + [HBM] * 3,
        0,
        4 * message * row_count,
        0,
        (pltpu.SemaphoreType.DMA((3,)),),
        mib=BIG,
    )
    offsets = [0, 1, -1, spans // 2]
    far = shifted(own, offsets[3])
    conv, gate, taps = call(
        own_conv_body,
        (shape(flat, F32), shape((2,) + flat, F32), shape((columns, LANES), F32)),
        (g_conv, pre, kernel),
        [HBM] * 3,
        2 * KW * columns * row_count,
        20 * columns * row_count,
        columns * row_count,
        (
            pltpu.VMEM((columns, row_count + 2 * LANES), F32),
            pltpu.VMEM(flat, BF16),
            pltpu.VMEM((2,) + flat, BF16),
            pltpu.VMEM((KW, columns), F32),
            pltpu.SemaphoreType.DMA((3,)),
        ),
        mib=BIG,
    )
    point_grad = call(
        functools.partial(edge_body, columns),
        shape((model, row_count), BF16),
        (before, after, conv, gate, taps, w_point.reshape(2 * columns, model)),
        [VMEM] * 5 + [HBM],
        4 * columns * model * row_count,
        4 * columns * model,
        0,
        (
            pltpu.VMEM((2 * columns, row_count), BF16),
            pltpu.VMEM((2 * columns, model), BF16),
            pltpu.SemaphoreType.DMA,
        ),
        mib=BIG,
    )
    parts = lax.all_to_all(
        point_grad.reshape(groups, columns, row_count), "head", 0, 0, tiled=False
    )
    later, far, _ = lax.optimization_barrier((own, far, point_grad))
    one, two = [shifted(later, offset) for offset in offsets[1:3]]
    soft = call(
        functools.partial(softmax_body, columns),
        shape((columns + 8, row_count), F32),
        (own, one, two),
        [VMEM] * 3,
        6 * square,
        6 * message * row_count,
        3 * columns // HEAD_DIM * row_count * row_count,
    )
    piece = jnp.sum(parts.astype(F32), axis=0)
    stream_grad = (g_out.astype(F32) + piece).astype(BF16)
    stream_full = lax.all_gather(stream_grad, "head", axis=0, tiled=True)
    grad = call(
        functools.partial(grad_body, columns),
        shape((columns + META, row_count), BF16),
        (w_out, stream_full, own, far, soft),
        [VMEM] * 5,
        2 * columns * model * row_count + 2 * square,
        2 * model * (columns + row_count),
        columns // HEAD_DIM * row_count * row_count,
    )
    grad_one, grad_two, grad_far = [shifted(grad, offset) for offset in offsets[1:]]
    grad_queries, acc = call(
        functools.partial(local_body, columns),
        (shape((columns, row_count), BF16), shape((2 * columns, row_count), F32)),
        (own, one, two, far, grad),
        [VMEM] * 5,
        3 * LINKS * square,
        8 * message * row_count,
        LINKS * columns // HEAD_DIM * row_count * row_count,
    )
    acc = call(
        functools.partial(near_body, columns),
        shape((2 * columns, row_count), F32),
        (own, one, two, grad_one, grad_two, acc),
        [VMEM] * 6,
        8 * square,
        8 * message * row_count,
        2 * columns // HEAD_DIM * row_count * row_count,
    )
    grad_keys, grad_values = call(
        functools.partial(far_body, columns),
        (shape((columns, row_count), BF16), shape((columns, row_count), BF16)),
        (own, far, grad_far, acc),
        [VMEM] * 4,
        4 * square,
        8 * message * row_count,
        columns // HEAD_DIM * row_count * row_count,
    )
    return (stream_grad.T, grad_queries.T, grad_keys.T, grad_values.T)


def solution(mesh):
    in_specs = (
        P("head", "ctx"),
        P(None, "head", "ctx"),
        P(None, "head"),
        P(None, "head", None),
        P("head", "ctx"),
        P("head", None),
        P("ctx", "head"),
        P("ctx", "head"),
        P("ctx", "head"),
        P("ctx", None, None),
        P("ctx"),
    )
    out_specs = (P("ctx", "head"), P("ctx", "head"), P("ctx", "head"), P("ctx", "head"))
    return jax.shard_map(
        per_device, mesh=mesh, in_specs=in_specs, out_specs=out_specs, check_vma=False
    )
```

```python
import functools
import math

import jax
import jax.numpy as jnp
from jax import lax
from jax.experimental import pallas as pl
from jax.experimental.pallas import tpu as pltpu
from jax.sharding import PartitionSpec as P

HEAD_DIM = 64
KW = 31
LINKS = 4
HALF = 15
LANES = 128
META = 16
BIG = 58
NEG = -1e30
SCALE = 1.0 / math.sqrt(HEAD_DIM)
SCALE2 = SCALE * math.log2(math.e)
MIRROR = (0, 2, 1, 3)
VMEM = pl.BlockSpec(memory_space=pltpu.VMEM)
HBM = pl.BlockSpec(memory_space=pltpu.HBM)
SMEM = pl.BlockSpec(memory_space=pltpu.SMEM)
F32 = jnp.float32
BF16 = jnp.bfloat16


def call(body, out_shapes, args, specs, flops, moved, exps=0, scratch=(), mib=24):
    return pl.pallas_call(
        body,
        out_shape=out_shapes,
        in_specs=specs,
        out_specs=jax.tree.map(lambda _: VMEM, out_shapes),
        scratch_shapes=list(scratch),
        compiler_params=pltpu.CompilerParams(vmem_limit_bytes=mib * 1024 * 1024),
        cost_estimate=pl.CostEstimate(flops=flops, bytes_accessed=moved, transcendentals=exps),
    )(*args)


def dot_tn(a, b):
    return lax.dot_general(a, b, (((0,), (0,)), ((), ())), preferred_element_type=F32)


def dot_nt(a, b):
    return lax.dot_general(a, b, (((1,), (1,)), ((), ())), preferred_element_type=F32)


def dot_nn(a, b):
    return lax.dot_general(a, b, (((1,), (0,)), ((), ())), preferred_element_type=F32)


def pack_body(mask_ref, count_ref, keys_ref, values_ref, queries_ref, out_ref):
    columns, rows = keys_ref.shape
    out_ref[0:columns, :] = keys_ref[...]
    out_ref[columns : 2 * columns, :] = values_ref[...]
    out_ref[2 * columns : 3 * columns, :] = queries_ref[...]
    row = lax.broadcasted_iota(jnp.int32, (META, rows), 0)
    first = lax.broadcasted_iota(jnp.int32, (META, rows), 1) < rows // 2
    meta = jnp.where(row == 0, count_ref[0].astype(F32), 0.0)
    for j in range(LINKS):
        for kb in range(2):
            picked = []
            for qb in range(2):
                bit = (mask_ref[qb, j, kb] > 0).astype(F32)
                if j == 0 and qb == kb:
                    bit = jnp.maximum(bit, 1.0)
                picked.append(bit)
            meta = jnp.where(
                row == 1 + 2 * j + kb, jnp.where(first, picked[0], picked[1]), meta
            )
    out_ref[3 * columns :, :] = meta.astype(BF16)


def conv_body(
    columns,
    before_ref,
    after_ref,
    g_ref,
    pre_ref,
    taps_ref,
    w_ref,
    out_ref,
    x_ref,
    moved_ref,
    g_low,
    pre_low,
    taps_low,
    w_low,
    sum_ref,
    low_ref,
    sems,
):
    copies = [
        pltpu.make_async_copy(g_ref, g_low, sems.at[0]),
        pltpu.make_async_copy(taps_ref, taps_low, sems.at[1]),
        pltpu.make_async_copy(pre_ref, pre_low, sems.at[2]),
        pltpu.make_async_copy(w_ref, w_low, sems.at[3]),
    ]
    for copy in copies:
        copy.start()
    rows = g_ref.shape[1]
    pad = 16
    x_ref[0:pad, :] = before_ref[:, rows - LANES :].astype(F32).T[LANES - pad :, :]
    x_ref[pad + rows :, :] = after_ref[:, :LANES].astype(F32).T[:pad, :]
    copies[0].wait()
    copies[1].wait()
    x_ref[pad : pad + rows, :] = g_low[...].astype(F32).T
    for shift in range(8):
        moved_ref[shift] = x_ref[shift : shift + rows + 24, :]
    step = 32

    def block(i, carry):
        at = pl.multiple_of(i * step, step)
        acc = jnp.zeros((step, columns), F32)
        for k in range(KW):
            a, shift = divmod(31 - k, 8)
            acc = acc + taps_low[k : k + 1, :] * moved_ref[shift, pl.ds(at + 8 * a, step), :]
        sum_ref[pl.ds(at, step), :] = acc
        return carry

    lax.fori_loop(0, rows // step, block, 0)
    grad = sum_ref[...].T
    copies[2].wait()
    value = pre_low[0].astype(F32)
    gate = jax.nn.sigmoid(pre_low[1].astype(F32))
    low_ref[0:columns, :] = (grad * gate).astype(BF16)
    low_ref[columns:, :] = (grad * value * gate * (1.0 - gate)).astype(BF16)
    copies[3].wait()
    low = low_ref[...].T
    model = w_ref.shape[1]
    chunk = 256 if model % 256 == 0 else LANES
    for at in range(0, model, chunk):
        out_ref[at : at + chunk, :] = dot_nn(low, w_low[:, at : at + chunk]).astype(BF16).T


def meta_of(ref, columns):
    return ref[3 * columns : 3 * columns + META, :].astype(F32)


def limits(query_meta, key_count, link):
    lane = lax.broadcasted_iota(jnp.int32, query_meta[0:1].shape, 1).astype(F32)
    valid = lane < query_meta[0:1]
    return [
        jnp.where(valid & (query_meta[1 + 2 * link + kb : 2 + 2 * link + kb] > 0.5), key_count, 0.0)
        for kb in range(2)
    ]


def masked(scores, limit_rows):
    rows = scores.shape[0]
    half = rows // 2
    parts = []
    for kb in range(2):
        index = lax.broadcasted_iota(jnp.int32, (half, scores.shape[1]), 0).astype(F32) + kb * half
        parts.append(
            jnp.where(index < limit_rows[kb], scores[kb * half : (kb + 1) * half], NEG)
        )
    return jnp.concatenate(parts, axis=0)


def softmax_of(refs, own_meta, columns, links, h, top):
    lo, hi = h * HEAD_DIM, (h + 1) * HEAD_DIM
    query = refs[0][2 * columns + lo : 2 * columns + hi, :]
    scores = []
    for ref, link in zip(refs[1:], links):
        limit = limits(own_meta, meta_of(ref, columns)[0:1], link)
        scores.append(masked(dot_tn(ref[lo:hi, :], query) * SCALE2, limit))
    top = functools.reduce(jnp.maximum, [jnp.max(s, axis=0, keepdims=True) for s in scores], top)
    total = jnp.zeros_like(top)
    mixed = jnp.zeros((HEAD_DIM, top.shape[1]), F32)
    for ref, score in zip(refs[1:], scores):
        expo = jnp.exp2(score - top)
        total = total + jnp.sum(expo, axis=0, keepdims=True)
        mixed = mixed + dot_nn(ref[columns + lo : columns + hi, :], expo.astype(BF16))
    return top, total, mixed


def softmax_body(columns, own_ref, one_ref, two_ref, out_ref):
    own_meta = meta_of(own_ref, columns)
    heads = columns // HEAD_DIM
    start = jnp.full(own_meta[0:1].shape, NEG, F32)
    out_ref[columns:, :] = jnp.zeros((8, own_ref.shape[1]), F32)
    for h in range(heads):
        top, total, mixed = softmax_of(
            (own_ref, own_ref, one_ref, two_ref), own_meta, columns, (0, 1, 2), h, start
        )
        out_ref[h * HEAD_DIM : (h + 1) * HEAD_DIM, :] = mixed
        out_ref[columns + h : columns + h + 1, :] = top
        out_ref[columns + heads + h : columns + heads + h + 1, :] = total


def pieces(value, count):
    found = []
    for _ in range(count):
        low = value.astype(BF16).astype(F32)
        found.append(low)
        value = value - low
    return found


def grad_body(columns, w_ref, stream_ref, own_ref, far_ref, soft_ref, out_ref):
    head_grad = dot_nn(w_ref[...], stream_ref[...])
    own_meta = meta_of(own_ref, columns)
    heads = columns // HEAD_DIM
    lane = lax.broadcasted_iota(jnp.int32, own_meta[0:1].shape, 1).astype(F32)
    valid = lane < own_meta[0:1]
    low = jnp.where(valid, head_grad, 0.0).astype(BF16)
    out_ref[0:columns, :] = low
    rows = []
    for h in range(heads):
        lo, hi = h * HEAD_DIM, (h + 1) * HEAD_DIM
        old_top = soft_ref[columns + h : columns + h + 1, :]
        top, total, mixed = softmax_of((own_ref, far_ref), own_meta, columns, (3,), h, old_top)
        factor = jnp.exp2(old_top - top)
        total = total + factor * soft_ref[columns + heads + h : columns + heads + h + 1, :]
        mixed = (mixed + factor * soft_ref[lo:hi, :]) / total
        delta = jnp.sum(low[lo:hi].astype(F32) * mixed, axis=0, keepdims=True)
        rows += pieces(jnp.where(valid, top + jnp.log2(total), -NEG), 3)
        rows += pieces(jnp.where(valid, delta, 0.0), 2)
    index = lax.broadcasted_iota(jnp.int32, (META, own_meta.shape[1]), 0)
    meta = jnp.zeros((META, own_meta.shape[1]), F32)
    for i, row in enumerate(rows):
        meta = jnp.where(index == i, row, meta)
    out_ref[columns:, :] = meta.astype(BF16)


def stats_of(ref, columns, h):
    meta = ref[columns : columns + META, :].astype(F32)
    at = 5 * h
    lse = (meta[at : at + 1] + meta[at + 1 : at + 2]) + meta[at + 2 : at + 3]
    delta = meta[at + 3 : at + 4] + meta[at + 4 : at + 5]
    return lse, delta


def tile(key, value, query, grad, lse, delta, limit):
    probs = jnp.exp2(masked(dot_tn(key, query) * SCALE2 - lse, limit))
    dscore = (probs * (dot_tn(value, grad) - delta)).astype(BF16)
    return probs.astype(BF16), dscore


def local_body(columns, own_ref, one_ref, two_ref, far_ref, grad_ref, query_out, acc_out):
    refs = (own_ref, one_ref, two_ref, far_ref)
    own_meta = meta_of(own_ref, columns)
    limit = [limits(own_meta, meta_of(refs[j], columns)[0:1], j) for j in range(LINKS)]
    for h in range(columns // HEAD_DIM):
        lo, hi = h * HEAD_DIM, (h + 1) * HEAD_DIM
        query = own_ref[2 * columns + lo : 2 * columns + hi, :]
        grad = grad_ref[lo:hi, :]
        lse, delta = stats_of(grad_ref, columns, h)
        total = jnp.zeros((HEAD_DIM, own_ref.shape[1]), F32)
        for j in range(LINKS):
            key = refs[j][lo:hi, :]
            value = refs[j][columns + lo : columns + hi, :]
            probs, dscore = tile(key, value, query, grad, lse, delta, limit[j])
            total = total + dot_nn(key, dscore)
            if j == 0:
                acc_out[lo:hi, :] = dot_nt(query, dscore)
                acc_out[columns + lo : columns + hi, :] = dot_nt(grad, probs)
        query_out[lo:hi, :] = (total * SCALE).astype(BF16)


def remote_terms(columns, links, own_ref, span_refs, grad_refs, h):
    lo, hi = h * HEAD_DIM, (h + 1) * HEAD_DIM
    key = own_ref[lo:hi, :]
    value = own_ref[columns + lo : columns + hi, :]
    count = meta_of(own_ref, columns)[0:1]
    key_term = value_term = 0.0
    for link, span_ref, grad_ref in zip(links, span_refs, grad_refs):
        query = span_ref[2 * columns + lo : 2 * columns + hi, :]
        grad = grad_ref[lo:hi, :]
        lse, delta = stats_of(grad_ref, columns, h)
        limit = limits(meta_of(span_ref, columns), count, link)
        probs, dscore = tile(key, value, query, grad, lse, delta, limit)
        key_term = key_term + dot_nt(query, dscore)
        value_term = value_term + dot_nt(grad, probs)
    return key_term, value_term


def near_body(columns, own_ref, one_ref, two_ref, grad_one_ref, grad_two_ref, acc_ref, acc_out):
    for h in range(columns // HEAD_DIM):
        lo, hi = h * HEAD_DIM, (h + 1) * HEAD_DIM
        key_term, value_term = remote_terms(
            columns,
            (MIRROR[1], MIRROR[2]),
            own_ref,
            (one_ref, two_ref),
            (grad_one_ref, grad_two_ref),
            h,
        )
        acc_out[lo:hi, :] = acc_ref[lo:hi, :] + key_term
        acc_out[columns + lo : columns + hi, :] = acc_ref[columns + lo : columns + hi, :] + value_term


def far_body(columns, own_ref, far_ref, grad_far_ref, acc_ref, key_out, value_out):
    for h in range(columns // HEAD_DIM):
        lo, hi = h * HEAD_DIM, (h + 1) * HEAD_DIM
        key_term, value_term = remote_terms(
            columns, (MIRROR[3],), own_ref, (far_ref,), (grad_far_ref,), h
        )
        key_out[lo:hi, :] = ((acc_ref[lo:hi, :] + key_term) * SCALE).astype(BF16)
        value_out[lo:hi, :] = (acc_ref[columns + lo : columns + hi, :] + value_term).astype(BF16)


def shifted(value, steps):
    count = lax.axis_size("ctx")
    pairs = [(source, (source + steps) % count) for source in range(count)]
    return lax.ppermute(value, "ctx", pairs)


def per_device(
    g_conv, pre, kernel, w_point, g_out, w_out, queries, keys, values, block_mask, counts
):
    columns, row_count = g_conv.shape
    model = w_point.shape[2]
    groups = lax.axis_size("head")
    spans = lax.axis_size("ctx")
    shape = jax.ShapeDtypeStruct
    queries, keys, values = (queries.T, keys.T, values.T)
    message = 3 * columns + META
    square = 2 * columns * row_count * row_count

    up = [(i, i + 1) for i in range(spans - 1)]
    before = lax.ppermute(g_conv, "ctx", up)
    after = lax.ppermute(g_conv, "ctx", [(j, i) for i, j in up])
    flat = (columns, row_count)
    own = call(
        pack_body,
        shape((message, row_count), BF16),
        (block_mask, counts, keys, values, queries),
        [SMEM] * 2 + [VMEM] * 3,
        0,
        4 * message * row_count,
    )
    offsets = [0, 1, -1, spans // 2]
    point_grad = call(
        functools.partial(conv_body, columns),
        shape((model, row_count), BF16),
        (before, after, g_conv, pre, kernel, w_point.reshape(2 * columns, model)),
        [VMEM] * 2 + [HBM] * 4,
        4 * columns * model * row_count,
        4 * columns * model,
        columns * row_count,
        (
            pltpu.VMEM((row_count + 32, columns), F32),
            pltpu.VMEM((8, row_count + 24, columns), F32),
            pltpu.VMEM(flat, BF16),
            pltpu.VMEM((2,) + flat, BF16),
            pltpu.VMEM((KW, columns), F32),
            pltpu.VMEM((2 * columns, model), BF16),
            pltpu.VMEM((row_count, columns), F32),
            pltpu.VMEM((2 * columns, row_count), BF16),
            pltpu.SemaphoreType.DMA((4,)),
        ),
        mib=BIG,
    )
    parts = lax.all_to_all(
        point_grad.reshape(groups, columns, row_count), "head", 0, 0, tiled=False
    )
    own, _ = lax.optimization_barrier((own, point_grad))
    one, two = [shifted(own, offset) for offset in offsets[1:3]]
    later, one, two = lax.optimization_barrier((own, one, two))
    far = shifted(later, offsets[3])
    soft = call(
        functools.partial(softmax_body, columns),
        shape((columns + 8, row_count), F32),
        (own, one, two),
        [VMEM] * 3,
        6 * square,
        6 * message * row_count,
        3 * columns // HEAD_DIM * row_count * row_count,
    )
    piece = jnp.sum(parts.astype(F32), axis=0)
    stream_grad = (g_out.astype(F32) + piece).astype(BF16)
    stream_full = lax.all_gather(stream_grad, "head", axis=0, tiled=True)
    grad = call(
        functools.partial(grad_body, columns),
        shape((columns + META, row_count), BF16),
        (w_out, stream_full, own, far, soft),
        [VMEM] * 5,
        2 * columns * model * row_count + 2 * square,
        2 * model * (columns + row_count),
        columns // HEAD_DIM * row_count * row_count,
    )
    grad_one, grad_two, grad_far = [shifted(grad, offset) for offset in offsets[1:]]
    grad_queries, acc = call(
        functools.partial(local_body, columns),
        (shape((columns, row_count), BF16), shape((2 * columns, row_count), F32)),
        (own, one, two, far, grad),
        [VMEM] * 5,
        3 * LINKS * square,
        8 * message * row_count,
        LINKS * columns // HEAD_DIM * row_count * row_count,
    )
    acc = call(
        functools.partial(near_body, columns),
        shape((2 * columns, row_count), F32),
        (own, one, two, grad_one, grad_two, acc),
        [VMEM] * 6,
        8 * square,
        8 * message * row_count,
        2 * columns // HEAD_DIM * row_count * row_count,
    )
    grad_keys, grad_values = call(
        functools.partial(far_body, columns),
        (shape((columns, row_count), BF16), shape((columns, row_count), BF16)),
        (own, far, grad_far, acc),
        [VMEM] * 4,
        4 * square,
        8 * message * row_count,
        columns // HEAD_DIM * row_count * row_count,
    )
    return (stream_grad.T, grad_queries.T, grad_keys.T, grad_values.T)


def solution(mesh):
    in_specs = (
        P("head", "ctx"),
        P(None, "head", "ctx"),
        P(None, "head"),
        P(None, "head", None),
        P("head", "ctx"),
        P("head", None),
        P("ctx", "head"),
        P("ctx", "head"),
        P("ctx", "head"),
        P("ctx", None, None),
        P("ctx"),
    )
    out_specs = (P("ctx", "head"), P("ctx", "head"), P("ctx", "head"), P("ctx", "head"))
    return jax.shard_map(
        per_device, mesh=mesh, in_specs=in_specs, out_specs=out_specs, check_vma=False
    )
```

```python
import functools
import math

import jax
import jax.numpy as jnp
from jax import lax
from jax.experimental import pallas as pl
from jax.experimental.pallas import tpu as pltpu
from jax.sharding import PartitionSpec as P

HEAD_DIM = 64
KW = 31
LINKS = 4
HALF = 15
LANES = 128
META = 16
BIG = 58
PAD = 16
NEG = -1e30
SCALE = 1.0 / math.sqrt(HEAD_DIM)
SCALE2 = SCALE * math.log2(math.e)
MIRROR = (0, 2, 1, 3)
VMEM = pl.BlockSpec(memory_space=pltpu.VMEM)
HBM = pl.BlockSpec(memory_space=pltpu.HBM)
SMEM = pl.BlockSpec(memory_space=pltpu.SMEM)
F32 = jnp.float32
BF16 = jnp.bfloat16


def call(body, out_shapes, args, specs, flops, moved, exps=0, scratch=(), mib=24):
    return pl.pallas_call(
        body,
        out_shape=out_shapes,
        in_specs=specs,
        out_specs=jax.tree.map(lambda _: VMEM, out_shapes),
        scratch_shapes=list(scratch),
        compiler_params=pltpu.CompilerParams(vmem_limit_bytes=mib * 1024 * 1024),
        cost_estimate=pl.CostEstimate(flops=flops, bytes_accessed=moved, transcendentals=exps),
    )(*args)


def dot_tn(a, b):
    return lax.dot_general(a, b, (((0,), (0,)), ((), ())), preferred_element_type=F32)


def dot_nt(a, b):
    return lax.dot_general(a, b, (((1,), (1,)), ((), ())), preferred_element_type=F32)


def dot_nn(a, b):
    return lax.dot_general(a, b, (((1,), (0,)), ((), ())), preferred_element_type=F32)


def pack_body(mask_ref, count_ref, keys_ref, values_ref, queries_ref, out_ref):
    columns, rows = keys_ref.shape
    out_ref[0:columns, :] = keys_ref[...]
    out_ref[columns : 2 * columns, :] = values_ref[...]
    out_ref[2 * columns : 3 * columns, :] = queries_ref[...]
    row = lax.broadcasted_iota(jnp.int32, (META, rows), 0)
    first = lax.broadcasted_iota(jnp.int32, (META, rows), 1) < rows // 2
    meta = jnp.where(row == 0, count_ref[0].astype(F32), 0.0)
    for j in range(LINKS):
        for kb in range(2):
            picked = []
            for qb in range(2):
                bit = (mask_ref[qb, j, kb] > 0).astype(F32)
                if j == 0 and qb == kb:
                    bit = jnp.maximum(bit, 1.0)
                picked.append(bit)
            meta = jnp.where(
                row == 1 + 2 * j + kb, jnp.where(first, picked[0], picked[1]), meta
            )
    out_ref[3 * columns :, :] = meta.astype(BF16)


def own_conv_body(
    g_ref,
    pre_ref,
    taps_ref,
    w_ref,
    sum_out,
    gate_out,
    w_out,
    x_ref,
    moved_ref,
    g_low,
    pre_low,
    taps_low,
    w_low,
    sems,
):
    copies = [
        pltpu.make_async_copy(g_ref, g_low, sems.at[0]),
        pltpu.make_async_copy(taps_ref, taps_low, sems.at[1]),
        pltpu.make_async_copy(pre_ref, pre_low, sems.at[2]),
        pltpu.make_async_copy(w_ref, w_low, sems.at[3]),
    ]
    for copy in copies:
        copy.start()
    columns, rows = g_ref.shape
    x_ref[0:PAD, :] = jnp.zeros((PAD, columns), F32)
    x_ref[PAD + rows :, :] = jnp.zeros((PAD, columns), F32)
    copies[0].wait()
    copies[1].wait()
    x_ref[PAD : PAD + rows, :] = g_low[...].astype(F32).T
    for shift in range(8):
        moved_ref[shift] = x_ref[shift : shift + rows + 24, :]
    step = 32

    def block(i, carry):
        at = pl.multiple_of(i * step, step)
        acc = jnp.zeros((step, columns), F32)
        for k in range(KW):
            a, shift = divmod(PAD + HALF - k, 8)
            acc = acc + taps_low[k : k + 1, :] * moved_ref[shift, pl.ds(at + 8 * a, step), :]
        sum_out[pl.ds(at, step), :] = acc
        return carry

    lax.fori_loop(0, rows // step, block, 0)
    copies[2].wait()
    value = pre_low[0].astype(F32)
    gate = jax.nn.sigmoid(pre_low[1].astype(F32))
    gate_out[0] = gate.T
    gate_out[1] = (value * gate * (1.0 - gate)).T
    copies[3].wait()
    for half in range(2):
        for at in range(0, w_ref.shape[2], LANES):
            w_out[half, at : at + LANES, :] = w_low[half, :, at : at + LANES].T


def edge_body(before_ref, after_ref, sum_ref, gate_ref, taps_ref, w_ref, out_ref, head, tail):
    rows, columns = sum_ref.shape
    blank = jnp.zeros((PAD, columns), F32)
    head[0:PAD, :] = before_ref[:, rows - LANES :].astype(F32).T[LANES - PAD :, :]
    head[PAD:, :] = blank
    tail[0:PAD, :] = blank
    tail[PAD:, :] = after_ref[:, :LANES].astype(F32).T[:PAD, :]
    first, last = blank, blank
    for d in range(1, HALF + 1):
        first = first + taps_ref[HALF + d : HALF + d + 1, :] * head[PAD - d : 2 * PAD - d, :]
        last = last + taps_ref[HALF - d : HALF - d + 1, :] * tail[d : PAD + d, :]
    grad = jnp.concatenate(
        [sum_ref[0:PAD, :] + first, sum_ref[PAD : rows - PAD, :], sum_ref[rows - PAD :, :] + last],
        axis=0,
    )
    low = [(grad * gate_ref[half]).astype(BF16) for half in range(2)]
    model = w_ref.shape[1]
    chunk = 256 if model % 256 == 0 else LANES
    for at in range(0, model, chunk):
        here = slice(at, at + chunk)
        out_ref[here, :] = (
            dot_nt(w_ref[0, here, :], low[0]) + dot_nt(w_ref[1, here, :], low[1])
        ).astype(BF16)


def meta_of(ref, columns):
    return ref[3 * columns : 3 * columns + META, :].astype(F32)


def limits(query_meta, key_count, link):
    lane = lax.broadcasted_iota(jnp.int32, query_meta[0:1].shape, 1).astype(F32)
    valid = lane < query_meta[0:1]
    return [
        jnp.where(valid & (query_meta[1 + 2 * link + kb : 2 + 2 * link + kb] > 0.5), key_count, 0.0)
        for kb in range(2)
    ]


def masked(scores, limit_rows):
    rows = scores.shape[0]
    half = rows // 2
    parts = []
    for kb in range(2):
        index = lax.broadcasted_iota(jnp.int32, (half, scores.shape[1]), 0).astype(F32) + kb * half
        parts.append(
            jnp.where(index < limit_rows[kb], scores[kb * half : (kb + 1) * half], NEG)
        )
    return jnp.concatenate(parts, axis=0)


def pieces(value, count):
    found = []
    for _ in range(count):
        low = value.astype(BF16).astype(F32)
        found.append(low)
        value = value - low
    return found


def grad_body(
    columns, w_ref, stream_ref, own_ref, one_ref, two_ref, far_ref, out_ref, tile_out, inverse_out
):
    refs = (own_ref, one_ref, two_ref, far_ref)
    own_meta = meta_of(own_ref, columns)
    lane = lax.broadcasted_iota(jnp.int32, own_meta[0:1].shape, 1).astype(F32)
    valid = lane < own_meta[0:1]
    limit = [limits(own_meta, meta_of(refs[j], columns)[0:1], j) for j in range(LINKS)]
    low = jnp.where(valid, dot_nn(w_ref[...], stream_ref[...]), 0.0).astype(BF16)
    out_ref[0:columns, :] = low
    rows = []
    inverse_out[...] = jnp.zeros(inverse_out.shape, F32)
    for h in range(columns // HEAD_DIM):
        lo, hi = h * HEAD_DIM, (h + 1) * HEAD_DIM
        query = own_ref[2 * columns + lo : 2 * columns + hi, :]
        scores = [
            masked(dot_tn(refs[j][lo:hi, :], query) * SCALE2, limit[j]) for j in range(LINKS)
        ]
        top = functools.reduce(jnp.maximum, [jnp.max(s, axis=0, keepdims=True) for s in scores])
        total = jnp.zeros_like(top)
        mixed = jnp.zeros((HEAD_DIM, own_ref.shape[1]), F32)
        for j in range(LINKS):
            expo = jnp.exp2(scores[j] - top)
            tile_out[LINKS * h + j] = expo
            total = total + jnp.sum(expo, axis=0, keepdims=True)
            mixed = mixed + dot_nn(refs[j][columns + lo : columns + hi, :], expo.astype(BF16))
        inverse = jnp.where(valid, 1.0 / total, 0.0)
        inverse_out[h : h + 1, :] = inverse
        delta = jnp.sum(low[lo:hi].astype(F32) * mixed, axis=0, keepdims=True) * inverse
        rows += pieces(jnp.where(valid, top + jnp.log2(total), -NEG), 3)
        rows += pieces(delta, 2)
    index = lax.broadcasted_iota(jnp.int32, (META, own_meta.shape[1]), 0)
    meta = jnp.zeros((META, own_meta.shape[1]), F32)
    for i, row in enumerate(rows):
        meta = jnp.where(index == i, row, meta)
    out_ref[columns:, :] = meta.astype(BF16)


def stats_of(ref, columns, h):
    meta = ref[columns : columns + META, :].astype(F32)
    at = 5 * h
    lse = (meta[at : at + 1] + meta[at + 1 : at + 2]) + meta[at + 2 : at + 3]
    delta = meta[at + 3 : at + 4] + meta[at + 4 : at + 5]
    return lse, delta


def tile(key, value, query, grad, lse, delta, limit):
    probs = jnp.exp2(masked(dot_tn(key, query) * SCALE2 - lse, limit))
    dscore = (probs * (dot_tn(value, grad) - delta)).astype(BF16)
    return probs.astype(BF16), dscore


def local_body(
    columns,
    own_ref,
    one_ref,
    two_ref,
    far_ref,
    grad_ref,
    tile_ref,
    inverse_ref,
    query_out,
    acc_out,
):
    refs = (own_ref, one_ref, two_ref, far_ref)
    for h in range(columns // HEAD_DIM):
        lo, hi = h * HEAD_DIM, (h + 1) * HEAD_DIM
        grad = grad_ref[lo:hi, :]
        inverse = inverse_ref[h : h + 1, :]
        _, delta = stats_of(grad_ref, columns, h)
        total = jnp.zeros((HEAD_DIM, own_ref.shape[1]), F32)
        for j in range(LINKS):
            value = refs[j][columns + lo : columns + hi, :]
            probs = tile_ref[LINKS * h + j] * inverse
            dscore = (probs * (dot_tn(value, grad) - delta)).astype(BF16)
            total = total + dot_nn(refs[j][lo:hi, :], dscore)
            if j == 0:
                query = own_ref[2 * columns + lo : 2 * columns + hi, :]
                acc_out[lo:hi, :] = dot_nt(query, dscore)
                acc_out[columns + lo : columns + hi, :] = dot_nt(grad, probs.astype(BF16))
        query_out[lo:hi, :] = (total * SCALE).astype(BF16)


def remote_terms(columns, links, own_ref, span_refs, grad_refs, h):
    lo, hi = h * HEAD_DIM, (h + 1) * HEAD_DIM
    key = own_ref[lo:hi, :]
    value = own_ref[columns + lo : columns + hi, :]
    count = meta_of(own_ref, columns)[0:1]
    key_term = value_term = 0.0
    for link, span_ref, grad_ref in zip(links, span_refs, grad_refs):
        query = span_ref[2 * columns + lo : 2 * columns + hi, :]
        grad = grad_ref[lo:hi, :]
        lse, delta = stats_of(grad_ref, columns, h)
        limit = limits(meta_of(span_ref, columns), count, link)
        probs, dscore = tile(key, value, query, grad, lse, delta, limit)
        key_term = key_term + dot_nt(query, dscore)
        value_term = value_term + dot_nt(grad, probs)
    return key_term, value_term


def near_body(columns, own_ref, one_ref, two_ref, grad_one_ref, grad_two_ref, acc_ref, acc_out):
    for h in range(columns // HEAD_DIM):
        lo, hi = h * HEAD_DIM, (h + 1) * HEAD_DIM
        key_term, value_term = remote_terms(
            columns,
            (MIRROR[1], MIRROR[2]),
            own_ref,
            (one_ref, two_ref),
            (grad_one_ref, grad_two_ref),
            h,
        )
        acc_out[lo:hi, :] = acc_ref[lo:hi, :] + key_term
        acc_out[columns + lo : columns + hi, :] = acc_ref[columns + lo : columns + hi, :] + value_term


def far_body(columns, own_ref, far_ref, grad_far_ref, acc_ref, key_out, value_out):
    for h in range(columns // HEAD_DIM):
        lo, hi = h * HEAD_DIM, (h + 1) * HEAD_DIM
        key_term, value_term = remote_terms(
            columns, (MIRROR[3],), own_ref, (far_ref,), (grad_far_ref,), h
        )
        key_out[lo:hi, :] = ((acc_ref[lo:hi, :] + key_term) * SCALE).astype(BF16)
        value_out[lo:hi, :] = (acc_ref[columns + lo : columns + hi, :] + value_term).astype(BF16)


def shifted(value, steps):
    count = lax.axis_size("ctx")
    pairs = [(source, (source + steps) % count) for source in range(count)]
    return lax.ppermute(value, "ctx", pairs)


def per_device(
    g_conv, pre, kernel, w_point, g_out, w_out, queries, keys, values, block_mask, counts
):
    columns, row_count = g_conv.shape
    model = w_point.shape[2]
    groups = lax.axis_size("head")
    spans = lax.axis_size("ctx")
    shape = jax.ShapeDtypeStruct
    queries, keys, values = (queries.T, keys.T, values.T)
    message = 3 * columns + META
    square = 2 * columns * row_count * row_count

    up = [(i, i + 1) for i in range(spans - 1)]
    before = lax.ppermute(g_conv, "ctx", up)
    after = lax.ppermute(g_conv, "ctx", [(j, i) for i, j in up])
    flat = (columns, row_count)
    own = call(
        pack_body,
        shape((message, row_count), BF16),
        (block_mask, counts, keys, values, queries),
        [SMEM] * 2 + [VMEM] * 3,
        0,
        4 * message * row_count,
    )
    offsets = [0, 1, -1, spans // 2]
    conv, gate, w_turned = call(
        own_conv_body,
        (
            shape((row_count, columns), F32),
            shape((2, row_count, columns), F32),
            shape((2, model, columns), BF16),
        ),
        (g_conv, pre, kernel, w_point),
        [HBM] * 4,
        2 * KW * columns * row_count,
        8 * columns * model,
        columns * row_count,
        (
            pltpu.VMEM((row_count + 2 * PAD, columns), F32),
            pltpu.VMEM((8, row_count + 24, columns), F32),
            pltpu.VMEM(flat, BF16),
            pltpu.VMEM((2,) + flat, BF16),
            pltpu.VMEM((KW, columns), F32),
            pltpu.VMEM((2, columns, model), BF16),
            pltpu.SemaphoreType.DMA((4,)),
        ),
        mib=BIG,
    )
    point_grad = call(
        edge_body,
        shape((model, row_count), BF16),
        (before, after, conv, gate, kernel, w_turned),
        [VMEM] * 6,
        4 * columns * model * row_count,
        4 * columns * model,
        0,
        (pltpu.VMEM((2 * PAD, columns), F32), pltpu.VMEM((2 * PAD, columns), F32)),
    )
    parts = lax.all_to_all(
        point_grad.reshape(groups, columns, row_count), "head", 0, 0, tiled=False
    )
    own, _ = lax.optimization_barrier((own, point_grad))
    one, two, far = [shifted(own, offset) for offset in offsets[1:]]
    piece = jnp.sum(parts.astype(F32), axis=0)
    stream_grad = (g_out.astype(F32) + piece).astype(BF16)
    stream_full = lax.all_gather(stream_grad, "head", axis=0, tiled=True)
    tiles = (LINKS * columns // HEAD_DIM, row_count, row_count)
    grad, tile, inverse = call(
        functools.partial(grad_body, columns),
        (shape((columns + META, row_count), BF16), shape(tiles, F32), shape((8, row_count), F32)),
        (w_out, stream_full, own, one, two, far),
        [VMEM] * 6,
        2 * columns * model * row_count + 2 * LINKS * square,
        2 * model * (columns + row_count),
        LINKS * columns // HEAD_DIM * row_count * row_count,
    )
    grad_one, grad_two, grad_far = [shifted(grad, offset) for offset in offsets[1:]]
    grad_queries, acc = call(
        functools.partial(local_body, columns),
        (shape((columns, row_count), BF16), shape((2 * columns, row_count), F32)),
        (own, one, two, far, grad, tile, inverse),
        [VMEM] * 7,
        3 * LINKS * square,
        8 * message * row_count,
    )
    acc = call(
        functools.partial(near_body, columns),
        shape((2 * columns, row_count), F32),
        (own, one, two, grad_one, grad_two, acc),
        [VMEM] * 6,
        8 * square,
        8 * message * row_count,
        2 * columns // HEAD_DIM * row_count * row_count,
    )
    grad_keys, grad_values = call(
        functools.partial(far_body, columns),
        (shape((columns, row_count), BF16), shape((columns, row_count), BF16)),
        (own, far, grad_far, acc),
        [VMEM] * 4,
        4 * square,
        8 * message * row_count,
        columns // HEAD_DIM * row_count * row_count,
    )
    return (stream_grad.T, grad_queries.T, grad_keys.T, grad_values.T)


def solution(mesh):
    in_specs = (
        P("head", "ctx"),
        P(None, "head", "ctx"),
        P(None, "head"),
        P(None, "head", None),
        P("head", "ctx"),
        P("head", None),
        P("ctx", "head"),
        P("ctx", "head"),
        P("ctx", "head"),
        P("ctx", None, None),
        P("ctx"),
    )
    out_specs = (P("ctx", "head"), P("ctx", "head"), P("ctx", "head"), P("ctx", "head"))
    return jax.shard_map(
        per_device, mesh=mesh, in_specs=in_specs, out_specs=out_specs, check_vma=False
    )
```

```python
import functools
import math

import jax
import jax.numpy as jnp
from jax import lax
from jax.experimental import pallas as pl
from jax.experimental.pallas import tpu as pltpu
from jax.sharding import PartitionSpec as P

HEAD_DIM = 64
KW = 31
LINKS = 4
HALF = 15
LANES = 128
META = 16
BIG = 58
PAD = 16
NEG = -1e30
SCALE = 1.0 / math.sqrt(HEAD_DIM)
SCALE2 = SCALE * math.log2(math.e)
VMEM = pl.BlockSpec(memory_space=pltpu.VMEM)
HBM = pl.BlockSpec(memory_space=pltpu.HBM)
SMEM = pl.BlockSpec(memory_space=pltpu.SMEM)
F32 = jnp.float32
BF16 = jnp.bfloat16


def call(body, out_shapes, args, specs, flops, moved, exps=0, scratch=(), mib=24):
    return pl.pallas_call(
        body,
        out_shape=out_shapes,
        in_specs=specs,
        out_specs=jax.tree.map(lambda _: VMEM, out_shapes),
        scratch_shapes=list(scratch),
        compiler_params=pltpu.CompilerParams(vmem_limit_bytes=mib * 1024 * 1024),
        cost_estimate=pl.CostEstimate(flops=flops, bytes_accessed=moved, transcendentals=exps),
    )(*args)


def dot_tn(a, b):
    return lax.dot_general(a, b, (((0,), (0,)), ((), ())), preferred_element_type=F32)


def dot_nt(a, b):
    return lax.dot_general(a, b, (((1,), (1,)), ((), ())), preferred_element_type=F32)


def dot_nn(a, b):
    return lax.dot_general(a, b, (((1,), (0,)), ((), ())), preferred_element_type=F32)


def pack_body(odd_ref, mask_ref, count_ref, keys_ref, values_ref, queries_ref, out_ref):
    columns, rows = keys_ref.shape
    out_ref[0:columns, :] = keys_ref[...]
    out_ref[columns : 2 * columns, :] = values_ref[...]
    out_ref[2 * columns : 3 * columns, :] = queries_ref[...]
    row = lax.broadcasted_iota(jnp.int32, (META, rows), 0)
    first = lax.broadcasted_iota(jnp.int32, (META, rows), 1) < rows // 2
    meta = jnp.where(row == 0, count_ref[0].astype(F32), 0.0)
    links = (0, 2 - odd_ref[0], 1 + odd_ref[0], 3)
    for slot, link in enumerate(links):
        for kb in range(2):
            picked = []
            for qb in range(2):
                bit = (mask_ref[qb, link, kb] > 0).astype(F32)
                if slot == 0 and qb == kb:
                    bit = jnp.maximum(bit, 1.0)
                picked.append(bit)
            meta = jnp.where(
                row == 1 + 2 * slot + kb, jnp.where(first, picked[0], picked[1]), meta
            )
    out_ref[3 * columns :, :] = meta.astype(BF16)


def own_conv_body(
    g_ref,
    pre_ref,
    taps_ref,
    w_ref,
    sum_out,
    gate_out,
    w_out,
    x_ref,
    moved_ref,
    sum_ref,
    g_low,
    pre_low,
    taps_low,
    w_low,
    sems,
):
    copies = [
        pltpu.make_async_copy(g_ref, g_low, sems.at[0]),
        pltpu.make_async_copy(taps_ref, taps_low, sems.at[1]),
        pltpu.make_async_copy(pre_ref, pre_low, sems.at[2]),
        pltpu.make_async_copy(w_ref, w_low, sems.at[3]),
    ]
    for copy in copies:
        copy.start()
    columns, rows = g_ref.shape
    x_ref[0:PAD, :] = jnp.zeros((PAD, columns), F32)
    x_ref[PAD + rows :, :] = jnp.zeros((PAD, columns), F32)
    copies[0].wait()
    copies[1].wait()
    x_ref[PAD : PAD + rows, :] = g_low[...].astype(F32).T
    for shift in range(8):
        moved_ref[shift] = x_ref[shift : shift + rows + 24, :]
    step = 32

    def block(i, carry):
        at = pl.multiple_of(i * step, step)
        acc = jnp.zeros((step, columns), F32)
        for k in range(KW):
            a, shift = divmod(PAD + HALF - k, 8)
            acc = acc + taps_low[k : k + 1, :] * moved_ref[shift, pl.ds(at + 8 * a, step), :]
        sum_ref[pl.ds(at, step), :] = acc
        return carry

    lax.fori_loop(0, rows // step, block, 0)
    sum_out[...] = sum_ref[...].T
    copies[2].wait()
    value = pre_low[0].astype(F32)
    gate = jax.nn.sigmoid(pre_low[1].astype(F32))
    gate_out[0] = gate
    gate_out[1] = value * gate * (1.0 - gate)
    copies[3].wait()
    for at in range(0, w_ref.shape[1], LANES):
        w_out[at : at + LANES, :] = w_low[:, at : at + LANES].T


def edge_body(
    odd_ref,
    two_ref,
    one_ref,
    taps_ref,
    sum_ref,
    gate_ref,
    w_ref,
    out_ref,
    head,
    tail,
    two_low,
    one_low,
    taps_low,
    sum_low,
    gate_low,
    w_low,
    sems,
):
    copies = [
        pltpu.make_async_copy(ref, low, sems.at[i])
        for i, (ref, low) in enumerate(
            (
                (two_ref, two_low),
                (one_ref, one_low),
                (taps_ref, taps_low),
                (sum_ref, sum_low),
                (gate_ref, gate_low),
                (w_ref, w_low),
            )
        )
    ]
    for copy in copies:
        copy.start()
    columns, rows = sum_ref.shape
    odd = odd_ref[0] > 0
    for copy in copies[:3]:
        copy.wait()
    before = jnp.where(odd, one_low[:, rows - LANES :], two_low[:, rows - LANES :]).astype(F32)
    after = jnp.where(odd, two_low[:, :LANES], one_low[:, :LANES]).astype(F32)
    blank = jnp.zeros((PAD, columns), F32)
    head[0:PAD, :] = before.T[LANES - PAD :, :]
    head[PAD:, :] = blank
    tail[0:PAD, :] = blank
    tail[PAD:, :] = after.T[:PAD, :]
    first, last = blank, blank
    for d in range(1, HALF + 1):
        first = first + taps_low[HALF + d : HALF + d + 1, :] * head[PAD - d : 2 * PAD - d, :]
        last = last + taps_low[HALF - d : HALF - d + 1, :] * tail[d : PAD + d, :]
    rest = jnp.zeros((LANES - PAD, columns), F32)
    left = jnp.concatenate([first, rest], axis=0).T
    right = jnp.concatenate([rest, last], axis=0).T
    copies[3].wait()
    grad = sum_low[...] + jnp.concatenate([left, right], axis=1)
    copies[4].wait()
    low = jnp.concatenate([(grad * gate_low[half]).astype(BF16) for half in range(2)], axis=0)
    copies[5].wait()
    model = w_ref.shape[0]
    chunk = 256 if model % 256 == 0 else LANES
    for at in range(0, model, chunk):
        out_ref[at : at + chunk, :] = dot_nn(w_low[at : at + chunk, :], low).astype(BF16)


def meta_of(ref, columns):
    return ref[3 * columns : 3 * columns + META, :].astype(F32)


def limits(query_meta, key_count, slot):
    lane = lax.broadcasted_iota(jnp.int32, query_meta[0:1].shape, 1).astype(F32)
    valid = lane < query_meta[0:1]
    return [
        jnp.where(valid & (query_meta[1 + 2 * slot + kb : 2 + 2 * slot + kb] > 0.5), key_count, 0.0)
        for kb in range(2)
    ]


def masked(scores, limit_rows):
    rows = scores.shape[0]
    half = rows // 2
    parts = []
    for kb in range(2):
        index = lax.broadcasted_iota(jnp.int32, (half, scores.shape[1]), 0).astype(F32) + kb * half
        parts.append(
            jnp.where(index < limit_rows[kb], scores[kb * half : (kb + 1) * half], NEG)
        )
    return jnp.concatenate(parts, axis=0)


def pieces(value, count):
    found = []
    for _ in range(count):
        low = value.astype(BF16).astype(F32)
        found.append(low)
        value = value - low
    return found


def grad_body(
    columns, w_ref, stream_ref, own_ref, one_ref, far_ref, two_ref, out_ref, tile_out, inverse_out
):
    refs = (own_ref, one_ref, two_ref, far_ref)
    own_meta = meta_of(own_ref, columns)
    lane = lax.broadcasted_iota(jnp.int32, own_meta[0:1].shape, 1).astype(F32)
    valid = lane < own_meta[0:1]
    limit = [limits(own_meta, meta_of(refs[j], columns)[0:1], j) for j in range(LINKS)]
    low = jnp.where(valid, dot_nn(w_ref[...], stream_ref[...]), 0.0).astype(BF16)
    out_ref[0:columns, :] = low
    rows = []
    inverse_out[...] = jnp.zeros(inverse_out.shape, F32)
    for h in range(columns // HEAD_DIM):
        lo, hi = h * HEAD_DIM, (h + 1) * HEAD_DIM
        query = own_ref[2 * columns + lo : 2 * columns + hi, :]
        scores = [
            masked(dot_tn(refs[j][lo:hi, :], query) * SCALE2, limit[j]) for j in range(LINKS)
        ]
        top = functools.reduce(jnp.maximum, [jnp.max(s, axis=0, keepdims=True) for s in scores])
        total = jnp.zeros_like(top)
        mixed = jnp.zeros((HEAD_DIM, own_ref.shape[1]), F32)
        for j in range(LINKS):
            expo = jnp.exp2(scores[j] - top)
            tile_out[LINKS * h + j] = expo
            total = total + jnp.sum(expo, axis=0, keepdims=True)
            mixed = mixed + dot_nn(refs[j][columns + lo : columns + hi, :], expo.astype(BF16))
        inverse = jnp.where(valid, 1.0 / total, 0.0)
        inverse_out[h : h + 1, :] = inverse
        delta = jnp.sum(low[lo:hi].astype(F32) * mixed, axis=0, keepdims=True) * inverse
        rows += pieces(jnp.where(valid, top + jnp.log2(total), -NEG), 3)
        rows += pieces(delta, 2)
    index = lax.broadcasted_iota(jnp.int32, (META, own_meta.shape[1]), 0)
    meta = jnp.zeros((META, own_meta.shape[1]), F32)
    for i, row in enumerate(rows):
        meta = jnp.where(index == i, row, meta)
    out_ref[columns:, :] = meta.astype(BF16)


def stats_of(ref, columns, h):
    meta = ref[columns : columns + META, :].astype(F32)
    at = 5 * h
    lse = (meta[at : at + 1] + meta[at + 1 : at + 2]) + meta[at + 2 : at + 3]
    delta = meta[at + 3 : at + 4] + meta[at + 4 : at + 5]
    return lse, delta


def tile(key, value, query, grad, lse, delta, limit):
    probs = jnp.exp2(masked(dot_tn(key, query) * SCALE2 - lse, limit))
    dscore = (probs * (dot_tn(value, grad) - delta)).astype(BF16)
    return probs.astype(BF16), dscore


def local_body(
    columns,
    own_ref,
    one_ref,
    two_ref,
    far_ref,
    grad_ref,
    tile_ref,
    inverse_ref,
    query_out,
    acc_out,
):
    refs = (own_ref, one_ref, two_ref, far_ref)
    for h in range(columns // HEAD_DIM):
        lo, hi = h * HEAD_DIM, (h + 1) * HEAD_DIM
        grad = grad_ref[lo:hi, :]
        inverse = inverse_ref[h : h + 1, :]
        _, delta = stats_of(grad_ref, columns, h)
        total = jnp.zeros((HEAD_DIM, own_ref.shape[1]), F32)
        for j in range(LINKS):
            value = refs[j][columns + lo : columns + hi, :]
            probs = tile_ref[LINKS * h + j] * inverse
            dscore = (probs * (dot_tn(value, grad) - delta)).astype(BF16)
            total = total + dot_nn(refs[j][lo:hi, :], dscore)
            if j == 0:
                query = own_ref[2 * columns + lo : 2 * columns + hi, :]
                acc_out[lo:hi, :] = dot_nt(query, dscore)
                acc_out[columns + lo : columns + hi, :] = dot_nt(grad, probs.astype(BF16))
        query_out[lo:hi, :] = (total * SCALE).astype(BF16)


def remote_terms(columns, slots, own_ref, span_refs, grad_refs, h):
    lo, hi = h * HEAD_DIM, (h + 1) * HEAD_DIM
    key = own_ref[lo:hi, :]
    value = own_ref[columns + lo : columns + hi, :]
    count = meta_of(own_ref, columns)[0:1]
    key_term = value_term = 0.0
    for slot, span_ref, grad_ref in zip(slots, span_refs, grad_refs):
        query = span_ref[2 * columns + lo : 2 * columns + hi, :]
        grad = grad_ref[lo:hi, :]
        lse, delta = stats_of(grad_ref, columns, h)
        limit = limits(meta_of(span_ref, columns), count, slot)
        probs, dscore = tile(key, value, query, grad, lse, delta, limit)
        key_term = key_term + dot_nt(query, dscore)
        value_term = value_term + dot_nt(grad, probs)
    return key_term, value_term


def middle_body(columns, own_ref, two_ref, far_ref, grad_two_ref, grad_far_ref, acc_ref, acc_out):
    for h in range(columns // HEAD_DIM):
        lo, hi = h * HEAD_DIM, (h + 1) * HEAD_DIM
        key_term, value_term = remote_terms(
            columns, (2, 3), own_ref, (two_ref, far_ref), (grad_two_ref, grad_far_ref), h
        )
        acc_out[lo:hi, :] = acc_ref[lo:hi, :] + key_term
        acc_out[columns + lo : columns + hi, :] = acc_ref[columns + lo : columns + hi, :] + value_term


def last_body(columns, own_ref, one_ref, grad_one_ref, acc_ref, key_out, value_out):
    for h in range(columns // HEAD_DIM):
        lo, hi = h * HEAD_DIM, (h + 1) * HEAD_DIM
        key_term, value_term = remote_terms(
            columns, (1,), own_ref, (one_ref,), (grad_one_ref,), h
        )
        key_out[lo:hi, :] = ((acc_ref[lo:hi, :] + key_term) * SCALE).astype(BF16)
        value_out[lo:hi, :] = (acc_ref[columns + lo : columns + hi, :] + value_term).astype(BF16)


def exchange(value, slot, closed=True):
    count = lax.axis_size("ctx")
    if slot == 3:
        pairs = [(c, (c + count // 2) % count) for c in range(count)]
    else:
        pairs = [(c, (c + (1 if (c + slot) % 2 else -1)) % count) for c in range(count)]
    if not closed:
        pairs = [(i, j) for i, j in pairs if abs(i - j) == 1]
    return lax.ppermute(value, "ctx", pairs)


def per_device(
    g_conv, pre, kernel, w_point, g_out, w_out, queries, keys, values, block_mask, counts
):
    columns, row_count = g_conv.shape
    model = w_point.shape[2]
    groups = lax.axis_size("head")
    shape = jax.ShapeDtypeStruct
    queries, keys, values = (queries.T, keys.T, values.T)
    message = 3 * columns + META
    square = 2 * columns * row_count * row_count

    odd = (lax.axis_index("ctx") % 2).astype(jnp.int32).reshape(1)
    near = [exchange(g_conv, slot, closed=False) for slot in (2, 1)]
    flat = (columns, row_count)
    own = call(
        pack_body,
        shape((message, row_count), BF16),
        (odd, block_mask, counts, keys, values, queries),
        [SMEM] * 3 + [VMEM] * 3,
        0,
        4 * message * row_count,
    )
    conv, gate, w_turned = call(
        own_conv_body,
        (shape(flat, F32), shape((2,) + flat, F32), shape((model, 2 * columns), BF16)),
        (g_conv, pre, kernel, w_point.reshape(2 * columns, model)),
        [HBM] * 4,
        2 * KW * columns * row_count,
        8 * columns * model,
        columns * row_count,
        (
            pltpu.VMEM((row_count + 2 * PAD, columns), F32),
            pltpu.VMEM((8, row_count + 24, columns), F32),
            pltpu.VMEM((row_count, columns), F32),
            pltpu.VMEM(flat, BF16),
            pltpu.VMEM((2,) + flat, BF16),
            pltpu.VMEM((KW, columns), F32),
            pltpu.VMEM((2 * columns, model), BF16),
            pltpu.SemaphoreType.DMA((4,)),
        ),
        mib=BIG,
    )
    point_grad = call(
        edge_body,
        shape((model, row_count), BF16),
        (odd, *near, kernel, conv, gate, w_turned),
        [SMEM] + [HBM] * 6,
        4 * columns * model * row_count,
        4 * columns * model,
        0,
        (
            pltpu.VMEM((2 * PAD, columns), F32),
            pltpu.VMEM((2 * PAD, columns), F32),
            pltpu.VMEM(flat, BF16),
            pltpu.VMEM(flat, BF16),
            pltpu.VMEM((KW, columns), F32),
            pltpu.VMEM(flat, F32),
            pltpu.VMEM((2,) + flat, F32),
            pltpu.VMEM((model, 2 * columns), BF16),
            pltpu.SemaphoreType.DMA((6,)),
        ),
        mib=BIG,
    )
    parts = lax.all_to_all(
        point_grad.reshape(groups, columns, row_count), "head", 0, 0, tiled=False
    )
    own, _ = lax.optimization_barrier((own, point_grad))
    one, two = [exchange(own, slot) for slot in (1, 2)]
    far = exchange(own, 3)
    piece = jnp.sum(parts.astype(F32), axis=0)
    stream_grad = (g_out.astype(F32) + piece).astype(BF16)
    stream_full = lax.all_gather(stream_grad, "head", axis=0, tiled=True)
    tiles = (LINKS * columns // HEAD_DIM, row_count, row_count)
    grad, tile, inverse = call(
        functools.partial(grad_body, columns),
        (shape((columns + META, row_count), BF16), shape(tiles, F32), shape((8, row_count), F32)),
        (w_out, stream_full, own, one, far, two),
        [VMEM] * 6,
        2 * columns * model * row_count + 2 * LINKS * square,
        2 * model * (columns + row_count),
        LINKS * columns // HEAD_DIM * row_count * row_count,
    )
    grad_one, grad_two, grad_far = [exchange(grad, slot) for slot in (1, 2, 3)]
    grad_queries, acc = call(
        functools.partial(local_body, columns),
        (shape((columns, row_count), BF16), shape((2 * columns, row_count), F32)),
        (own, one, two, far, grad, tile, inverse),
        [VMEM] * 7,
        3 * LINKS * square,
        8 * message * row_count,
    )
    acc = call(
        functools.partial(middle_body, columns),
        shape((2 * columns, row_count), F32),
        (own, two, far, grad_two, grad_far, acc),
        [VMEM] * 6,
        8 * square,
        8 * message * row_count,
        2 * columns // HEAD_DIM * row_count * row_count,
    )
    grad_keys, grad_values = call(
        functools.partial(last_body, columns),
        (shape((columns, row_count), BF16), shape((columns, row_count), BF16)),
        (own, one, grad_one, acc),
        [VMEM] * 4,
        4 * square,
        8 * message * row_count,
        columns // HEAD_DIM * row_count * row_count,
    )
    return (stream_grad.T, grad_queries.T, grad_keys.T, grad_values.T)


def solution(mesh):
    in_specs = (
        P("head", "ctx"),
        P(None, "head", "ctx"),
        P(None, "head"),
        P(None, "head", None),
        P("head", "ctx"),
        P("head", None),
        P("ctx", "head"),
        P("ctx", "head"),
        P("ctx", "head"),
        P("ctx", None, None),
        P("ctx"),
    )
    out_specs = (P("ctx", "head"), P("ctx", "head"), P("ctx", "head"), P("ctx", "head"))
    return jax.shard_map(
        per_device, mesh=mesh, in_specs=in_specs, out_specs=out_specs, check_vma=False
    )
```

```python
import functools
import math

import jax
import jax.numpy as jnp
from jax import lax
from jax.experimental import pallas as pl
from jax.experimental.pallas import tpu as pltpu
from jax.sharding import PartitionSpec as P

HEAD_DIM = 64
KW = 31
LINKS = 4
HALF = 15
LANES = 128
META = 16
PAD = 16
NEG = -1e30
SCALE = 1.0 / math.sqrt(HEAD_DIM)
SCALE2 = SCALE * math.log2(math.e)
VMEM = pl.BlockSpec(memory_space=pltpu.VMEM)
SMEM = pl.BlockSpec(memory_space=pltpu.SMEM)
F32 = jnp.float32
BF16 = jnp.bfloat16


def call(body, out_shapes, args, specs, flops, moved, exps=0, scratch=()):
    return pl.pallas_call(
        body,
        out_shape=out_shapes,
        in_specs=specs,
        out_specs=jax.tree.map(lambda _: VMEM, out_shapes),
        scratch_shapes=list(scratch),
        compiler_params=pltpu.CompilerParams(vmem_limit_bytes=24 * 1024 * 1024),
        cost_estimate=pl.CostEstimate(flops=flops, bytes_accessed=moved, transcendentals=exps),
    )(*args)


def dot_tn(a, b):
    return lax.dot_general(a, b, (((0,), (0,)), ((), ())), preferred_element_type=F32)


def dot_nt(a, b):
    return lax.dot_general(a, b, (((1,), (1,)), ((), ())), preferred_element_type=F32)


def dot_nn(a, b):
    return lax.dot_general(a, b, (((1,), (0,)), ((), ())), preferred_element_type=F32)


def pack_body(odd_ref, mask_ref, count_ref, keys_ref, values_ref, queries_ref, out_ref):
    columns, rows = keys_ref.shape
    out_ref[0:columns, :] = keys_ref[...]
    out_ref[columns : 2 * columns, :] = values_ref[...]
    out_ref[2 * columns : 3 * columns, :] = queries_ref[...]
    row = lax.broadcasted_iota(jnp.int32, (META, rows), 0)
    first = lax.broadcasted_iota(jnp.int32, (META, rows), 1) < rows // 2
    meta = jnp.where(row == 0, count_ref[0].astype(F32), 0.0)
    links = (0, 2 - odd_ref[0], 1 + odd_ref[0], 3)
    for slot, link in enumerate(links):
        for kb in range(2):
            picked = []
            for qb in range(2):
                bit = (mask_ref[qb, link, kb] > 0).astype(F32)
                if slot == 0 and qb == kb:
                    bit = jnp.maximum(bit, 1.0)
                picked.append(bit)
            meta = jnp.where(
                row == 1 + 2 * slot + kb, jnp.where(first, picked[0], picked[1]), meta
            )
    out_ref[3 * columns :, :] = meta.astype(BF16)


def own_conv_body(g_ref, taps_ref, sum_out, x_ref, moved_ref, sum_ref):
    columns, rows = g_ref.shape
    x_ref[0:PAD, :] = jnp.zeros((PAD, columns), F32)
    x_ref[PAD + rows :, :] = jnp.zeros((PAD, columns), F32)
    x_ref[PAD : PAD + rows, :] = g_ref[...].astype(F32).T
    for shift in range(8):
        moved_ref[shift] = x_ref[shift : shift + rows + 24, :]
    step = 32

    def block(i, carry):
        at = pl.multiple_of(i * step, step)
        acc = jnp.zeros((step, columns), F32)
        for k in range(KW):
            a, shift = divmod(PAD + HALF - k, 8)
            acc = acc + taps_ref[k : k + 1, :] * moved_ref[shift, pl.ds(at + 8 * a, step), :]
        sum_ref[pl.ds(at, step), :] = acc
        return carry

    lax.fori_loop(0, rows // step, block, 0)
    sum_out[...] = sum_ref[...].T


def edge_body(
    odd_ref, two_ref, one_ref, taps_ref, sum_ref, value_ref, gate_ref, w_ref, out_ref, head, tail
):
    columns, rows = sum_ref.shape
    odd = odd_ref[0] > 0
    before = jnp.where(odd, one_ref[:, rows - LANES :], two_ref[:, rows - LANES :]).astype(F32)
    after = jnp.where(odd, two_ref[:, :LANES], one_ref[:, :LANES]).astype(F32)
    blank = jnp.zeros((PAD, columns), F32)
    head[0:PAD, :] = before.T[LANES - PAD :, :]
    head[PAD:, :] = blank
    tail[0:PAD, :] = blank
    tail[PAD:, :] = after.T[:PAD, :]
    first, last = blank, blank
    for d in range(1, HALF + 1):
        first = first + taps_ref[HALF + d : HALF + d + 1, :] * head[PAD - d : 2 * PAD - d, :]
        last = last + taps_ref[HALF - d : HALF - d + 1, :] * tail[d : PAD + d, :]
    rest = jnp.zeros((LANES - PAD, columns), F32)
    left = jnp.concatenate([first, rest], axis=0).T
    right = jnp.concatenate([rest, last], axis=0).T
    grad = sum_ref[...] + jnp.concatenate([left, right], axis=1)
    low = jnp.concatenate(
        [(grad * value_ref[...]).astype(BF16), (grad * gate_ref[...]).astype(BF16)], axis=0
    )
    model = w_ref.shape[0]
    chunk = 256 if model % 256 == 0 else LANES
    for at in range(0, model, chunk):
        out_ref[at : at + chunk, :] = dot_nn(w_ref[at : at + chunk, :], low).astype(BF16)


def meta_of(ref, columns):
    return ref[3 * columns : 3 * columns + META, :].astype(F32)


def limits(query_meta, key_count, slot):
    lane = lax.broadcasted_iota(jnp.int32, query_meta[0:1].shape, 1).astype(F32)
    valid = lane < query_meta[0:1]
    return [
        jnp.where(valid & (query_meta[1 + 2 * slot + kb : 2 + 2 * slot + kb] > 0.5), key_count, 0.0)
        for kb in range(2)
    ]


def masked(scores, limit_rows):
    rows = scores.shape[0]
    half = rows // 2
    parts = []
    for kb in range(2):
        index = lax.broadcasted_iota(jnp.int32, (half, scores.shape[1]), 0).astype(F32) + kb * half
        parts.append(
            jnp.where(index < limit_rows[kb], scores[kb * half : (kb + 1) * half], NEG)
        )
    return jnp.concatenate(parts, axis=0)


def pieces(value, count):
    found = []
    for _ in range(count):
        low = value.astype(BF16).astype(F32)
        found.append(low)
        value = value - low
    return found


def grad_body(
    columns, w_ref, stream_ref, own_ref, one_ref, far_ref, two_ref, out_ref, tile_out, inverse_out
):
    refs = (own_ref, one_ref, two_ref, far_ref)
    own_meta = meta_of(own_ref, columns)
    lane = lax.broadcasted_iota(jnp.int32, own_meta[0:1].shape, 1).astype(F32)
    valid = lane < own_meta[0:1]
    limit = [limits(own_meta, meta_of(refs[j], columns)[0:1], j) for j in range(LINKS)]
    low = jnp.where(valid, dot_nn(w_ref[...], stream_ref[...]), 0.0).astype(BF16)
    out_ref[0:columns, :] = low
    rows = []
    inverse_out[...] = jnp.zeros(inverse_out.shape, F32)
    for h in range(columns // HEAD_DIM):
        lo, hi = h * HEAD_DIM, (h + 1) * HEAD_DIM
        query = own_ref[2 * columns + lo : 2 * columns + hi, :]
        scores = [
            masked(dot_tn(refs[j][lo:hi, :], query) * SCALE2, limit[j]) for j in range(LINKS)
        ]
        top = functools.reduce(jnp.maximum, [jnp.max(s, axis=0, keepdims=True) for s in scores])
        total = jnp.zeros_like(top)
        mixed = jnp.zeros((HEAD_DIM, own_ref.shape[1]), F32)
        for j in range(LINKS):
            expo = jnp.exp2(scores[j] - top)
            tile_out[LINKS * h + j] = expo
            total = total + jnp.sum(expo, axis=0, keepdims=True)
            mixed = mixed + dot_nn(refs[j][columns + lo : columns + hi, :], expo.astype(BF16))
        inverse = jnp.where(valid, 1.0 / total, 0.0)
        inverse_out[h : h + 1, :] = inverse
        delta = jnp.sum(low[lo:hi].astype(F32) * mixed, axis=0, keepdims=True) * inverse
        rows += pieces(jnp.where(valid, top + jnp.log2(total), -NEG), 3)
        rows += pieces(delta, 2)
    index = lax.broadcasted_iota(jnp.int32, (META, own_meta.shape[1]), 0)
    meta = jnp.zeros((META, own_meta.shape[1]), F32)
    for i, row in enumerate(rows):
        meta = jnp.where(index == i, row, meta)
    out_ref[columns:, :] = meta.astype(BF16)


def stats_of(ref, columns, h):
    meta = ref[columns : columns + META, :].astype(F32)
    at = 5 * h
    lse = (meta[at : at + 1] + meta[at + 1 : at + 2]) + meta[at + 2 : at + 3]
    delta = meta[at + 3 : at + 4] + meta[at + 4 : at + 5]
    return lse, delta


def tile(key, value, query, grad, lse, delta, limit):
    probs = jnp.exp2(masked(dot_tn(key, query) * SCALE2 - lse, limit))
    dscore = (probs * (dot_tn(value, grad) - delta)).astype(BF16)
    return probs.astype(BF16), dscore


def local_body(
    columns,
    own_ref,
    one_ref,
    two_ref,
    far_ref,
    grad_ref,
    tile_ref,
    inverse_ref,
    query_out,
    acc_out,
):
    refs = (own_ref, one_ref, two_ref, far_ref)
    for h in range(columns // HEAD_DIM):
        lo, hi = h * HEAD_DIM, (h + 1) * HEAD_DIM
        grad = grad_ref[lo:hi, :]
        inverse = inverse_ref[h : h + 1, :]
        _, delta = stats_of(grad_ref, columns, h)
        total = jnp.zeros((HEAD_DIM, own_ref.shape[1]), F32)
        for j in range(LINKS):
            value = refs[j][columns + lo : columns + hi, :]
            probs = tile_ref[LINKS * h + j] * inverse
            dscore = (probs * (dot_tn(value, grad) - delta)).astype(BF16)
            total = total + dot_nn(refs[j][lo:hi, :], dscore)
            if j == 0:
                query = own_ref[2 * columns + lo : 2 * columns + hi, :]
                acc_out[lo:hi, :] = dot_nt(query, dscore)
                acc_out[columns + lo : columns + hi, :] = dot_nt(grad, probs.astype(BF16))
        query_out[lo:hi, :] = (total * SCALE).astype(BF16)


def remote_terms(columns, slots, own_ref, span_refs, grad_refs, h):
    lo, hi = h * HEAD_DIM, (h + 1) * HEAD_DIM
    key = own_ref[lo:hi, :]
    value = own_ref[columns + lo : columns + hi, :]
    count = meta_of(own_ref, columns)[0:1]
    key_term = value_term = 0.0
    for slot, span_ref, grad_ref in zip(slots, span_refs, grad_refs):
        query = span_ref[2 * columns + lo : 2 * columns + hi, :]
        grad = grad_ref[lo:hi, :]
        lse, delta = stats_of(grad_ref, columns, h)
        limit = limits(meta_of(span_ref, columns), count, slot)
        probs, dscore = tile(key, value, query, grad, lse, delta, limit)
        key_term = key_term + dot_nt(query, dscore)
        value_term = value_term + dot_nt(grad, probs)
    return key_term, value_term


def middle_body(columns, own_ref, one_ref, far_ref, grad_one_ref, grad_far_ref, acc_ref, acc_out):
    for h in range(columns // HEAD_DIM):
        lo, hi = h * HEAD_DIM, (h + 1) * HEAD_DIM
        key_term, value_term = remote_terms(
            columns, (1, 3), own_ref, (one_ref, far_ref), (grad_one_ref, grad_far_ref), h
        )
        acc_out[lo:hi, :] = acc_ref[lo:hi, :] + key_term
        acc_out[columns + lo : columns + hi, :] = acc_ref[columns + lo : columns + hi, :] + value_term


def last_body(columns, own_ref, two_ref, grad_two_ref, acc_ref, key_out, value_out):
    for h in range(columns // HEAD_DIM):
        lo, hi = h * HEAD_DIM, (h + 1) * HEAD_DIM
        key_term, value_term = remote_terms(
            columns, (2,), own_ref, (two_ref,), (grad_two_ref,), h
        )
        key_out[lo:hi, :] = ((acc_ref[lo:hi, :] + key_term) * SCALE).astype(BF16)
        value_out[lo:hi, :] = (acc_ref[columns + lo : columns + hi, :] + value_term).astype(BF16)


def exchange(value, slot, closed=True):
    count = lax.axis_size("ctx")
    if slot == 3:
        pairs = [(c, (c + count // 2) % count) for c in range(count)]
    else:
        pairs = [(c, (c + (1 if (c + slot) % 2 else -1)) % count) for c in range(count)]
    if not closed:
        pairs = [(i, j) for i, j in pairs if abs(i - j) == 1]
    return lax.ppermute(value, "ctx", pairs)


def per_device(
    g_conv, pre, kernel, w_point, g_out, w_out, queries, keys, values, block_mask, counts
):
    columns, row_count = g_conv.shape
    model = w_point.shape[2]
    groups = lax.axis_size("head")
    shape = jax.ShapeDtypeStruct
    queries, keys, values = (queries.T, keys.T, values.T)
    message = 3 * columns + META
    square = 2 * columns * row_count * row_count

    odd = (lax.axis_index("ctx") % 2).astype(jnp.int32).reshape(1)
    near = [exchange(g_conv, slot, closed=False) for slot in (2, 1)]
    flat = (columns, row_count)
    own = call(
        pack_body,
        shape((message, row_count), BF16),
        (odd, block_mask, counts, keys, values, queries),
        [SMEM] * 3 + [VMEM] * 3,
        0,
        4 * message * row_count,
    )
    conv = call(
        own_conv_body,
        shape(flat, F32),
        (g_conv, kernel),
        [VMEM] * 2,
        2 * KW * columns * row_count,
        6 * columns * row_count,
        0,
        (
            pltpu.VMEM((row_count + 2 * PAD, columns), F32),
            pltpu.VMEM((8, row_count + 24, columns), F32),
            pltpu.VMEM((row_count, columns), F32),
        ),
    )
    wide = pre.astype(F32)
    gate = jax.nn.sigmoid(wide[1])
    slope = wide[0] * gate * (1.0 - gate)
    w_turned = w_point.reshape(2 * columns, model).T
    point_grad = call(
        edge_body,
        shape((model, row_count), BF16),
        (odd, *near, kernel, conv, gate, slope, w_turned),
        [SMEM] + [VMEM] * 7,
        4 * columns * model * row_count,
        4 * columns * model,
        0,
        (pltpu.VMEM((2 * PAD, columns), F32), pltpu.VMEM((2 * PAD, columns), F32)),
    )
    parts = lax.all_to_all(
        point_grad.reshape(groups, columns, row_count), "head", 0, 0, tiled=False
    )
    own, _ = lax.optimization_barrier((own, point_grad))
    one, two = [exchange(own, slot) for slot in (1, 2)]
    far = exchange(own, 3)
    piece = jnp.sum(parts.astype(F32), axis=0)
    stream_grad = (g_out.astype(F32) + piece).astype(BF16)
    stream_full = lax.all_gather(stream_grad, "head", axis=0, tiled=True)
    tiles = (LINKS * columns // HEAD_DIM, row_count, row_count)
    grad, tile, inverse = call(
        functools.partial(grad_body, columns),
        (shape((columns + META, row_count), BF16), shape(tiles, F32), shape((8, row_count), F32)),
        (w_out, stream_full, own, one, far, two),
        [VMEM] * 6,
        2 * columns * model * row_count + 2 * LINKS * square,
        2 * model * (columns + row_count),
        LINKS * columns // HEAD_DIM * row_count * row_count,
    )
    grad_one, grad_two, grad_far = [exchange(grad, slot) for slot in (1, 2, 3)]
    grad_queries, acc = call(
        functools.partial(local_body, columns),
        (shape((columns, row_count), BF16), shape((2 * columns, row_count), F32)),
        (own, one, two, far, grad, tile, inverse),
        [VMEM] * 7,
        3 * LINKS * square,
        8 * message * row_count,
    )
    acc = call(
        functools.partial(middle_body, columns),
        shape((2 * columns, row_count), F32),
        (own, one, far, grad_one, grad_far, acc),
        [VMEM] * 6,
        8 * square,
        8 * message * row_count,
        2 * columns // HEAD_DIM * row_count * row_count,
    )
    grad_keys, grad_values = call(
        functools.partial(last_body, columns),
        (shape((columns, row_count), BF16), shape((columns, row_count), BF16)),
        (own, two, grad_two, acc),
        [VMEM] * 4,
        4 * square,
        8 * message * row_count,
        columns // HEAD_DIM * row_count * row_count,
    )
    return (stream_grad.T, grad_queries.T, grad_keys.T, grad_values.T)


def solution(mesh):
    in_specs = (
        P("head", "ctx"),
        P(None, "head", "ctx"),
        P(None, "head"),
        P(None, "head", None),
        P("head", "ctx"),
        P("head", None),
        P("ctx", "head"),
        P("ctx", "head"),
        P("ctx", "head"),
        P("ctx", None, None),
        P("ctx"),
    )
    out_specs = (P("ctx", "head"), P("ctx", "head"), P("ctx", "head"), P("ctx", "head"))
    return jax.shard_map(
        per_device, mesh=mesh, in_specs=in_specs, out_specs=out_specs, check_vma=False
    )
```

```python
import functools
import math

import jax
import jax.numpy as jnp
from jax import lax
from jax.experimental import pallas as pl
from jax.experimental.pallas import tpu as pltpu
from jax.sharding import PartitionSpec as P

HEAD_DIM = 64
KW = 31
LINKS = 4
HALF = 15
LANES = 128
META = 16
PAD = 16
NEG = -1e30
SCALE = 1.0 / math.sqrt(HEAD_DIM)
SCALE2 = SCALE * math.log2(math.e)
VMEM = pl.BlockSpec(memory_space=pltpu.VMEM)
SMEM = pl.BlockSpec(memory_space=pltpu.SMEM)
F32 = jnp.float32
BF16 = jnp.bfloat16


def call(body, out_shapes, args, specs, flops, moved, exps=0, scratch=()):
    return pl.pallas_call(
        body,
        out_shape=out_shapes,
        in_specs=specs,
        out_specs=jax.tree.map(lambda _: VMEM, out_shapes),
        scratch_shapes=list(scratch),
        compiler_params=pltpu.CompilerParams(vmem_limit_bytes=24 * 1024 * 1024),
        cost_estimate=pl.CostEstimate(flops=flops, bytes_accessed=moved, transcendentals=exps),
    )(*args)


def dot_tn(a, b):
    return lax.dot_general(a, b, (((0,), (0,)), ((), ())), preferred_element_type=F32)


def dot_nt(a, b):
    return lax.dot_general(a, b, (((1,), (1,)), ((), ())), preferred_element_type=F32)


def dot_nn(a, b):
    return lax.dot_general(a, b, (((1,), (0,)), ((), ())), preferred_element_type=F32)


def own_body(
    odd_ref,
    mask_ref,
    count_ref,
    keys_ref,
    values_ref,
    queries_ref,
    g_ref,
    pre_ref,
    taps_ref,
    out_ref,
    sum_out,
    gate_out,
    slope_out,
    x_ref,
    moved_ref,
    sum_ref,
):
    columns, rows = g_ref.shape
    x_ref[0:PAD, :] = jnp.zeros((PAD, columns), F32)
    x_ref[PAD + rows :, :] = jnp.zeros((PAD, columns), F32)
    x_ref[PAD : PAD + rows, :] = g_ref[...].astype(F32).T
    for shift in range(8):
        moved_ref[shift] = x_ref[shift : shift + rows + 24, :]
    out_ref[0:columns, :] = keys_ref[...]
    out_ref[columns : 2 * columns, :] = values_ref[...]
    out_ref[2 * columns : 3 * columns, :] = queries_ref[...]
    row = lax.broadcasted_iota(jnp.int32, (META, rows), 0)
    first = lax.broadcasted_iota(jnp.int32, (META, rows), 1) < rows // 2
    meta = jnp.where(row == 0, count_ref[0].astype(F32), 0.0)
    links = (0, 2 - odd_ref[0], 1 + odd_ref[0], 3)
    for slot, link in enumerate(links):
        for kb in range(2):
            picked = []
            for qb in range(2):
                bit = (mask_ref[qb, link, kb] > 0).astype(F32)
                if slot == 0 and qb == kb:
                    bit = jnp.maximum(bit, 1.0)
                picked.append(bit)
            meta = jnp.where(
                row == 1 + 2 * slot + kb, jnp.where(first, picked[0], picked[1]), meta
            )
    out_ref[3 * columns :, :] = meta.astype(BF16)
    step = 32

    def block(i, carry):
        at = pl.multiple_of(i * step, step)
        acc = jnp.zeros((step, columns), F32)
        for k in range(KW):
            a, shift = divmod(PAD + HALF - k, 8)
            acc = acc + taps_ref[k : k + 1, :] * moved_ref[shift, pl.ds(at + 8 * a, step), :]
        sum_ref[pl.ds(at, step), :] = acc
        return carry

    lax.fori_loop(0, rows // step, block, 0)
    sum_out[...] = sum_ref[...].T
    gate = jax.nn.sigmoid(pre_ref[1].astype(F32))
    gate_out[...] = gate
    slope_out[...] = pre_ref[0].astype(F32) * gate * (1.0 - gate)


def edge_body(
    odd_ref, two_ref, one_ref, taps_ref, sum_ref, gate_ref, slope_ref, w_ref, out_ref, head, tail
):
    columns, rows = sum_ref.shape
    odd = odd_ref[0] > 0
    before = jnp.where(odd, one_ref[:, rows - LANES :], two_ref[:, rows - LANES :]).astype(F32)
    after = jnp.where(odd, two_ref[:, :LANES], one_ref[:, :LANES]).astype(F32)
    blank = jnp.zeros((PAD, columns), F32)
    head[0:PAD, :] = before.T[LANES - PAD :, :]
    head[PAD:, :] = blank
    tail[0:PAD, :] = blank
    tail[PAD:, :] = after.T[:PAD, :]
    first, last = blank, blank
    for d in range(1, HALF + 1):
        first = first + taps_ref[HALF + d : HALF + d + 1, :] * head[PAD - d : 2 * PAD - d, :]
        last = last + taps_ref[HALF - d : HALF - d + 1, :] * tail[d : PAD + d, :]
    rest = jnp.zeros((LANES - PAD, columns), F32)
    left = jnp.concatenate([first, rest], axis=0).T
    right = jnp.concatenate([rest, last], axis=0).T
    grad = sum_ref[...] + jnp.concatenate([left, right], axis=1)
    low = jnp.concatenate(
        [(grad * gate_ref[...]).astype(BF16), (grad * slope_ref[...]).astype(BF16)], axis=0
    )
    model = w_ref.shape[0]
    chunk = 256 if model % 256 == 0 else LANES
    for at in range(0, model, chunk):
        out_ref[at : at + chunk, :] = dot_nn(w_ref[at : at + chunk, :], low).astype(BF16)


def meta_of(ref, columns):
    return ref[3 * columns : 3 * columns + META, :].astype(F32)


def limits(query_meta, key_count, slot):
    lane = lax.broadcasted_iota(jnp.int32, query_meta[0:1].shape, 1).astype(F32)
    valid = lane < query_meta[0:1]
    return [
        jnp.where(valid & (query_meta[1 + 2 * slot + kb : 2 + 2 * slot + kb] > 0.5), key_count, 0.0)
        for kb in range(2)
    ]


def masked(scores, limit_rows):
    rows = scores.shape[0]
    half = rows // 2
    parts = []
    for kb in range(2):
        index = lax.broadcasted_iota(jnp.int32, (half, scores.shape[1]), 0).astype(F32) + kb * half
        parts.append(
            jnp.where(index < limit_rows[kb], scores[kb * half : (kb + 1) * half], NEG)
        )
    return jnp.concatenate(parts, axis=0)


def pieces(value, count):
    found = []
    for _ in range(count):
        low = value.astype(BF16).astype(F32)
        found.append(low)
        value = value - low
    return found


def grad_body(
    columns, w_ref, stream_ref, own_ref, one_ref, far_ref, two_ref, out_ref, tile_out, inverse_out
):
    refs = (own_ref, one_ref, two_ref, far_ref)
    own_meta = meta_of(own_ref, columns)
    lane = lax.broadcasted_iota(jnp.int32, own_meta[0:1].shape, 1).astype(F32)
    valid = lane < own_meta[0:1]
    limit = [limits(own_meta, meta_of(refs[j], columns)[0:1], j) for j in range(LINKS)]
    low = jnp.where(valid, dot_nn(w_ref[...], stream_ref[...]), 0.0).astype(BF16)
    out_ref[0:columns, :] = low
    rows = []
    inverse_out[...] = jnp.zeros(inverse_out.shape, F32)
    for h in range(columns // HEAD_DIM):
        lo, hi = h * HEAD_DIM, (h + 1) * HEAD_DIM
        query = own_ref[2 * columns + lo : 2 * columns + hi, :]
        scores = [
            masked(dot_tn(refs[j][lo:hi, :], query) * SCALE2, limit[j]) for j in range(LINKS)
        ]
        top = functools.reduce(jnp.maximum, [jnp.max(s, axis=0, keepdims=True) for s in scores])
        total = jnp.zeros_like(top)
        mixed = jnp.zeros((HEAD_DIM, own_ref.shape[1]), F32)
        for j in range(LINKS):
            expo = jnp.exp2(scores[j] - top)
            tile_out[LINKS * h + j] = expo
            total = total + jnp.sum(expo, axis=0, keepdims=True)
            mixed = mixed + dot_nn(refs[j][columns + lo : columns + hi, :], expo.astype(BF16))
        inverse = jnp.where(valid, 1.0 / total, 0.0)
        inverse_out[h : h + 1, :] = inverse
        delta = jnp.sum(low[lo:hi].astype(F32) * mixed, axis=0, keepdims=True) * inverse
        rows += pieces(jnp.where(valid, top + jnp.log2(total), -NEG), 3)
        rows += pieces(delta, 2)
    index = lax.broadcasted_iota(jnp.int32, (META, own_meta.shape[1]), 0)
    meta = jnp.zeros((META, own_meta.shape[1]), F32)
    for i, row in enumerate(rows):
        meta = jnp.where(index == i, row, meta)
    out_ref[columns:, :] = meta.astype(BF16)


def stats_of(ref, columns, h):
    meta = ref[columns : columns + META, :].astype(F32)
    at = 5 * h
    lse = (meta[at : at + 1] + meta[at + 1 : at + 2]) + meta[at + 2 : at + 3]
    delta = meta[at + 3 : at + 4] + meta[at + 4 : at + 5]
    return lse, delta


def tile(key, value, query, grad, lse, delta, limit):
    probs = jnp.exp2(masked(dot_tn(key, query) * SCALE2 - lse, limit))
    dscore = (probs * (dot_tn(value, grad) - delta)).astype(BF16)
    return probs.astype(BF16), dscore


def local_body(
    columns,
    own_ref,
    one_ref,
    two_ref,
    far_ref,
    grad_ref,
    tile_ref,
    inverse_ref,
    query_out,
    acc_out,
):
    refs = (own_ref, one_ref, two_ref, far_ref)
    for h in range(columns // HEAD_DIM):
        lo, hi = h * HEAD_DIM, (h + 1) * HEAD_DIM
        grad = grad_ref[lo:hi, :]
        inverse = inverse_ref[h : h + 1, :]
        _, delta = stats_of(grad_ref, columns, h)
        total = jnp.zeros((HEAD_DIM, own_ref.shape[1]), F32)
        for j in range(LINKS):
            value = refs[j][columns + lo : columns + hi, :]
            probs = tile_ref[LINKS * h + j] * inverse
            dscore = (probs * (dot_tn(value, grad) - delta)).astype(BF16)
            total = total + dot_nn(refs[j][lo:hi, :], dscore)
            if j == 0:
                query = own_ref[2 * columns + lo : 2 * columns + hi, :]
                acc_out[lo:hi, :] = dot_nt(query, dscore)
                acc_out[columns + lo : columns + hi, :] = dot_nt(grad, probs.astype(BF16))
        query_out[lo:hi, :] = (total * SCALE).astype(BF16)


def remote_terms(columns, slots, own_ref, span_refs, grad_refs, h):
    lo, hi = h * HEAD_DIM, (h + 1) * HEAD_DIM
    key = own_ref[lo:hi, :]
    value = own_ref[columns + lo : columns + hi, :]
    count = meta_of(own_ref, columns)[0:1]
    key_term = value_term = 0.0
    for slot, span_ref, grad_ref in zip(slots, span_refs, grad_refs):
        query = span_ref[2 * columns + lo : 2 * columns + hi, :]
        grad = grad_ref[lo:hi, :]
        lse, delta = stats_of(grad_ref, columns, h)
        limit = limits(meta_of(span_ref, columns), count, slot)
        probs, dscore = tile(key, value, query, grad, lse, delta, limit)
        key_term = key_term + dot_nt(query, dscore)
        value_term = value_term + dot_nt(grad, probs)
    return key_term, value_term


def middle_body(columns, own_ref, one_ref, far_ref, grad_one_ref, grad_far_ref, acc_ref, acc_out):
    for h in range(columns // HEAD_DIM):
        lo, hi = h * HEAD_DIM, (h + 1) * HEAD_DIM
        key_term, value_term = remote_terms(
            columns, (1, 3), own_ref, (one_ref, far_ref), (grad_one_ref, grad_far_ref), h
        )
        acc_out[lo:hi, :] = acc_ref[lo:hi, :] + key_term
        acc_out[columns + lo : columns + hi, :] = acc_ref[columns + lo : columns + hi, :] + value_term


def last_body(columns, own_ref, two_ref, grad_two_ref, acc_ref, key_out, value_out):
    for h in range(columns // HEAD_DIM):
        lo, hi = h * HEAD_DIM, (h + 1) * HEAD_DIM
        key_term, value_term = remote_terms(
            columns, (2,), own_ref, (two_ref,), (grad_two_ref,), h
        )
        key_out[lo:hi, :] = ((acc_ref[lo:hi, :] + key_term) * SCALE).astype(BF16)
        value_out[lo:hi, :] = (acc_ref[columns + lo : columns + hi, :] + value_term).astype(BF16)


def exchange(value, slot, closed=True):
    count = lax.axis_size("ctx")
    if slot == 3:
        pairs = [(c, (c + count // 2) % count) for c in range(count)]
    else:
        pairs = [(c, (c + (1 if (c + slot) % 2 else -1)) % count) for c in range(count)]
    if not closed:
        pairs = [(i, j) for i, j in pairs if abs(i - j) == 1]
    return lax.ppermute(value, "ctx", pairs)


def per_device(
    g_conv, pre, kernel, w_point, g_out, w_out, queries, keys, values, block_mask, counts
):
    columns, row_count = g_conv.shape
    model = w_point.shape[2]
    groups = lax.axis_size("head")
    shape = jax.ShapeDtypeStruct
    queries, keys, values = (queries.T, keys.T, values.T)
    message = 3 * columns + META
    square = 2 * columns * row_count * row_count

    odd = (lax.axis_index("ctx") % 2).astype(jnp.int32).reshape(1)
    near = [exchange(g_conv, slot, closed=False) for slot in (2, 1)]
    flat = (columns, row_count)
    own, conv, gate, slope = call(
        own_body,
        (shape((message, row_count), BF16),) + (shape(flat, F32),) * 3,
        (odd, block_mask, counts, keys, values, queries, g_conv, pre, kernel),
        [SMEM] * 3 + [VMEM] * 6,
        2 * KW * columns * row_count,
        6 * message * row_count,
        columns * row_count,
        (
            pltpu.VMEM((row_count + 2 * PAD, columns), F32),
            pltpu.VMEM((8, row_count + 24, columns), F32),
            pltpu.VMEM((row_count, columns), F32),
        ),
    )
    w_turned = w_point.reshape(2 * columns, model).T
    point_grad = call(
        edge_body,
        shape((model, row_count), BF16),
        (odd, *near, kernel, conv, gate, slope, w_turned),
        [SMEM] + [VMEM] * 7,
        4 * columns * model * row_count,
        4 * columns * model,
        0,
        (pltpu.VMEM((2 * PAD, columns), F32), pltpu.VMEM((2 * PAD, columns), F32)),
    )
    parts = lax.all_to_all(
        point_grad.reshape(groups, columns, row_count), "head", 0, 0, tiled=False
    )
    own, _ = lax.optimization_barrier((own, point_grad))
    two, one, far = [exchange(own, slot) for slot in (2, 1, 3)]
    piece = jnp.sum(parts.astype(F32), axis=0)
    stream_grad = (g_out.astype(F32) + piece).astype(BF16)
    stream_full = lax.all_gather(stream_grad, "head", axis=0, tiled=True)
    tiles = (LINKS * columns // HEAD_DIM, row_count, row_count)
    grad, tile, inverse = call(
        functools.partial(grad_body, columns),
        (shape((columns + META, row_count), BF16), shape(tiles, F32), shape((8, row_count), F32)),
        (w_out, stream_full, own, one, far, two),
        [VMEM] * 6,
        2 * columns * model * row_count + 2 * LINKS * square,
        2 * model * (columns + row_count),
        LINKS * columns // HEAD_DIM * row_count * row_count,
    )
    grad_one, grad_two, grad_far = [exchange(grad, slot) for slot in (1, 2, 3)]
    grad_queries, acc = call(
        functools.partial(local_body, columns),
        (shape((columns, row_count), BF16), shape((2 * columns, row_count), F32)),
        (own, one, two, far, grad, tile, inverse),
        [VMEM] * 7,
        3 * LINKS * square,
        8 * message * row_count,
    )
    acc = call(
        functools.partial(middle_body, columns),
        shape((2 * columns, row_count), F32),
        (own, one, far, grad_one, grad_far, acc),
        [VMEM] * 6,
        8 * square,
        8 * message * row_count,
        2 * columns // HEAD_DIM * row_count * row_count,
    )
    grad_keys, grad_values = call(
        functools.partial(last_body, columns),
        (shape((columns, row_count), BF16), shape((columns, row_count), BF16)),
        (own, two, grad_two, acc),
        [VMEM] * 4,
        4 * square,
        8 * message * row_count,
        columns // HEAD_DIM * row_count * row_count,
    )
    return (stream_grad.T, grad_queries.T, grad_keys.T, grad_values.T)


def solution(mesh):
    in_specs = (
        P("head", "ctx"),
        P(None, "head", "ctx"),
        P(None, "head"),
        P(None, "head", None),
        P("head", "ctx"),
        P("head", None),
        P("ctx", "head"),
        P("ctx", "head"),
        P("ctx", "head"),
        P("ctx", None, None),
        P("ctx"),
    )
    out_specs = (P("ctx", "head"), P("ctx", "head"), P("ctx", "head"), P("ctx", "head"))
    return jax.shard_map(
        per_device, mesh=mesh, in_specs=in_specs, out_specs=out_specs, check_vma=False
    )
```

```python
import functools
import math

import jax
import jax.numpy as jnp
from jax import lax
from jax.experimental import pallas as pl
from jax.experimental.pallas import tpu as pltpu
from jax.sharding import PartitionSpec as P

HEAD_DIM = 64
KW = 31
LINKS = 4
HALF = 15
LANES = 128
META = 16
PAD = 16
NEG = -1e30
SCALE = 1.0 / math.sqrt(HEAD_DIM)
SCALE2 = SCALE * math.log2(math.e)
VMEM = pl.BlockSpec(memory_space=pltpu.VMEM)
F32 = jnp.float32
BF16 = jnp.bfloat16


def call(body, out_shapes, args, specs, flops, moved, exps=0, scratch=()):
    return pl.pallas_call(
        body,
        out_shape=out_shapes,
        in_specs=specs,
        out_specs=jax.tree.map(lambda _: VMEM, out_shapes),
        scratch_shapes=list(scratch),
        compiler_params=pltpu.CompilerParams(vmem_limit_bytes=24 * 1024 * 1024),
        cost_estimate=pl.CostEstimate(flops=flops, bytes_accessed=moved, transcendentals=exps),
    )(*args)


def dot_tn(a, b):
    return lax.dot_general(a, b, (((0,), (0,)), ((), ())), preferred_element_type=F32)


def dot_nt(a, b):
    return lax.dot_general(a, b, (((1,), (1,)), ((), ())), preferred_element_type=F32)


def dot_nn(a, b):
    return lax.dot_general(a, b, (((1,), (0,)), ((), ())), preferred_element_type=F32)


def own_body(
    odd_ref,
    mask_ref,
    count_ref,
    keys_ref,
    values_ref,
    queries_ref,
    g_ref,
    pre_ref,
    taps_ref,
    out_ref,
    sum_out,
    gate_out,
    slope_out,
    x_ref,
    moved_ref,
    sum_ref,
):
    columns, rows = g_ref.shape
    x_ref[0:PAD, :] = jnp.zeros((PAD, columns), F32)
    x_ref[PAD + rows :, :] = jnp.zeros((PAD, columns), F32)
    x_ref[PAD : PAD + rows, :] = g_ref[...].astype(F32).T
    for shift in range(8):
        moved_ref[shift] = x_ref[shift : shift + rows + 24, :]
    out_ref[0:columns, :] = keys_ref[...]
    out_ref[columns : 2 * columns, :] = values_ref[...]
    out_ref[2 * columns : 3 * columns, :] = queries_ref[...]
    row = lax.broadcasted_iota(jnp.int32, (META, rows), 0)
    first = lax.broadcasted_iota(jnp.int32, (META, rows), 1) < rows // 2
    odd = odd_ref[...] > 0
    meta = jnp.where(row == 0, count_ref[...].astype(F32), 0.0)
    for kb in range(2):
        bits = []
        for qb in range(2):
            given = [
                (mask_ref[qb, kb : kb + 1, j : j + 1] > 0).astype(F32) for j in range(LINKS)
            ]
            own_bit = jnp.ones_like(given[0]) if qb == kb else given[0]
            bits.append(
                (
                    own_bit,
                    jnp.where(odd, given[1], given[2]),
                    jnp.where(odd, given[2], given[1]),
                    given[3],
                )
            )
        for slot in range(LINKS):
            meta = jnp.where(
                row == 1 + 2 * slot + kb, jnp.where(first, bits[0][slot], bits[1][slot]), meta
            )
    out_ref[3 * columns :, :] = meta.astype(BF16)
    step = 32

    def block(i, carry):
        at = pl.multiple_of(i * step, step)
        acc = jnp.zeros((step, columns), F32)
        for k in range(KW):
            a, shift = divmod(PAD + HALF - k, 8)
            acc = acc + taps_ref[k : k + 1, :] * moved_ref[shift, pl.ds(at + 8 * a, step), :]
        sum_ref[pl.ds(at, step), :] = acc
        return carry

    lax.fori_loop(0, rows // step, block, 0)
    sum_out[...] = sum_ref[...].T
    gate = jax.nn.sigmoid(pre_ref[1].astype(F32))
    gate_out[...] = gate
    slope_out[...] = pre_ref[0].astype(F32) * gate * (1.0 - gate)


def edge_body(
    odd_ref, two_ref, one_ref, taps_ref, sum_ref, gate_ref, slope_ref, w_ref, out_ref, head, tail
):
    columns, rows = sum_ref.shape
    odd = jnp.broadcast_to(odd_ref[...] > 0, (columns, LANES))
    before = jnp.where(odd, one_ref[:, rows - LANES :], two_ref[:, rows - LANES :]).astype(F32)
    after = jnp.where(odd, two_ref[:, :LANES], one_ref[:, :LANES]).astype(F32)
    blank = jnp.zeros((PAD, columns), F32)
    head[0:PAD, :] = before.T[LANES - PAD :, :]
    head[PAD:, :] = blank
    tail[0:PAD, :] = blank
    tail[PAD:, :] = after.T[:PAD, :]
    first, last = blank, blank
    for d in range(1, HALF + 1):
        first = first + taps_ref[HALF + d : HALF + d + 1, :] * head[PAD - d : 2 * PAD - d, :]
        last = last + taps_ref[HALF - d : HALF - d + 1, :] * tail[d : PAD + d, :]
    rest = jnp.zeros((LANES - PAD, columns), F32)
    left = jnp.concatenate([first, rest], axis=0).T
    right = jnp.concatenate([rest, last], axis=0).T
    grad = sum_ref[...] + jnp.concatenate([left, right], axis=1)
    low = jnp.concatenate(
        [(grad * gate_ref[...]).astype(BF16), (grad * slope_ref[...]).astype(BF16)], axis=0
    )
    model = w_ref.shape[0]
    chunk = 256 if model % 256 == 0 else LANES
    for at in range(0, model, chunk):
        out_ref[at : at + chunk, :] = dot_nn(w_ref[at : at + chunk, :], low).astype(BF16)


def meta_of(ref, columns):
    return ref[3 * columns : 3 * columns + META, :].astype(F32)


def limits(query_meta, key_count, slot):
    lane = lax.broadcasted_iota(jnp.int32, query_meta[0:1].shape, 1).astype(F32)
    valid = lane < query_meta[0:1]
    return [
        jnp.where(valid & (query_meta[1 + 2 * slot + kb : 2 + 2 * slot + kb] > 0.5), key_count, 0.0)
        for kb in range(2)
    ]


def masked(scores, limit_rows):
    rows = scores.shape[0]
    half = rows // 2
    parts = []
    for kb in range(2):
        index = lax.broadcasted_iota(jnp.int32, (half, scores.shape[1]), 0).astype(F32) + kb * half
        parts.append(
            jnp.where(index < limit_rows[kb], scores[kb * half : (kb + 1) * half], NEG)
        )
    return jnp.concatenate(parts, axis=0)


def pieces(value, count):
    found = []
    for _ in range(count):
        low = value.astype(BF16).astype(F32)
        found.append(low)
        value = value - low
    return found


def grad_body(
    columns, w_ref, stream_ref, own_ref, one_ref, far_ref, two_ref, out_ref, tile_out, inverse_out
):
    refs = (own_ref, one_ref, two_ref, far_ref)
    own_meta = meta_of(own_ref, columns)
    lane = lax.broadcasted_iota(jnp.int32, own_meta[0:1].shape, 1).astype(F32)
    valid = lane < own_meta[0:1]
    limit = [limits(own_meta, meta_of(refs[j], columns)[0:1], j) for j in range(LINKS)]
    low = jnp.where(valid, dot_nn(w_ref[...], stream_ref[...]), 0.0).astype(BF16)
    out_ref[0:columns, :] = low
    rows = []
    inverse_out[...] = jnp.zeros(inverse_out.shape, F32)
    for h in range(columns // HEAD_DIM):
        lo, hi = h * HEAD_DIM, (h + 1) * HEAD_DIM
        query = own_ref[2 * columns + lo : 2 * columns + hi, :]
        scores = [
            masked(dot_tn(refs[j][lo:hi, :], query) * SCALE2, limit[j]) for j in range(LINKS)
        ]
        top = functools.reduce(jnp.maximum, [jnp.max(s, axis=0, keepdims=True) for s in scores])
        total = jnp.zeros_like(top)
        mixed = jnp.zeros_like(top)
        for j in range(LINKS):
            expo = jnp.exp2(scores[j] - top)
            dprob = dot_tn(refs[j][columns + lo : columns + hi, :], low[lo:hi])
            tile_out[2 * (LINKS * h + j)] = expo
            tile_out[2 * (LINKS * h + j) + 1] = dprob
            total = total + jnp.sum(expo, axis=0, keepdims=True)
            mixed = mixed + jnp.sum(expo * dprob, axis=0, keepdims=True)
        inverse = jnp.where(valid, 1.0 / total, 0.0)
        inverse_out[h : h + 1, :] = inverse
        delta = mixed * inverse
        rows += pieces(jnp.where(valid, top + jnp.log2(total), -NEG), 3)
        rows += pieces(delta, 2)
    index = lax.broadcasted_iota(jnp.int32, (META, own_meta.shape[1]), 0)
    meta = jnp.zeros((META, own_meta.shape[1]), F32)
    for i, row in enumerate(rows):
        meta = jnp.where(index == i, row, meta)
    out_ref[columns:, :] = meta.astype(BF16)


def stats_of(ref, columns, h):
    meta = ref[columns : columns + META, :].astype(F32)
    at = 5 * h
    lse = (meta[at : at + 1] + meta[at + 1 : at + 2]) + meta[at + 2 : at + 3]
    delta = meta[at + 3 : at + 4] + meta[at + 4 : at + 5]
    return lse, delta


def tile(key, value, query, grad, lse, delta, limit):
    probs = jnp.exp2(masked(dot_tn(key, query) * SCALE2 - lse, limit))
    dscore = (probs * (dot_tn(value, grad) - delta)).astype(BF16)
    return probs.astype(BF16), dscore


def local_body(
    columns,
    own_ref,
    one_ref,
    two_ref,
    far_ref,
    grad_ref,
    tile_ref,
    inverse_ref,
    query_out,
    acc_out,
):
    refs = (own_ref, one_ref, two_ref, far_ref)
    for h in range(columns // HEAD_DIM):
        lo, hi = h * HEAD_DIM, (h + 1) * HEAD_DIM
        grad = grad_ref[lo:hi, :]
        inverse = inverse_ref[h : h + 1, :]
        _, delta = stats_of(grad_ref, columns, h)
        total = jnp.zeros((HEAD_DIM, own_ref.shape[1]), F32)
        for j in range(LINKS):
            probs = tile_ref[2 * (LINKS * h + j)] * inverse
            dscore = (probs * (tile_ref[2 * (LINKS * h + j) + 1] - delta)).astype(BF16)
            total = total + dot_nn(refs[j][lo:hi, :], dscore)
            if j == 0:
                query = own_ref[2 * columns + lo : 2 * columns + hi, :]
                acc_out[lo:hi, :] = dot_nt(query, dscore)
                acc_out[columns + lo : columns + hi, :] = dot_nt(grad, probs.astype(BF16))
        query_out[lo:hi, :] = (total * SCALE).astype(BF16)


def remote_terms(columns, slots, own_ref, span_refs, grad_refs, h):
    lo, hi = h * HEAD_DIM, (h + 1) * HEAD_DIM
    key = own_ref[lo:hi, :]
    value = own_ref[columns + lo : columns + hi, :]
    count = meta_of(own_ref, columns)[0:1]
    key_term = value_term = 0.0
    for slot, span_ref, grad_ref in zip(slots, span_refs, grad_refs):
        query = span_ref[2 * columns + lo : 2 * columns + hi, :]
        grad = grad_ref[lo:hi, :]
        lse, delta = stats_of(grad_ref, columns, h)
        limit = limits(meta_of(span_ref, columns), count, slot)
        probs, dscore = tile(key, value, query, grad, lse, delta, limit)
        key_term = key_term + dot_nt(query, dscore)
        value_term = value_term + dot_nt(grad, probs)
    return key_term, value_term


def middle_body(columns, own_ref, one_ref, far_ref, grad_one_ref, grad_far_ref, acc_ref, acc_out):
    for h in range(columns // HEAD_DIM):
        lo, hi = h * HEAD_DIM, (h + 1) * HEAD_DIM
        key_term, value_term = remote_terms(
            columns, (1, 3), own_ref, (one_ref, far_ref), (grad_one_ref, grad_far_ref), h
        )
        acc_out[lo:hi, :] = acc_ref[lo:hi, :] + key_term
        acc_out[columns + lo : columns + hi, :] = acc_ref[columns + lo : columns + hi, :] + value_term


def last_body(columns, own_ref, two_ref, grad_two_ref, acc_ref, key_out, value_out):
    for h in range(columns // HEAD_DIM):
        lo, hi = h * HEAD_DIM, (h + 1) * HEAD_DIM
        key_term, value_term = remote_terms(
            columns, (2,), own_ref, (two_ref,), (grad_two_ref,), h
        )
        key_out[lo:hi, :] = ((acc_ref[lo:hi, :] + key_term) * SCALE).astype(BF16)
        value_out[lo:hi, :] = (acc_ref[columns + lo : columns + hi, :] + value_term).astype(BF16)


def exchange(value, slot, closed=True):
    count = lax.axis_size("ctx")
    if slot == 3:
        pairs = [(c, (c + count // 2) % count) for c in range(count)]
    else:
        pairs = [(c, (c + (1 if (c + slot) % 2 else -1)) % count) for c in range(count)]
    if not closed:
        pairs = [(i, j) for i, j in pairs if abs(i - j) == 1]
    return lax.ppermute(value, "ctx", pairs)


def per_device(
    g_conv, pre, kernel, w_point, g_out, w_out, queries, keys, values, block_mask, counts
):
    columns, row_count = g_conv.shape
    model = w_point.shape[2]
    groups = lax.axis_size("head")
    shape = jax.ShapeDtypeStruct
    queries, keys, values = (queries.T, keys.T, values.T)
    message = 3 * columns + META
    square = 2 * columns * row_count * row_count

    odd = (lax.axis_index("ctx") % 2).astype(jnp.int32).reshape(1, 1)
    near = [exchange(g_conv, slot, closed=False) for slot in (2, 1)]
    flat = (columns, row_count)
    own, conv, gate, slope = call(
        own_body,
        (shape((message, row_count), BF16),) + (shape(flat, F32),) * 3,
        (
            odd,
            block_mask.transpose(0, 2, 1),
            counts.reshape(1, 1),
            keys,
            values,
            queries,
            g_conv,
            pre,
            kernel,
        ),
        [VMEM] * 9,
        2 * KW * columns * row_count,
        6 * message * row_count,
        columns * row_count,
        (
            pltpu.VMEM((row_count + 2 * PAD, columns), F32),
            pltpu.VMEM((8, row_count + 24, columns), F32),
            pltpu.VMEM((row_count, columns), F32),
        ),
    )
    w_turned = w_point.reshape(2 * columns, model).T
    point_grad = call(
        edge_body,
        shape((model, row_count), BF16),
        (odd, *near, kernel, conv, gate, slope, w_turned),
        [VMEM] * 8,
        4 * columns * model * row_count,
        4 * columns * model,
        0,
        (pltpu.VMEM((2 * PAD, columns), F32), pltpu.VMEM((2 * PAD, columns), F32)),
    )
    parts = lax.all_to_all(
        point_grad.reshape(groups, columns, row_count), "head", 0, 0, tiled=False
    )
    own, _ = lax.optimization_barrier((own, point_grad))
    two, one, far = [exchange(own, slot) for slot in (2, 1, 3)]
    piece = jnp.sum(parts.astype(F32), axis=0)
    stream_grad = (g_out.astype(F32) + piece).astype(BF16)
    stream_full = lax.all_gather(stream_grad, "head", axis=0, tiled=True)
    tiles = (2 * LINKS * columns // HEAD_DIM, row_count, row_count)
    grad, tile, inverse = call(
        functools.partial(grad_body, columns),
        (shape((columns + META, row_count), BF16), shape(tiles, F32), shape((8, row_count), F32)),
        (w_out, stream_full, own, one, far, two),
        [VMEM] * 6,
        2 * columns * model * row_count + 2 * LINKS * square,
        2 * model * (columns + row_count),
        LINKS * columns // HEAD_DIM * row_count * row_count,
    )
    grad_one, grad_two, grad_far = [exchange(grad, slot) for slot in (1, 2, 3)]
    grad_queries, acc = call(
        functools.partial(local_body, columns),
        (shape((columns, row_count), BF16), shape((2 * columns, row_count), F32)),
        (own, one, two, far, grad, tile, inverse),
        [VMEM] * 7,
        3 * LINKS * square,
        8 * message * row_count,
    )
    acc = call(
        functools.partial(middle_body, columns),
        shape((2 * columns, row_count), F32),
        (own, one, far, grad_one, grad_far, acc),
        [VMEM] * 6,
        8 * square,
        8 * message * row_count,
        2 * columns // HEAD_DIM * row_count * row_count,
    )
    grad_keys, grad_values = call(
        functools.partial(last_body, columns),
        (shape((columns, row_count), BF16), shape((columns, row_count), BF16)),
        (own, two, grad_two, acc),
        [VMEM] * 4,
        4 * square,
        8 * message * row_count,
        columns // HEAD_DIM * row_count * row_count,
    )
    return (stream_grad.T, grad_queries.T, grad_keys.T, grad_values.T)


def solution(mesh):
    in_specs = (
        P("head", "ctx"),
        P(None, "head", "ctx"),
        P(None, "head"),
        P(None, "head", None),
        P("head", "ctx"),
        P("head", None),
        P("ctx", "head"),
        P("ctx", "head"),
        P("ctx", "head"),
        P("ctx", None, None),
        P("ctx"),
    )
    out_specs = (P("ctx", "head"), P("ctx", "head"), P("ctx", "head"), P("ctx", "head"))
    return jax.shard_map(
        per_device, mesh=mesh, in_specs=in_specs, out_specs=out_specs, check_vma=False
    )
```

```python
import functools
import math

import jax
import jax.numpy as jnp
from jax import lax
from jax.experimental import pallas as pl
from jax.experimental.pallas import tpu as pltpu
from jax.sharding import PartitionSpec as P

HEAD_DIM = 64
KW = 31
LINKS = 4
HALF = 15
LANES = 128
META = 16
PAD = 16
NEG = -1e30
SCALE = 1.0 / math.sqrt(HEAD_DIM)
SCALE2 = SCALE * math.log2(math.e)
VMEM = pl.BlockSpec(memory_space=pltpu.VMEM)
F32 = jnp.float32
BF16 = jnp.bfloat16


def call(body, out_shapes, args, specs, flops, moved, exps=0, scratch=()):
    return pl.pallas_call(
        body,
        out_shape=out_shapes,
        in_specs=specs,
        out_specs=jax.tree.map(lambda _: VMEM, out_shapes),
        scratch_shapes=list(scratch),
        compiler_params=pltpu.CompilerParams(vmem_limit_bytes=24 * 1024 * 1024),
        cost_estimate=pl.CostEstimate(flops=flops, bytes_accessed=moved, transcendentals=exps),
    )(*args)


def dot_tn(a, b):
    return lax.dot_general(a, b, (((0,), (0,)), ((), ())), preferred_element_type=F32)


def dot_nt(a, b):
    return lax.dot_general(a, b, (((1,), (1,)), ((), ())), preferred_element_type=F32)


def dot_nn(a, b):
    return lax.dot_general(a, b, (((1,), (0,)), ((), ())), preferred_element_type=F32)


def own_body(
    odd_ref,
    mask_ref,
    count_ref,
    keys_ref,
    values_ref,
    queries_ref,
    g_ref,
    pre_ref,
    taps_ref,
    out_ref,
    sum_out,
    gate_out,
    slope_out,
    x_ref,
    moved_ref,
    sum_ref,
):
    columns, rows = g_ref.shape
    x_ref[0:PAD, :] = jnp.zeros((PAD, columns), F32)
    x_ref[PAD + rows :, :] = jnp.zeros((PAD, columns), F32)
    x_ref[PAD : PAD + rows, :] = g_ref[...].astype(F32).T
    for shift in range(8):
        moved_ref[shift] = x_ref[shift : shift + rows + 24, :]
    out_ref[0:columns, :] = keys_ref[...]
    out_ref[columns : 2 * columns, :] = values_ref[...]
    out_ref[2 * columns : 3 * columns, :] = queries_ref[...]
    row = lax.broadcasted_iota(jnp.int32, (META, rows), 0)
    first = lax.broadcasted_iota(jnp.int32, (META, rows), 1) < rows // 2
    odd = odd_ref[...] > 0
    meta = jnp.where(row == 0, count_ref[...].astype(F32).reshape(1, 1), 0.0)
    for kb in range(2):
        bits = []
        for qb in range(2):
            given = [
                (mask_ref[qb, kb : kb + 1, j : j + 1] > 0).astype(F32) for j in range(LINKS)
            ]
            own_bit = jnp.ones_like(given[0]) if qb == kb else given[0]
            bits.append(
                (
                    own_bit,
                    jnp.where(odd, given[1], given[2]),
                    jnp.where(odd, given[2], given[1]),
                    given[3],
                )
            )
        for slot in range(LINKS):
            meta = jnp.where(
                row == 1 + 2 * slot + kb, jnp.where(first, bits[0][slot], bits[1][slot]), meta
            )
    out_ref[3 * columns :, :] = meta.astype(BF16)
    step = 32

    def block(i, carry):
        at = pl.multiple_of(i * step, step)
        acc = jnp.zeros((step, columns), F32)
        for k in range(KW):
            a, shift = divmod(PAD + HALF - k, 8)
            acc = acc + taps_ref[k : k + 1, :] * moved_ref[shift, pl.ds(at + 8 * a, step), :]
        sum_ref[pl.ds(at, step), :] = acc
        return carry

    lax.fori_loop(0, rows // step, block, 0)
    sum_out[...] = sum_ref[...].T
    gate = jax.nn.sigmoid(pre_ref[1].astype(F32))
    gate_out[...] = gate
    slope_out[...] = pre_ref[0].astype(F32) * gate * (1.0 - gate)


def edge_body(
    odd_ref, two_ref, one_ref, taps_ref, sum_ref, gate_ref, slope_ref, w_ref, out_ref, head, tail
):
    columns, rows = sum_ref.shape
    odd = jnp.broadcast_to(odd_ref[...] > 0, (columns, LANES))
    before = jnp.where(odd, one_ref[:, rows - LANES :], two_ref[:, rows - LANES :]).astype(F32)
    after = jnp.where(odd, two_ref[:, :LANES], one_ref[:, :LANES]).astype(F32)
    blank = jnp.zeros((PAD, columns), F32)
    head[0:PAD, :] = before.T[LANES - PAD :, :]
    head[PAD:, :] = blank
    tail[0:PAD, :] = blank
    tail[PAD:, :] = after.T[:PAD, :]
    first, last = blank, blank
    for d in range(1, HALF + 1):
        first = first + taps_ref[HALF + d : HALF + d + 1, :] * head[PAD - d : 2 * PAD - d, :]
        last = last + taps_ref[HALF - d : HALF - d + 1, :] * tail[d : PAD + d, :]
    rest = jnp.zeros((LANES - PAD, columns), F32)
    left = jnp.concatenate([first, rest], axis=0).T
    right = jnp.concatenate([rest, last], axis=0).T
    grad = sum_ref[...] + jnp.concatenate([left, right], axis=1)
    low = jnp.concatenate(
        [(grad * gate_ref[...]).astype(BF16), (grad * slope_ref[...]).astype(BF16)], axis=0
    )
    model = w_ref.shape[0]
    chunk = 256 if model % 256 == 0 else LANES
    for at in range(0, model, chunk):
        out_ref[at : at + chunk, :] = dot_nn(w_ref[at : at + chunk, :], low).astype(BF16)


def meta_of(ref, columns):
    return ref[3 * columns : 3 * columns + META, :].astype(F32)


def limits(query_meta, key_count, slot):
    lane = lax.broadcasted_iota(jnp.int32, query_meta[0:1].shape, 1).astype(F32)
    valid = lane < query_meta[0:1]
    return [
        jnp.where(valid & (query_meta[1 + 2 * slot + kb : 2 + 2 * slot + kb] > 0.5), key_count, 0.0)
        for kb in range(2)
    ]


def masked(scores, limit_rows):
    rows = scores.shape[0]
    half = rows // 2
    parts = []
    for kb in range(2):
        index = lax.broadcasted_iota(jnp.int32, (half, scores.shape[1]), 0).astype(F32) + kb * half
        parts.append(
            jnp.where(index < limit_rows[kb], scores[kb * half : (kb + 1) * half], NEG)
        )
    return jnp.concatenate(parts, axis=0)


def pieces(value, count):
    found = []
    for _ in range(count):
        low = value.astype(BF16).astype(F32)
        found.append(low)
        value = value - low
    return found


def part_of(refs, slots, own_ref, own_meta, low, columns, h, top, tile_out):
    lo, hi = h * HEAD_DIM, (h + 1) * HEAD_DIM
    query = own_ref[2 * columns + lo : 2 * columns + hi, :]
    scores = []
    for ref, slot in zip(refs, slots):
        limit = limits(own_meta, meta_of(ref, columns)[0:1], slot)
        scores.append(masked(dot_tn(ref[lo:hi, :], query) * SCALE2, limit))
    top = functools.reduce(jnp.maximum, [jnp.max(s, axis=0, keepdims=True) for s in scores], top)
    total = jnp.zeros_like(top)
    mixed = jnp.zeros_like(top)
    for i, ref in enumerate(refs):
        expo = jnp.exp2(scores[i] - top)
        dprob = dot_tn(ref[columns + lo : columns + hi, :], low[lo:hi])
        at = 2 * (len(refs) * h + i)
        tile_out[at] = expo
        tile_out[at + 1] = dprob
        total = total + jnp.sum(expo, axis=0, keepdims=True)
        mixed = mixed + jnp.sum(expo * dprob, axis=0, keepdims=True)
    return top, total, mixed


def valid_of(meta):
    return lax.broadcasted_iota(jnp.int32, meta[0:1].shape, 1).astype(F32) < meta[0:1]


def near_body(
    columns, w_ref, stream_ref, own_ref, one_ref, two_ref, low_out, tile_out, part_out
):
    own_meta = meta_of(own_ref, columns)
    low = jnp.where(valid_of(own_meta), dot_nn(w_ref[...], stream_ref[...]), 0.0).astype(BF16)
    low_out[...] = low
    start = jnp.full(own_meta[0:1].shape, NEG, F32)
    part_out[...] = jnp.zeros(part_out.shape, F32)
    for h in range(columns // HEAD_DIM):
        found = part_of(
            (own_ref, one_ref, two_ref), (0, 1, 2), own_ref, own_meta, low, columns, h, start, tile_out
        )
        for i, row in enumerate(found):
            part_out[3 * h + i : 3 * h + i + 1, :] = row


def grad_body(columns, own_ref, far_ref, low_ref, part_ref, out_ref, tile_out, factor_out):
    own_meta = meta_of(own_ref, columns)
    valid = valid_of(own_meta)
    low = low_ref[...]
    out_ref[0:columns, :] = low
    factor_out[...] = jnp.zeros(factor_out.shape, F32)
    rows = []
    for h in range(columns // HEAD_DIM):
        old = [part_ref[3 * h + i : 3 * h + i + 1, :] for i in range(3)]
        top, total, mixed = part_of(
            (far_ref,), (3,), own_ref, own_meta, low, columns, h, old[0], tile_out
        )
        scale = jnp.exp2(old[0] - top)
        total = total + scale * old[1]
        inverse = jnp.where(valid, 1.0 / total, 0.0)
        factor_out[2 * h : 2 * h + 1, :] = inverse * scale
        factor_out[2 * h + 1 : 2 * h + 2, :] = inverse
        rows += pieces(jnp.where(valid, top + jnp.log2(total), -NEG), 3)
        rows += pieces((mixed + scale * old[2]) * inverse, 2)
    index = lax.broadcasted_iota(jnp.int32, (META, own_meta.shape[1]), 0)
    meta = jnp.zeros((META, own_meta.shape[1]), F32)
    for i, row in enumerate(rows):
        meta = jnp.where(index == i, row, meta)
    out_ref[columns:, :] = meta.astype(BF16)


def stats_of(ref, columns, h):
    meta = ref[columns : columns + META, :].astype(F32)
    at = 5 * h
    lse = (meta[at : at + 1] + meta[at + 1 : at + 2]) + meta[at + 2 : at + 3]
    delta = meta[at + 3 : at + 4] + meta[at + 4 : at + 5]
    return lse, delta


def tile(key, value, query, grad, lse, delta, limit):
    probs = jnp.exp2(masked(dot_tn(key, query) * SCALE2 - lse, limit))
    dscore = (probs * (dot_tn(value, grad) - delta)).astype(BF16)
    return probs.astype(BF16), dscore


def local_body(
    columns,
    own_ref,
    one_ref,
    two_ref,
    far_ref,
    grad_ref,
    near_tile_ref,
    far_tile_ref,
    factor_ref,
    query_out,
    acc_out,
):
    refs = (own_ref, one_ref, two_ref, far_ref)
    for h in range(columns // HEAD_DIM):
        lo, hi = h * HEAD_DIM, (h + 1) * HEAD_DIM
        grad = grad_ref[lo:hi, :]
        _, delta = stats_of(grad_ref, columns, h)
        total = jnp.zeros((HEAD_DIM, own_ref.shape[1]), F32)
        for j in range(LINKS):
            tiles, at = (near_tile_ref, 2 * (3 * h + j)) if j < 3 else (far_tile_ref, 2 * h)
            row = 2 * h + (j == 3)
            probs = tiles[at] * factor_ref[row : row + 1, :]
            dscore = (probs * (tiles[at + 1] - delta)).astype(BF16)
            total = total + dot_nn(refs[j][lo:hi, :], dscore)
            if j == 0:
                query = own_ref[2 * columns + lo : 2 * columns + hi, :]
                acc_out[lo:hi, :] = dot_nt(query, dscore)
                acc_out[columns + lo : columns + hi, :] = dot_nt(grad, probs.astype(BF16))
        query_out[lo:hi, :] = (total * SCALE).astype(BF16)


def remote_terms(columns, slots, own_ref, span_refs, grad_refs, h):
    lo, hi = h * HEAD_DIM, (h + 1) * HEAD_DIM
    key = own_ref[lo:hi, :]
    value = own_ref[columns + lo : columns + hi, :]
    count = meta_of(own_ref, columns)[0:1]
    key_term = value_term = 0.0
    for slot, span_ref, grad_ref in zip(slots, span_refs, grad_refs):
        query = span_ref[2 * columns + lo : 2 * columns + hi, :]
        grad = grad_ref[lo:hi, :]
        lse, delta = stats_of(grad_ref, columns, h)
        limit = limits(meta_of(span_ref, columns), count, slot)
        probs, dscore = tile(key, value, query, grad, lse, delta, limit)
        key_term = key_term + dot_nt(query, dscore)
        value_term = value_term + dot_nt(grad, probs)
    return key_term, value_term


def middle_body(columns, own_ref, far_ref, grad_far_ref, acc_ref, acc_out):
    for h in range(columns // HEAD_DIM):
        lo, hi = h * HEAD_DIM, (h + 1) * HEAD_DIM
        key_term, value_term = remote_terms(
            columns, (3,), own_ref, (far_ref,), (grad_far_ref,), h
        )
        acc_out[lo:hi, :] = acc_ref[lo:hi, :] + key_term
        acc_out[columns + lo : columns + hi, :] = acc_ref[columns + lo : columns + hi, :] + value_term


def last_body(
    columns, own_ref, one_ref, two_ref, grad_one_ref, grad_two_ref, acc_ref, key_out, value_out
):
    for h in range(columns // HEAD_DIM):
        lo, hi = h * HEAD_DIM, (h + 1) * HEAD_DIM
        key_term, value_term = remote_terms(
            columns, (1, 2), own_ref, (one_ref, two_ref), (grad_one_ref, grad_two_ref), h
        )
        key_out[lo:hi, :] = ((acc_ref[lo:hi, :] + key_term) * SCALE).astype(BF16)
        value_out[lo:hi, :] = (acc_ref[columns + lo : columns + hi, :] + value_term).astype(BF16)


def exchange(value, slot, closed=True):
    count = lax.axis_size("ctx")
    if slot == 3:
        pairs = [(c, (c + count // 2) % count) for c in range(count)]
    else:
        pairs = [(c, (c + (1 if (c + slot) % 2 else -1)) % count) for c in range(count)]
    if not closed:
        pairs = [(i, j) for i, j in pairs if abs(i - j) == 1]
    return lax.ppermute(value, "ctx", pairs)


def per_device(
    g_conv, pre, kernel, w_point, g_out, w_out, queries, keys, values, block_mask, counts
):
    columns, row_count = g_conv.shape
    model = w_point.shape[2]
    groups = lax.axis_size("head")
    shape = jax.ShapeDtypeStruct
    queries, keys, values = (queries.T, keys.T, values.T)
    message = 3 * columns + META
    square = 2 * columns * row_count * row_count

    odd = (lax.axis_index("ctx") % 2).astype(jnp.int32).reshape(1, 1)
    near = [exchange(g_conv, slot, closed=False) for slot in (2, 1)]
    flat = (columns, row_count)
    own, conv, gate, slope = call(
        own_body,
        (shape((message, row_count), BF16),) + (shape(flat, F32),) * 3,
        (
            odd,
            block_mask.transpose(0, 2, 1),
            counts,
            keys,
            values,
            queries,
            g_conv,
            pre,
            kernel,
        ),
        [VMEM] * 9,
        2 * KW * columns * row_count,
        6 * message * row_count,
        columns * row_count,
        (
            pltpu.VMEM((row_count + 2 * PAD, columns), F32),
            pltpu.VMEM((8, row_count + 24, columns), F32),
            pltpu.VMEM((row_count, columns), F32),
        ),
    )
    w_turned = w_point.reshape(2 * columns, model).T
    point_grad = call(
        edge_body,
        shape((model, row_count), BF16),
        (odd, *near, kernel, conv, gate, slope, w_turned),
        [VMEM] * 8,
        4 * columns * model * row_count,
        4 * columns * model,
        0,
        (pltpu.VMEM((2 * PAD, columns), F32), pltpu.VMEM((2 * PAD, columns), F32)),
    )
    parts = lax.all_to_all(
        point_grad.reshape(groups, columns, row_count), "head", 0, 0, tiled=False
    )
    own, _ = lax.optimization_barrier((own, point_grad))
    two, one, far = [exchange(own, slot) for slot in (2, 1, 3)]
    piece = jnp.sum(parts.astype(F32), axis=0)
    stream_grad = (g_out.astype(F32) + piece).astype(BF16)
    stream_full = lax.all_gather(stream_grad, "head", axis=0, tiled=True)
    heads = columns // HEAD_DIM
    low, near_tiles, part = call(
        functools.partial(near_body, columns),
        (
            shape(flat, BF16),
            shape((6 * heads, row_count, row_count), F32),
            shape((3 * heads, row_count), F32),
        ),
        (w_out, stream_full, own, one, two),
        [VMEM] * 5,
        2 * columns * model * row_count + 6 * square,
        2 * model * (columns + row_count),
        3 * heads * row_count * row_count,
    )
    grad, far_tiles, factor = call(
        functools.partial(grad_body, columns),
        (
            shape((columns + META, row_count), BF16),
            shape((2 * heads, row_count, row_count), F32),
            shape((2 * heads, row_count), F32),
        ),
        (own, far, low, part),
        [VMEM] * 4,
        2 * square,
        4 * message * row_count,
        heads * row_count * row_count,
    )
    grad_one, grad_two, grad_far = [exchange(grad, slot) for slot in (1, 2, 3)]
    grad_queries, acc = call(
        functools.partial(local_body, columns),
        (shape(flat, BF16), shape((2 * columns, row_count), F32)),
        (own, one, two, far, grad, near_tiles, far_tiles, factor),
        [VMEM] * 8,
        3 * LINKS * square,
        8 * message * row_count,
    )
    acc = call(
        functools.partial(middle_body, columns),
        shape((2 * columns, row_count), F32),
        (own, far, grad_far, acc),
        [VMEM] * 4,
        4 * square,
        6 * message * row_count,
        heads * row_count * row_count,
    )
    grad_keys, grad_values = call(
        functools.partial(last_body, columns),
        (shape(flat, BF16), shape(flat, BF16)),
        (own, one, two, grad_one, grad_two, acc),
        [VMEM] * 6,
        8 * square,
        8 * message * row_count,
        2 * heads * row_count * row_count,
    )
    return (stream_grad.T, grad_queries.T, grad_keys.T, grad_values.T)


def solution(mesh):
    in_specs = (
        P("head", "ctx"),
        P(None, "head", "ctx"),
        P(None, "head"),
        P(None, "head", None),
        P("head", "ctx"),
        P("head", None),
        P("ctx", "head"),
        P("ctx", "head"),
        P("ctx", "head"),
        P("ctx", None, None),
        P("ctx"),
    )
    out_specs = (P("ctx", "head"), P("ctx", "head"), P("ctx", "head"), P("ctx", "head"))
    return jax.shard_map(
        per_device, mesh=mesh, in_specs=in_specs, out_specs=out_specs, check_vma=False
    )
```

```python
import functools
import math

import jax
import jax.numpy as jnp
from jax import lax
from jax.experimental import pallas as pl
from jax.experimental.pallas import tpu as pltpu
from jax.sharding import PartitionSpec as P

HEAD_DIM = 64
KW = 31
LINKS = 4
HALF = 15
LANES = 128
META = 16
PAD = 16
NEG = -1e30
SCALE = 1.0 / math.sqrt(HEAD_DIM)
SCALE2 = SCALE * math.log2(math.e)
VMEM = pl.BlockSpec(memory_space=pltpu.VMEM)
F32 = jnp.float32
BF16 = jnp.bfloat16


def call(body, out_shapes, args, specs, flops, moved, exps=0, scratch=()):
    return pl.pallas_call(
        body,
        out_shape=out_shapes,
        in_specs=specs,
        out_specs=jax.tree.map(lambda _: VMEM, out_shapes),
        scratch_shapes=list(scratch),
        compiler_params=pltpu.CompilerParams(vmem_limit_bytes=24 * 1024 * 1024),
        cost_estimate=pl.CostEstimate(flops=flops, bytes_accessed=moved, transcendentals=exps),
    )(*args)


def dot_tn(a, b):
    return lax.dot_general(a, b, (((0,), (0,)), ((), ())), preferred_element_type=F32)


def dot_nt(a, b):
    return lax.dot_general(a, b, (((1,), (1,)), ((), ())), preferred_element_type=F32)


def dot_nn(a, b):
    return lax.dot_general(a, b, (((1,), (0,)), ((), ())), preferred_element_type=F32)


def own_body(
    odd_ref,
    mask_ref,
    count_ref,
    keys_ref,
    values_ref,
    queries_ref,
    g_ref,
    pre_ref,
    taps_ref,
    out_ref,
    sum_out,
    gate_out,
    slope_out,
    x_ref,
    moved_ref,
    sum_ref,
):
    columns, rows = g_ref.shape
    x_ref[0:PAD, :] = jnp.zeros((PAD, columns), F32)
    x_ref[PAD + rows :, :] = jnp.zeros((PAD, columns), F32)
    x_ref[PAD : PAD + rows, :] = g_ref[...].astype(F32).T
    for shift in range(8):
        moved_ref[shift] = x_ref[shift : shift + rows + 24, :]
    out_ref[0:columns, :] = keys_ref[...]
    out_ref[columns : 2 * columns, :] = values_ref[...]
    out_ref[2 * columns : 3 * columns, :] = queries_ref[...]
    row = lax.broadcasted_iota(jnp.int32, (META, rows), 0)
    first = lax.broadcasted_iota(jnp.int32, (META, rows), 1) < rows // 2
    odd = odd_ref[...] > 0
    meta = jnp.where(row == 0, count_ref[...].astype(F32).reshape(1, 1), 0.0)
    for kb in range(2):
        bits = []
        for qb in range(2):
            given = [
                (mask_ref[qb, kb : kb + 1, j : j + 1] > 0).astype(F32) for j in range(LINKS)
            ]
            own_bit = jnp.ones_like(given[0]) if qb == kb else given[0]
            bits.append(
                (
                    own_bit,
                    jnp.where(odd, given[1], given[2]),
                    jnp.where(odd, given[2], given[1]),
                    given[3],
                )
            )
        for slot in range(LINKS):
            meta = jnp.where(
                row == 1 + 2 * slot + kb, jnp.where(first, bits[0][slot], bits[1][slot]), meta
            )
    out_ref[3 * columns :, :] = meta.astype(BF16)
    step = 32

    def block(i, carry):
        at = pl.multiple_of(i * step, step)
        acc = jnp.zeros((step, columns), F32)
        for k in range(KW):
            a, shift = divmod(PAD + HALF - k, 8)
            acc = acc + taps_ref[k : k + 1, :] * moved_ref[shift, pl.ds(at + 8 * a, step), :]
        sum_ref[pl.ds(at, step), :] = acc
        return carry

    lax.fori_loop(0, rows // step, block, 0)
    sum_out[...] = sum_ref[...].T
    gate = jax.nn.sigmoid(pre_ref[1].astype(F32))
    gate_out[...] = gate
    slope_out[...] = pre_ref[0].astype(F32) * gate * (1.0 - gate)


def edge_body(
    odd_ref, two_ref, one_ref, taps_ref, sum_ref, gate_ref, slope_ref, w_ref, out_ref, head, tail
):
    columns, rows = sum_ref.shape
    odd = jnp.broadcast_to(odd_ref[...] > 0, (columns, LANES))
    before = jnp.where(odd, one_ref[:, rows - LANES :], two_ref[:, rows - LANES :]).astype(F32)
    after = jnp.where(odd, two_ref[:, :LANES], one_ref[:, :LANES]).astype(F32)
    blank = jnp.zeros((PAD, columns), F32)
    head[0:PAD, :] = before.T[LANES - PAD :, :]
    head[PAD:, :] = blank
    tail[0:PAD, :] = blank
    tail[PAD:, :] = after.T[:PAD, :]
    first, last = blank, blank
    for d in range(1, HALF + 1):
        first = first + taps_ref[HALF + d : HALF + d + 1, :] * head[PAD - d : 2 * PAD - d, :]
        last = last + taps_ref[HALF - d : HALF - d + 1, :] * tail[d : PAD + d, :]
    rest = jnp.zeros((LANES - PAD, columns), F32)
    left = jnp.concatenate([first, rest], axis=0).T
    right = jnp.concatenate([rest, last], axis=0).T
    grad = sum_ref[...] + jnp.concatenate([left, right], axis=1)
    low = jnp.concatenate(
        [(grad * gate_ref[...]).astype(BF16), (grad * slope_ref[...]).astype(BF16)], axis=0
    )
    model = w_ref.shape[0]
    chunk = 256 if model % 256 == 0 else LANES
    for at in range(0, model, chunk):
        out_ref[at : at + chunk, :] = dot_nn(w_ref[at : at + chunk, :], low).astype(BF16)


def meta_of(ref, columns):
    return ref[3 * columns : 3 * columns + META, :].astype(F32)


def limits(query_meta, key_count, slot):
    lane = lax.broadcasted_iota(jnp.int32, query_meta[0:1].shape, 1).astype(F32)
    valid = lane < query_meta[0:1]
    return [
        jnp.where(valid & (query_meta[1 + 2 * slot + kb : 2 + 2 * slot + kb] > 0.5), key_count, 0.0)
        for kb in range(2)
    ]


def masked(scores, limit_rows):
    rows = scores.shape[0]
    half = rows // 2
    parts = []
    for kb in range(2):
        index = lax.broadcasted_iota(jnp.int32, (half, scores.shape[1]), 0).astype(F32) + kb * half
        parts.append(
            jnp.where(index < limit_rows[kb], scores[kb * half : (kb + 1) * half], NEG)
        )
    return jnp.concatenate(parts, axis=0)


def pieces(value, count):
    found = []
    for _ in range(count):
        low = value.astype(BF16).astype(F32)
        found.append(low)
        value = value - low
    return found


def part_of(refs, slots, own_ref, own_meta, low, columns, h, top, tile_out):
    lo, hi = h * HEAD_DIM, (h + 1) * HEAD_DIM
    query = own_ref[2 * columns + lo : 2 * columns + hi, :]
    scores = []
    for ref, slot in zip(refs, slots):
        limit = limits(own_meta, meta_of(ref, columns)[0:1], slot)
        scores.append(masked(dot_tn(ref[lo:hi, :], query) * SCALE2, limit))
    top = functools.reduce(jnp.maximum, [jnp.max(s, axis=0, keepdims=True) for s in scores], top)
    total = jnp.zeros_like(top)
    mixed = jnp.zeros_like(top)
    for i, ref in enumerate(refs):
        expo = jnp.exp2(scores[i] - top)
        dprob = dot_tn(ref[columns + lo : columns + hi, :], low[lo:hi])
        at = 2 * (len(refs) * h + i)
        tile_out[at] = expo
        tile_out[at + 1] = dprob
        total = total + jnp.sum(expo, axis=0, keepdims=True)
        mixed = mixed + jnp.sum(expo * dprob, axis=0, keepdims=True)
    return top, total, mixed


def valid_of(meta):
    return lax.broadcasted_iota(jnp.int32, meta[0:1].shape, 1).astype(F32) < meta[0:1]


def near_body(
    columns, w_ref, stream_ref, own_ref, one_ref, low_out, tile_out, part_out
):
    own_meta = meta_of(own_ref, columns)
    low = jnp.where(valid_of(own_meta), dot_nn(w_ref[...], stream_ref[...]), 0.0).astype(BF16)
    low_out[...] = low
    start = jnp.full(own_meta[0:1].shape, NEG, F32)
    part_out[...] = jnp.zeros(part_out.shape, F32)
    for h in range(columns // HEAD_DIM):
        found = part_of(
            (own_ref, one_ref), (0, 1), own_ref, own_meta, low, columns, h, start, tile_out
        )
        for i, row in enumerate(found):
            part_out[3 * h + i : 3 * h + i + 1, :] = row


def grad_body(
    columns, own_ref, two_ref, far_ref, low_ref, part_ref, out_ref, tile_out, factor_out
):
    own_meta = meta_of(own_ref, columns)
    valid = valid_of(own_meta)
    low = low_ref[...]
    out_ref[0:columns, :] = low
    factor_out[...] = jnp.zeros(factor_out.shape, F32)
    rows = []
    for h in range(columns // HEAD_DIM):
        old = [part_ref[3 * h + i : 3 * h + i + 1, :] for i in range(3)]
        top, total, mixed = part_of(
            (two_ref, far_ref), (2, 3), own_ref, own_meta, low, columns, h, old[0], tile_out
        )
        scale = jnp.exp2(old[0] - top)
        total = total + scale * old[1]
        inverse = jnp.where(valid, 1.0 / total, 0.0)
        factor_out[2 * h : 2 * h + 1, :] = inverse * scale
        factor_out[2 * h + 1 : 2 * h + 2, :] = inverse
        rows += pieces(jnp.where(valid, top + jnp.log2(total), -NEG), 3)
        rows += pieces((mixed + scale * old[2]) * inverse, 2)
    index = lax.broadcasted_iota(jnp.int32, (META, own_meta.shape[1]), 0)
    meta = jnp.zeros((META, own_meta.shape[1]), F32)
    for i, row in enumerate(rows):
        meta = jnp.where(index == i, row, meta)
    out_ref[columns:, :] = meta.astype(BF16)


def stats_of(ref, columns, h):
    meta = ref[columns : columns + META, :].astype(F32)
    at = 5 * h
    lse = (meta[at : at + 1] + meta[at + 1 : at + 2]) + meta[at + 2 : at + 3]
    delta = meta[at + 3 : at + 4] + meta[at + 4 : at + 5]
    return lse, delta


def tile(key, value, query, grad, lse, delta, limit):
    probs = jnp.exp2(masked(dot_tn(key, query) * SCALE2 - lse, limit))
    dscore = (probs * (dot_tn(value, grad) - delta)).astype(BF16)
    return probs.astype(BF16), dscore


def local_body(
    columns,
    own_ref,
    one_ref,
    two_ref,
    far_ref,
    grad_ref,
    first_tile_ref,
    other_tile_ref,
    factor_ref,
    query_out,
    acc_out,
):
    refs = (own_ref, one_ref, two_ref, far_ref)
    for h in range(columns // HEAD_DIM):
        lo, hi = h * HEAD_DIM, (h + 1) * HEAD_DIM
        grad = grad_ref[lo:hi, :]
        _, delta = stats_of(grad_ref, columns, h)
        total = jnp.zeros((HEAD_DIM, own_ref.shape[1]), F32)
        for j in range(LINKS):
            tiles = first_tile_ref if j < 2 else other_tile_ref
            at = 2 * (2 * h + j % 2)
            row = 2 * h + j // 2
            probs = tiles[at] * factor_ref[row : row + 1, :]
            dscore = (probs * (tiles[at + 1] - delta)).astype(BF16)
            total = total + dot_nn(refs[j][lo:hi, :], dscore)
            if j == 0:
                query = own_ref[2 * columns + lo : 2 * columns + hi, :]
                acc_out[lo:hi, :] = dot_nt(query, dscore)
                acc_out[columns + lo : columns + hi, :] = dot_nt(grad, probs.astype(BF16))
        query_out[lo:hi, :] = (total * SCALE).astype(BF16)


def remote_terms(columns, slots, own_ref, span_refs, grad_refs, h):
    lo, hi = h * HEAD_DIM, (h + 1) * HEAD_DIM
    key = own_ref[lo:hi, :]
    value = own_ref[columns + lo : columns + hi, :]
    count = meta_of(own_ref, columns)[0:1]
    key_term = value_term = 0.0
    for slot, span_ref, grad_ref in zip(slots, span_refs, grad_refs):
        query = span_ref[2 * columns + lo : 2 * columns + hi, :]
        grad = grad_ref[lo:hi, :]
        lse, delta = stats_of(grad_ref, columns, h)
        limit = limits(meta_of(span_ref, columns), count, slot)
        probs, dscore = tile(key, value, query, grad, lse, delta, limit)
        key_term = key_term + dot_nt(query, dscore)
        value_term = value_term + dot_nt(grad, probs)
    return key_term, value_term


def middle_body(columns, own_ref, two_ref, grad_two_ref, acc_ref, acc_out):
    for h in range(columns // HEAD_DIM):
        lo, hi = h * HEAD_DIM, (h + 1) * HEAD_DIM
        key_term, value_term = remote_terms(
            columns, (2,), own_ref, (two_ref,), (grad_two_ref,), h
        )
        acc_out[lo:hi, :] = acc_ref[lo:hi, :] + key_term
        acc_out[columns + lo : columns + hi, :] = acc_ref[columns + lo : columns + hi, :] + value_term


def last_body(
    columns, own_ref, one_ref, far_ref, grad_one_ref, grad_far_ref, acc_ref, key_out, value_out
):
    for h in range(columns // HEAD_DIM):
        lo, hi = h * HEAD_DIM, (h + 1) * HEAD_DIM
        key_term, value_term = remote_terms(
            columns, (1, 3), own_ref, (one_ref, far_ref), (grad_one_ref, grad_far_ref), h
        )
        key_out[lo:hi, :] = ((acc_ref[lo:hi, :] + key_term) * SCALE).astype(BF16)
        value_out[lo:hi, :] = (acc_ref[columns + lo : columns + hi, :] + value_term).astype(BF16)


def exchange(value, slot, closed=True):
    count = lax.axis_size("ctx")
    if slot == 3:
        pairs = [(c, (c + count // 2) % count) for c in range(count)]
    else:
        pairs = [(c, (c + (1 if (c + slot) % 2 else -1)) % count) for c in range(count)]
    if not closed:
        pairs = [(i, j) for i, j in pairs if abs(i - j) == 1]
    return lax.ppermute(value, "ctx", pairs)


def per_device(
    g_conv, pre, kernel, w_point, g_out, w_out, queries, keys, values, block_mask, counts
):
    columns, row_count = g_conv.shape
    model = w_point.shape[2]
    groups = lax.axis_size("head")
    shape = jax.ShapeDtypeStruct
    queries, keys, values = (queries.T, keys.T, values.T)
    message = 3 * columns + META
    square = 2 * columns * row_count * row_count

    odd = (lax.axis_index("ctx") % 2).astype(jnp.int32).reshape(1, 1)
    near = [exchange(g_conv, slot, closed=False) for slot in (2, 1)]
    flat = (columns, row_count)
    own, conv, gate, slope = call(
        own_body,
        (shape((message, row_count), BF16),) + (shape(flat, F32),) * 3,
        (
            odd,
            block_mask.transpose(0, 2, 1),
            counts,
            keys,
            values,
            queries,
            g_conv,
            pre,
            kernel,
        ),
        [VMEM] * 9,
        2 * KW * columns * row_count,
        6 * message * row_count,
        columns * row_count,
        (
            pltpu.VMEM((row_count + 2 * PAD, columns), F32),
            pltpu.VMEM((8, row_count + 24, columns), F32),
            pltpu.VMEM((row_count, columns), F32),
        ),
    )
    w_turned = w_point.reshape(2 * columns, model).T
    point_grad = call(
        edge_body,
        shape((model, row_count), BF16),
        (odd, *near, kernel, conv, gate, slope, w_turned),
        [VMEM] * 8,
        4 * columns * model * row_count,
        4 * columns * model,
        0,
        (pltpu.VMEM((2 * PAD, columns), F32), pltpu.VMEM((2 * PAD, columns), F32)),
    )
    parts = lax.all_to_all(
        point_grad.reshape(groups, columns, row_count), "head", 0, 0, tiled=False
    )
    own, _ = lax.optimization_barrier((own, point_grad))
    two, one, far = [exchange(own, slot) for slot in (2, 1, 3)]
    piece = jnp.sum(parts.astype(F32), axis=0)
    stream_grad = (g_out.astype(F32) + piece).astype(BF16)
    stream_full = lax.all_gather(stream_grad, "head", axis=0, tiled=True)
    heads = columns // HEAD_DIM
    low, first_tiles, part = call(
        functools.partial(near_body, columns),
        (
            shape(flat, BF16),
            shape((4 * heads, row_count, row_count), F32),
            shape((3 * heads, row_count), F32),
        ),
        (w_out, stream_full, own, one),
        [VMEM] * 4,
        2 * columns * model * row_count + 4 * square,
        2 * model * (columns + row_count),
        2 * heads * row_count * row_count,
    )
    grad, other_tiles, factor = call(
        functools.partial(grad_body, columns),
        (
            shape((columns + META, row_count), BF16),
            shape((4 * heads, row_count, row_count), F32),
            shape((2 * heads, row_count), F32),
        ),
        (own, two, far, low, part),
        [VMEM] * 5,
        4 * square,
        6 * message * row_count,
        2 * heads * row_count * row_count,
    )
    grad_one, grad_two, grad_far = [exchange(grad, slot) for slot in (1, 2, 3)]
    grad_queries, acc = call(
        functools.partial(local_body, columns),
        (shape(flat, BF16), shape((2 * columns, row_count), F32)),
        (own, one, two, far, grad, first_tiles, other_tiles, factor),
        [VMEM] * 8,
        3 * LINKS * square,
        8 * message * row_count,
    )
    acc = call(
        functools.partial(middle_body, columns),
        shape((2 * columns, row_count), F32),
        (own, two, grad_two, acc),
        [VMEM] * 4,
        4 * square,
        6 * message * row_count,
        heads * row_count * row_count,
    )
    grad_keys, grad_values = call(
        functools.partial(last_body, columns),
        (shape(flat, BF16), shape(flat, BF16)),
        (own, one, far, grad_one, grad_far, acc),
        [VMEM] * 6,
        8 * square,
        8 * message * row_count,
        2 * heads * row_count * row_count,
    )
    return (stream_grad.T, grad_queries.T, grad_keys.T, grad_values.T)


def solution(mesh):
    in_specs = (
        P("head", "ctx"),
        P(None, "head", "ctx"),
        P(None, "head"),
        P(None, "head", None),
        P("head", "ctx"),
        P("head", None),
        P("ctx", "head"),
        P("ctx", "head"),
        P("ctx", "head"),
        P("ctx", None, None),
        P("ctx"),
    )
    out_specs = (P("ctx", "head"), P("ctx", "head"), P("ctx", "head"), P("ctx", "head"))
    return jax.shard_map(
        per_device, mesh=mesh, in_specs=in_specs, out_specs=out_specs, check_vma=False
    )
```

```python
import functools
import math

import jax
import jax.numpy as jnp
from jax import lax
from jax.experimental import pallas as pl
from jax.experimental.pallas import tpu as pltpu
from jax.sharding import PartitionSpec as P

HEAD_DIM = 64
KW = 31
LINKS = 4
HALF = 15
LANES = 128
META = 16
PAD = 16
NEG = -1e30
SCALE = 1.0 / math.sqrt(HEAD_DIM)
SCALE2 = SCALE * math.log2(math.e)
VMEM = pl.BlockSpec(memory_space=pltpu.VMEM)
F32 = jnp.float32
BF16 = jnp.bfloat16


def call(body, out_shapes, args, specs, flops, moved, exps=0, scratch=()):
    return pl.pallas_call(
        body,
        out_shape=out_shapes,
        in_specs=specs,
        out_specs=jax.tree.map(lambda _: VMEM, out_shapes),
        scratch_shapes=list(scratch),
        compiler_params=pltpu.CompilerParams(vmem_limit_bytes=24 * 1024 * 1024),
        cost_estimate=pl.CostEstimate(flops=flops, bytes_accessed=moved, transcendentals=exps),
    )(*args)


def dot_tn(a, b):
    return lax.dot_general(a, b, (((0,), (0,)), ((), ())), preferred_element_type=F32)


def dot_nt(a, b):
    return lax.dot_general(a, b, (((1,), (1,)), ((), ())), preferred_element_type=F32)


def dot_nn(a, b):
    return lax.dot_general(a, b, (((1,), (0,)), ((), ())), preferred_element_type=F32)


def own_body(
    odd_ref,
    mask_ref,
    count_ref,
    keys_ref,
    values_ref,
    queries_ref,
    g_ref,
    pre_ref,
    taps_ref,
    out_ref,
    sum_out,
    gate_out,
    slope_out,
    x_ref,
    moved_ref,
    sum_ref,
):
    columns, rows = g_ref.shape
    x_ref[0:PAD, :] = jnp.zeros((PAD, columns), F32)
    x_ref[PAD + rows :, :] = jnp.zeros((PAD, columns), F32)
    x_ref[PAD : PAD + rows, :] = g_ref[...].astype(F32).T
    for shift in range(8):
        moved_ref[shift] = x_ref[shift : shift + rows + 24, :]
    out_ref[0:columns, :] = keys_ref[...]
    out_ref[columns : 2 * columns, :] = values_ref[...]
    out_ref[2 * columns : 3 * columns, :] = queries_ref[...]
    row = lax.broadcasted_iota(jnp.int32, (META, rows), 0)
    first = lax.broadcasted_iota(jnp.int32, (META, rows), 1) < rows // 2
    odd = odd_ref[...] > 0
    meta = jnp.where(row == 0, count_ref[...].astype(F32).reshape(1, 1), 0.0)
    for kb in range(2):
        bits = []
        for qb in range(2):
            given = [
                (mask_ref[qb, kb : kb + 1, j : j + 1] > 0).astype(F32) for j in range(LINKS)
            ]
            own_bit = jnp.ones_like(given[0]) if qb == kb else given[0]
            bits.append(
                (
                    own_bit,
                    jnp.where(odd, given[1], given[2]),
                    jnp.where(odd, given[2], given[1]),
                    given[3],
                )
            )
        for slot in range(LINKS):
            meta = jnp.where(
                row == 1 + 2 * slot + kb, jnp.where(first, bits[0][slot], bits[1][slot]), meta
            )
    out_ref[3 * columns :, :] = meta.astype(BF16)
    step = 32

    def block(i, carry):
        at = pl.multiple_of(i * step, step)
        acc = jnp.zeros((step, columns), F32)
        for k in range(KW):
            a, shift = divmod(PAD + HALF - k, 8)
            acc = acc + taps_ref[k : k + 1, :] * moved_ref[shift, pl.ds(at + 8 * a, step), :]
        sum_ref[pl.ds(at, step), :] = acc
        return carry

    lax.fori_loop(0, rows // step, block, 0)
    sum_out[...] = sum_ref[...].T
    gate = jax.nn.sigmoid(pre_ref[1].astype(F32))
    gate_out[...] = gate
    slope_out[...] = pre_ref[0].astype(F32) * gate * (1.0 - gate)


def edge_body(
    odd_ref, two_ref, one_ref, taps_ref, sum_ref, gate_ref, slope_ref, w_ref, out_ref, head, tail
):
    columns, rows = sum_ref.shape
    odd = jnp.broadcast_to(odd_ref[...] > 0, (columns, LANES))
    before = jnp.where(odd, one_ref[:, rows - LANES :], two_ref[:, rows - LANES :]).astype(F32)
    after = jnp.where(odd, two_ref[:, :LANES], one_ref[:, :LANES]).astype(F32)
    blank = jnp.zeros((PAD, columns), F32)
    head[0:PAD, :] = before.T[LANES - PAD :, :]
    head[PAD:, :] = blank
    tail[0:PAD, :] = blank
    tail[PAD:, :] = after.T[:PAD, :]
    first, last = blank, blank
    for d in range(1, HALF + 1):
        first = first + taps_ref[HALF + d : HALF + d + 1, :] * head[PAD - d : 2 * PAD - d, :]
        last = last + taps_ref[HALF - d : HALF - d + 1, :] * tail[d : PAD + d, :]
    rest = jnp.zeros((LANES - PAD, columns), F32)
    left = jnp.concatenate([first, rest], axis=0).T
    right = jnp.concatenate([rest, last], axis=0).T
    grad = sum_ref[...] + jnp.concatenate([left, right], axis=1)
    low = jnp.concatenate(
        [(grad * gate_ref[...]).astype(BF16), (grad * slope_ref[...]).astype(BF16)], axis=0
    )
    model = w_ref.shape[0]
    chunk = 256 if model % 256 == 0 else LANES
    for at in range(0, model, chunk):
        out_ref[at : at + chunk, :] = dot_nn(w_ref[at : at + chunk, :], low).astype(BF16)


def meta_of(ref, columns):
    return ref[3 * columns : 3 * columns + META, :].astype(F32)


def limits(query_meta, key_count, slot):
    lane = lax.broadcasted_iota(jnp.int32, query_meta[0:1].shape, 1).astype(F32)
    valid = lane < query_meta[0:1]
    return [
        jnp.where(valid & (query_meta[1 + 2 * slot + kb : 2 + 2 * slot + kb] > 0.5), key_count, 0.0)
        for kb in range(2)
    ]


def masked(scores, limit_rows):
    rows = scores.shape[0]
    half = rows // 2
    parts = []
    for kb in range(2):
        index = lax.broadcasted_iota(jnp.int32, (half, scores.shape[1]), 0).astype(F32) + kb * half
        parts.append(
            jnp.where(index < limit_rows[kb], scores[kb * half : (kb + 1) * half], NEG)
        )
    return jnp.concatenate(parts, axis=0)


def pieces(value, count):
    found = []
    for _ in range(count):
        low = value.astype(BF16).astype(F32)
        found.append(low)
        value = value - low
    return found


def part_of(refs, slots, own_ref, own_meta, low, columns, h, top, tile_out):
    lo, hi = h * HEAD_DIM, (h + 1) * HEAD_DIM
    query = own_ref[2 * columns + lo : 2 * columns + hi, :]
    scores = []
    for ref, slot in zip(refs, slots):
        limit = limits(own_meta, meta_of(ref, columns)[0:1], slot)
        scores.append(masked(dot_tn(ref[lo:hi, :], query) * SCALE2, limit))
    top = functools.reduce(jnp.maximum, [jnp.max(s, axis=0, keepdims=True) for s in scores], top)
    total = jnp.zeros_like(top)
    mixed = jnp.zeros_like(top)
    for i, ref in enumerate(refs):
        expo = jnp.exp2(scores[i] - top)
        dprob = dot_tn(ref[columns + lo : columns + hi, :], low[lo:hi])
        at = 2 * (len(refs) * h + i)
        tile_out[at] = expo
        tile_out[at + 1] = dprob
        total = total + jnp.sum(expo, axis=0, keepdims=True)
        mixed = mixed + jnp.sum(expo * dprob, axis=0, keepdims=True)
    return top, total, mixed


def valid_of(meta):
    return lax.broadcasted_iota(jnp.int32, meta[0:1].shape, 1).astype(F32) < meta[0:1]


def near_body(
    columns, w_ref, stream_ref, own_ref, one_ref, low_out, tile_out, part_out
):
    own_meta = meta_of(own_ref, columns)
    low = jnp.where(valid_of(own_meta), dot_nn(w_ref[...], stream_ref[...]), 0.0).astype(BF16)
    low_out[...] = low
    start = jnp.full(own_meta[0:1].shape, NEG, F32)
    part_out[...] = jnp.zeros(part_out.shape, F32)
    for h in range(columns // HEAD_DIM):
        found = part_of(
            (own_ref, one_ref), (0, 1), own_ref, own_meta, low, columns, h, start, tile_out
        )
        for i, row in enumerate(found):
            part_out[3 * h + i : 3 * h + i + 1, :] = row


def grad_body(
    columns, own_ref, two_ref, far_ref, low_ref, part_ref, out_ref, tile_out, factor_out
):
    own_meta = meta_of(own_ref, columns)
    valid = valid_of(own_meta)
    low = low_ref[...]
    out_ref[0:columns, :] = low
    factor_out[...] = jnp.zeros(factor_out.shape, F32)
    rows = []
    for h in range(columns // HEAD_DIM):
        old = [part_ref[3 * h + i : 3 * h + i + 1, :] for i in range(3)]
        top, total, mixed = part_of(
            (two_ref, far_ref), (2, 3), own_ref, own_meta, low, columns, h, old[0], tile_out
        )
        scale = jnp.exp2(old[0] - top)
        total = total + scale * old[1]
        inverse = jnp.where(valid, 1.0 / total, 0.0)
        factor_out[2 * h : 2 * h + 1, :] = inverse * scale
        factor_out[2 * h + 1 : 2 * h + 2, :] = inverse
        rows += pieces(jnp.where(valid, top + jnp.log2(total), -NEG), 3)
        rows += pieces((mixed + scale * old[2]) * inverse, 2)
    index = lax.broadcasted_iota(jnp.int32, (META, own_meta.shape[1]), 0)
    meta = jnp.zeros((META, own_meta.shape[1]), F32)
    for i, row in enumerate(rows):
        meta = jnp.where(index == i, row, meta)
    out_ref[columns:, :] = meta.astype(BF16)


def stats_of(ref, columns, h):
    meta = ref[columns : columns + META, :].astype(F32)
    at = 5 * h
    lse = (meta[at : at + 1] + meta[at + 1 : at + 2]) + meta[at + 2 : at + 3]
    delta = meta[at + 3 : at + 4] + meta[at + 4 : at + 5]
    return lse, delta


def tile(key, value, query, grad, lse, delta, limit):
    probs = jnp.exp2(masked(dot_tn(key, query) * SCALE2 - lse, limit))
    dscore = (probs * (dot_tn(value, grad) - delta)).astype(BF16)
    return probs.astype(BF16), dscore


def local_body(
    columns,
    own_ref,
    one_ref,
    two_ref,
    far_ref,
    grad_ref,
    first_tile_ref,
    other_tile_ref,
    factor_ref,
    query_out,
    acc_out,
):
    refs = (own_ref, one_ref, two_ref, far_ref)
    for h in range(columns // HEAD_DIM):
        lo, hi = h * HEAD_DIM, (h + 1) * HEAD_DIM
        grad = grad_ref[lo:hi, :]
        _, delta = stats_of(grad_ref, columns, h)
        total = jnp.zeros((HEAD_DIM, own_ref.shape[1]), F32)
        for j in range(LINKS):
            tiles = first_tile_ref if j < 2 else other_tile_ref
            at = 2 * (2 * h + j % 2)
            row = 2 * h + j // 2
            probs = tiles[at] * factor_ref[row : row + 1, :]
            dscore = (probs * (tiles[at + 1] - delta)).astype(BF16)
            total = total + dot_nn(refs[j][lo:hi, :], dscore)
            if j == 0:
                query = own_ref[2 * columns + lo : 2 * columns + hi, :]
                acc_out[lo:hi, :] = dot_nt(query, dscore)
                acc_out[columns + lo : columns + hi, :] = dot_nt(grad, probs.astype(BF16))
        query_out[lo:hi, :] = (total * SCALE).astype(BF16)


def remote_terms(columns, slots, own_ref, span_refs, grad_refs, h):
    lo, hi = h * HEAD_DIM, (h + 1) * HEAD_DIM
    key = own_ref[lo:hi, :]
    value = own_ref[columns + lo : columns + hi, :]
    count = meta_of(own_ref, columns)[0:1]
    key_term = value_term = 0.0
    for slot, span_ref, grad_ref in zip(slots, span_refs, grad_refs):
        query = span_ref[2 * columns + lo : 2 * columns + hi, :]
        grad = grad_ref[lo:hi, :]
        lse, delta = stats_of(grad_ref, columns, h)
        limit = limits(meta_of(span_ref, columns), count, slot)
        probs, dscore = tile(key, value, query, grad, lse, delta, limit)
        key_term = key_term + dot_nt(query, dscore)
        value_term = value_term + dot_nt(grad, probs)
    return key_term, value_term


def middle_body(columns, own_ref, far_ref, grad_far_ref, acc_ref, acc_out):
    for h in range(columns // HEAD_DIM):
        lo, hi = h * HEAD_DIM, (h + 1) * HEAD_DIM
        key_term, value_term = remote_terms(
            columns, (3,), own_ref, (far_ref,), (grad_far_ref,), h
        )
        acc_out[lo:hi, :] = acc_ref[lo:hi, :] + key_term
        acc_out[columns + lo : columns + hi, :] = acc_ref[columns + lo : columns + hi, :] + value_term


def last_body(
    columns, own_ref, one_ref, two_ref, grad_one_ref, grad_two_ref, acc_ref, key_out, value_out
):
    for h in range(columns // HEAD_DIM):
        lo, hi = h * HEAD_DIM, (h + 1) * HEAD_DIM
        key_term, value_term = remote_terms(
            columns, (1, 2), own_ref, (one_ref, two_ref), (grad_one_ref, grad_two_ref), h
        )
        key_out[lo:hi, :] = ((acc_ref[lo:hi, :] + key_term) * SCALE).astype(BF16)
        value_out[lo:hi, :] = (acc_ref[columns + lo : columns + hi, :] + value_term).astype(BF16)


def exchange(value, slot, closed=True):
    count = lax.axis_size("ctx")
    if slot == 3:
        pairs = [(c, (c + count // 2) % count) for c in range(count)]
    else:
        pairs = [(c, (c + (1 if (c + slot) % 2 else -1)) % count) for c in range(count)]
    if not closed:
        pairs = [(i, j) for i, j in pairs if abs(i - j) == 1]
    return lax.ppermute(value, "ctx", pairs)


def per_device(
    g_conv, pre, kernel, w_point, g_out, w_out, queries, keys, values, block_mask, counts
):
    columns, row_count = g_conv.shape
    model = w_point.shape[2]
    groups = lax.axis_size("head")
    shape = jax.ShapeDtypeStruct
    queries, keys, values = (queries.T, keys.T, values.T)
    message = 3 * columns + META
    square = 2 * columns * row_count * row_count

    odd = (lax.axis_index("ctx") % 2).astype(jnp.int32).reshape(1, 1)
    near = [exchange(g_conv, slot, closed=False) for slot in (2, 1)]
    flat = (columns, row_count)
    own, conv, gate, slope = call(
        own_body,
        (shape((message, row_count), BF16),) + (shape(flat, F32),) * 3,
        (
            odd,
            block_mask.transpose(0, 2, 1),
            counts,
            keys,
            values,
            queries,
            g_conv,
            pre,
            kernel,
        ),
        [VMEM] * 9,
        2 * KW * columns * row_count,
        6 * message * row_count,
        columns * row_count,
        (
            pltpu.VMEM((row_count + 2 * PAD, columns), F32),
            pltpu.VMEM((8, row_count + 24, columns), F32),
            pltpu.VMEM((row_count, columns), F32),
        ),
    )
    w_turned = w_point.reshape(2 * columns, model).T
    point_grad = call(
        edge_body,
        shape((model, row_count), BF16),
        (odd, *near, kernel, conv, gate, slope, w_turned),
        [VMEM] * 8,
        4 * columns * model * row_count,
        4 * columns * model,
        0,
        (pltpu.VMEM((2 * PAD, columns), F32), pltpu.VMEM((2 * PAD, columns), F32)),
    )
    parts = lax.all_to_all(
        point_grad.reshape(groups, columns, row_count), "head", 0, 0, tiled=False
    )
    own, _ = lax.optimization_barrier((own, point_grad))
    two, one, far = [exchange(own, slot) for slot in (2, 1, 3)]
    piece = jnp.sum(parts.astype(F32), axis=0)
    stream_grad = (g_out.astype(F32) + piece).astype(BF16)
    stream_full = lax.all_gather(stream_grad, "head", axis=0, tiled=True)
    heads = columns // HEAD_DIM
    low, first_tiles, part = call(
        functools.partial(near_body, columns),
        (
            shape(flat, BF16),
            shape((4 * heads, row_count, row_count), F32),
            shape((3 * heads, row_count), F32),
        ),
        (w_out, stream_full, own, one),
        [VMEM] * 4,
        2 * columns * model * row_count + 4 * square,
        2 * model * (columns + row_count),
        2 * heads * row_count * row_count,
    )
    grad, other_tiles, factor = call(
        functools.partial(grad_body, columns),
        (
            shape((columns + META, row_count), BF16),
            shape((4 * heads, row_count, row_count), F32),
            shape((2 * heads, row_count), F32),
        ),
        (own, two, far, low, part),
        [VMEM] * 5,
        4 * square,
        6 * message * row_count,
        2 * heads * row_count * row_count,
    )
    grad_one, grad_two, grad_far = [exchange(grad, slot) for slot in (1, 2, 3)]
    grad_queries, acc = call(
        functools.partial(local_body, columns),
        (shape(flat, BF16), shape((2 * columns, row_count), F32)),
        (own, one, two, far, grad, first_tiles, other_tiles, factor),
        [VMEM] * 8,
        3 * LINKS * square,
        8 * message * row_count,
    )
    acc = call(
        functools.partial(middle_body, columns),
        shape((2 * columns, row_count), F32),
        (own, far, grad_far, acc),
        [VMEM] * 4,
        4 * square,
        6 * message * row_count,
        heads * row_count * row_count,
    )
    grad_keys, grad_values = call(
        functools.partial(last_body, columns),
        (shape(flat, BF16), shape(flat, BF16)),
        (own, one, two, grad_one, grad_two, acc),
        [VMEM] * 6,
        8 * square,
        8 * message * row_count,
        2 * heads * row_count * row_count,
    )
    return (stream_grad.T, grad_queries.T, grad_keys.T, grad_values.T)


def solution(mesh):
    in_specs = (
        P("head", "ctx"),
        P(None, "head", "ctx"),
        P(None, "head"),
        P(None, "head", None),
        P("head", "ctx"),
        P("head", None),
        P("ctx", "head"),
        P("ctx", "head"),
        P("ctx", "head"),
        P("ctx", None, None),
        P("ctx"),
    )
    out_specs = (P("ctx", "head"), P("ctx", "head"), P("ctx", "head"), P("ctx", "head"))
    return jax.shard_map(
        per_device, mesh=mesh, in_specs=in_specs, out_specs=out_specs, check_vma=False
    )
```

```python
import functools
import math

import jax
import jax.numpy as jnp
from jax import lax
from jax.experimental import pallas as pl
from jax.experimental.pallas import tpu as pltpu
from jax.sharding import PartitionSpec as P

HEAD_DIM = 64
KW = 31
LINKS = 4
HALF = 15
LANES = 128
META = 16
PAD = 16
NEG = -1e30
SCALE = 1.0 / math.sqrt(HEAD_DIM)
SCALE2 = SCALE * math.log2(math.e)
VMEM = pl.BlockSpec(memory_space=pltpu.VMEM)
F32 = jnp.float32
BF16 = jnp.bfloat16


def call(body, out_shapes, args, specs, flops, moved, exps=0, scratch=()):
    return pl.pallas_call(
        body,
        out_shape=out_shapes,
        in_specs=specs,
        out_specs=jax.tree.map(lambda _: VMEM, out_shapes),
        scratch_shapes=list(scratch),
        compiler_params=pltpu.CompilerParams(vmem_limit_bytes=24 * 1024 * 1024),
        cost_estimate=pl.CostEstimate(flops=flops, bytes_accessed=moved, transcendentals=exps),
    )(*args)


def dot_tn(a, b):
    return lax.dot_general(a, b, (((0,), (0,)), ((), ())), preferred_element_type=F32)


def dot_nt(a, b):
    return lax.dot_general(a, b, (((1,), (1,)), ((), ())), preferred_element_type=F32)


def dot_nn(a, b):
    return lax.dot_general(a, b, (((1,), (0,)), ((), ())), preferred_element_type=F32)


def own_body(
    odd_ref,
    mask_ref,
    count_ref,
    keys_ref,
    values_ref,
    queries_ref,
    g_ref,
    pre_ref,
    taps_ref,
    out_ref,
    sum_out,
    gate_out,
    slope_out,
    x_ref,
    moved_ref,
    sum_ref,
):
    columns, rows = g_ref.shape
    x_ref[0:PAD, :] = jnp.zeros((PAD, columns), F32)
    x_ref[PAD + rows :, :] = jnp.zeros((PAD, columns), F32)
    x_ref[PAD : PAD + rows, :] = g_ref[...].astype(F32).T
    for shift in range(8):
        moved_ref[shift] = x_ref[shift : shift + rows + 24, :]
    out_ref[0:columns, :] = keys_ref[...]
    out_ref[columns : 2 * columns, :] = values_ref[...]
    out_ref[2 * columns : 3 * columns, :] = queries_ref[...]
    row = lax.broadcasted_iota(jnp.int32, (META, rows), 0)
    first = lax.broadcasted_iota(jnp.int32, (META, rows), 1) < rows // 2
    odd = odd_ref[...] > 0
    meta = jnp.where(row == 0, count_ref[...].astype(F32).reshape(1, 1), 0.0)
    for kb in range(2):
        bits = []
        for qb in range(2):
            given = [
                (mask_ref[qb, kb : kb + 1, j : j + 1] > 0).astype(F32) for j in range(LINKS)
            ]
            own_bit = jnp.ones_like(given[0]) if qb == kb else given[0]
            bits.append(
                (
                    own_bit,
                    jnp.where(odd, given[1], given[2]),
                    jnp.where(odd, given[2], given[1]),
                    given[3],
                )
            )
        for slot in range(LINKS):
            meta = jnp.where(
                row == 1 + 2 * slot + kb, jnp.where(first, bits[0][slot], bits[1][slot]), meta
            )
    out_ref[3 * columns :, :] = meta.astype(BF16)
    step = 32

    def block(i, carry):
        at = pl.multiple_of(i * step, step)
        acc = jnp.zeros((step, columns), F32)
        for k in range(KW):
            a, shift = divmod(PAD + HALF - k, 8)
            acc = acc + taps_ref[k : k + 1, :] * moved_ref[shift, pl.ds(at + 8 * a, step), :]
        sum_ref[pl.ds(at, step), :] = acc
        return carry

    lax.fori_loop(0, rows // step, block, 0)
    sum_out[...] = sum_ref[...].T
    gate = jax.nn.sigmoid(pre_ref[1].astype(F32))
    gate_out[...] = gate
    slope_out[...] = pre_ref[0].astype(F32) * gate * (1.0 - gate)


def edge_body(
    odd_ref, two_ref, one_ref, taps_ref, sum_ref, gate_ref, slope_ref, w_ref, out_ref, head, tail
):
    columns, rows = sum_ref.shape
    odd = jnp.broadcast_to(odd_ref[...] > 0, (columns, LANES))
    before = jnp.where(odd, one_ref[:, rows - LANES :], two_ref[:, rows - LANES :]).astype(F32)
    after = jnp.where(odd, two_ref[:, :LANES], one_ref[:, :LANES]).astype(F32)
    blank = jnp.zeros((PAD, columns), F32)
    head[0:PAD, :] = before.T[LANES - PAD :, :]
    head[PAD:, :] = blank
    tail[0:PAD, :] = blank
    tail[PAD:, :] = after.T[:PAD, :]
    first, last = blank, blank
    for d in range(1, HALF + 1):
        first = first + taps_ref[HALF + d : HALF + d + 1, :] * head[PAD - d : 2 * PAD - d, :]
        last = last + taps_ref[HALF - d : HALF - d + 1, :] * tail[d : PAD + d, :]
    rest = jnp.zeros((LANES - PAD, columns), F32)
    left = jnp.concatenate([first, rest], axis=0).T
    right = jnp.concatenate([rest, last], axis=0).T
    grad = sum_ref[...] + jnp.concatenate([left, right], axis=1)
    low = jnp.concatenate(
        [(grad * gate_ref[...]).astype(BF16), (grad * slope_ref[...]).astype(BF16)], axis=0
    )
    model = w_ref.shape[0]
    chunk = 256 if model % 256 == 0 else LANES
    for at in range(0, model, chunk):
        out_ref[at : at + chunk, :] = dot_nn(w_ref[at : at + chunk, :], low).astype(BF16)


def meta_of(ref, columns):
    return ref[3 * columns : 3 * columns + META, :].astype(F32)


def limits(query_meta, key_count, slot):
    lane = lax.broadcasted_iota(jnp.int32, query_meta[0:1].shape, 1).astype(F32)
    valid = lane < query_meta[0:1]
    return [
        jnp.where(valid & (query_meta[1 + 2 * slot + kb : 2 + 2 * slot + kb] > 0.5), key_count, 0.0)
        for kb in range(2)
    ]


def masked(scores, limit_rows):
    rows = scores.shape[0]
    half = rows // 2
    parts = []
    for kb in range(2):
        index = lax.broadcasted_iota(jnp.int32, (half, scores.shape[1]), 0).astype(F32) + kb * half
        parts.append(
            jnp.where(index < limit_rows[kb], scores[kb * half : (kb + 1) * half], NEG)
        )
    return jnp.concatenate(parts, axis=0)


def pieces(value, count):
    found = []
    for _ in range(count):
        low = value.astype(BF16).astype(F32)
        found.append(low)
        value = value - low
    return found


def grad_body(
    columns, w_ref, stream_ref, own_ref, one_ref, far_ref, two_ref, out_ref, tile_out, inverse_out
):
    refs = (own_ref, one_ref, two_ref, far_ref)
    own_meta = meta_of(own_ref, columns)
    lane = lax.broadcasted_iota(jnp.int32, own_meta[0:1].shape, 1).astype(F32)
    valid = lane < own_meta[0:1]
    limit = [limits(own_meta, meta_of(refs[j], columns)[0:1], j) for j in range(LINKS)]
    low = jnp.where(valid, dot_nn(w_ref[...], stream_ref[...]), 0.0).astype(BF16)
    out_ref[0:columns, :] = low
    rows = []
    inverse_out[...] = jnp.zeros(inverse_out.shape, F32)
    for h in range(columns // HEAD_DIM):
        lo, hi = h * HEAD_DIM, (h + 1) * HEAD_DIM
        query = own_ref[2 * columns + lo : 2 * columns + hi, :]
        scores = [
            masked(dot_tn(refs[j][lo:hi, :], query) * SCALE2, limit[j]) for j in range(LINKS)
        ]
        top = functools.reduce(jnp.maximum, [jnp.max(s, axis=0, keepdims=True) for s in scores])
        total = jnp.zeros_like(top)
        mixed = jnp.zeros_like(top)
        for j in range(LINKS):
            expo = jnp.exp2(scores[j] - top)
            dprob = dot_tn(refs[j][columns + lo : columns + hi, :], low[lo:hi])
            tile_out[2 * (LINKS * h + j)] = expo
            tile_out[2 * (LINKS * h + j) + 1] = dprob
            total = total + jnp.sum(expo, axis=0, keepdims=True)
            mixed = mixed + jnp.sum(expo * dprob, axis=0, keepdims=True)
        inverse = jnp.where(valid, 1.0 / total, 0.0)
        inverse_out[h : h + 1, :] = inverse
        delta = mixed * inverse
        rows += pieces(jnp.where(valid, top + jnp.log2(total), -NEG), 3)
        rows += pieces(delta, 2)
    index = lax.broadcasted_iota(jnp.int32, (META, own_meta.shape[1]), 0)
    meta = jnp.zeros((META, own_meta.shape[1]), F32)
    for i, row in enumerate(rows):
        meta = jnp.where(index == i, row, meta)
    out_ref[columns:, :] = meta.astype(BF16)


def stats_of(ref, columns, h):
    meta = ref[columns : columns + META, :].astype(F32)
    at = 5 * h
    lse = (meta[at : at + 1] + meta[at + 1 : at + 2]) + meta[at + 2 : at + 3]
    delta = meta[at + 3 : at + 4] + meta[at + 4 : at + 5]
    return lse, delta


def tile(key, value, query, grad, lse, delta, limit):
    probs = jnp.exp2(masked(dot_tn(key, query) * SCALE2 - lse, limit))
    dscore = (probs * (dot_tn(value, grad) - delta)).astype(BF16)
    return probs.astype(BF16), dscore


def local_body(
    columns,
    own_ref,
    one_ref,
    two_ref,
    far_ref,
    grad_ref,
    tile_ref,
    inverse_ref,
    query_out,
    acc_out,
):
    refs = (own_ref, one_ref, two_ref, far_ref)
    for h in range(columns // HEAD_DIM):
        lo, hi = h * HEAD_DIM, (h + 1) * HEAD_DIM
        grad = grad_ref[lo:hi, :]
        inverse = inverse_ref[h : h + 1, :]
        _, delta = stats_of(grad_ref, columns, h)
        total = jnp.zeros((HEAD_DIM, own_ref.shape[1]), F32)
        for j in range(LINKS):
            probs = tile_ref[2 * (LINKS * h + j)] * inverse
            dscore = (probs * (tile_ref[2 * (LINKS * h + j) + 1] - delta)).astype(BF16)
            total = total + dot_nn(refs[j][lo:hi, :], dscore)
            if j == 0:
                query = own_ref[2 * columns + lo : 2 * columns + hi, :]
                acc_out[lo:hi, :] = dot_nt(query, dscore)
                acc_out[columns + lo : columns + hi, :] = dot_nt(grad, probs.astype(BF16))
        query_out[lo:hi, :] = (total * SCALE).astype(BF16)


def remote_terms(columns, slots, own_ref, span_refs, grad_refs, h):
    lo, hi = h * HEAD_DIM, (h + 1) * HEAD_DIM
    key = own_ref[lo:hi, :]
    value = own_ref[columns + lo : columns + hi, :]
    count = meta_of(own_ref, columns)[0:1]
    key_term = value_term = 0.0
    for slot, span_ref, grad_ref in zip(slots, span_refs, grad_refs):
        query = span_ref[2 * columns + lo : 2 * columns + hi, :]
        grad = grad_ref[lo:hi, :]
        lse, delta = stats_of(grad_ref, columns, h)
        limit = limits(meta_of(span_ref, columns), count, slot)
        probs, dscore = tile(key, value, query, grad, lse, delta, limit)
        key_term = key_term + dot_nt(query, dscore)
        value_term = value_term + dot_nt(grad, probs)
    return key_term, value_term


def middle_body(columns, own_ref, far_ref, grad_far_ref, acc_ref, acc_out):
    for h in range(columns // HEAD_DIM):
        lo, hi = h * HEAD_DIM, (h + 1) * HEAD_DIM
        key_term, value_term = remote_terms(
            columns, (3,), own_ref, (far_ref,), (grad_far_ref,), h
        )
        acc_out[lo:hi, :] = acc_ref[lo:hi, :] + key_term
        acc_out[columns + lo : columns + hi, :] = acc_ref[columns + lo : columns + hi, :] + value_term


def last_body(
    columns, own_ref, one_ref, two_ref, grad_one_ref, grad_two_ref, acc_ref, key_out, value_out
):
    for h in range(columns // HEAD_DIM):
        lo, hi = h * HEAD_DIM, (h + 1) * HEAD_DIM
        key_term, value_term = remote_terms(
            columns, (1, 2), own_ref, (one_ref, two_ref), (grad_one_ref, grad_two_ref), h
        )
        key_out[lo:hi, :] = ((acc_ref[lo:hi, :] + key_term) * SCALE).astype(BF16)
        value_out[lo:hi, :] = (acc_ref[columns + lo : columns + hi, :] + value_term).astype(BF16)


def exchange(value, slot, closed=True):
    count = lax.axis_size("ctx")
    if slot == 3:
        pairs = [(c, (c + count // 2) % count) for c in range(count)]
    else:
        pairs = [(c, (c + (1 if (c + slot) % 2 else -1)) % count) for c in range(count)]
    if not closed:
        pairs = [(i, j) for i, j in pairs if abs(i - j) == 1]
    return lax.ppermute(value, "ctx", pairs)


def per_device(
    g_conv, pre, kernel, w_point, g_out, w_out, queries, keys, values, block_mask, counts
):
    columns, row_count = g_conv.shape
    model = w_point.shape[2]
    groups = lax.axis_size("head")
    shape = jax.ShapeDtypeStruct
    queries, keys, values = (queries.T, keys.T, values.T)
    message = 3 * columns + META
    square = 2 * columns * row_count * row_count

    odd = (lax.axis_index("ctx") % 2).astype(jnp.int32).reshape(1, 1)
    near = [exchange(g_conv, slot, closed=False) for slot in (2, 1)]
    flat = (columns, row_count)
    own, conv, gate, slope = call(
        own_body,
        (shape((message, row_count), BF16),) + (shape(flat, F32),) * 3,
        (
            odd,
            block_mask.transpose(0, 2, 1),
            counts,
            keys,
            values,
            queries,
            g_conv,
            pre,
            kernel,
        ),
        [VMEM] * 9,
        2 * KW * columns * row_count,
        6 * message * row_count,
        columns * row_count,
        (
            pltpu.VMEM((row_count + 2 * PAD, columns), F32),
            pltpu.VMEM((8, row_count + 24, columns), F32),
            pltpu.VMEM((row_count, columns), F32),
        ),
    )
    w_turned = w_point.reshape(2 * columns, model).T
    point_grad = call(
        edge_body,
        shape((model, row_count), BF16),
        (odd, *near, kernel, conv, gate, slope, w_turned),
        [VMEM] * 8,
        4 * columns * model * row_count,
        4 * columns * model,
        0,
        (pltpu.VMEM((2 * PAD, columns), F32), pltpu.VMEM((2 * PAD, columns), F32)),
    )
    parts = lax.all_to_all(
        point_grad.reshape(groups, columns, row_count), "head", 0, 0, tiled=False
    )
    own, _ = lax.optimization_barrier((own, point_grad))
    two, one, far = [exchange(own, slot) for slot in (2, 1, 3)]
    piece = jnp.sum(parts.astype(F32), axis=0)
    stream_grad = (g_out.astype(F32) + piece).astype(BF16)
    stream_full = lax.all_gather(stream_grad, "head", axis=0, tiled=True)
    heads = columns // HEAD_DIM
    tiles = (2 * LINKS * columns // HEAD_DIM, row_count, row_count)
    grad, tile, inverse = call(
        functools.partial(grad_body, columns),
        (shape((columns + META, row_count), BF16), shape(tiles, F32), shape((8, row_count), F32)),
        (w_out, stream_full, own, one, far, two),
        [VMEM] * 6,
        2 * columns * model * row_count + 2 * LINKS * square,
        2 * model * (columns + row_count),
        LINKS * columns // HEAD_DIM * row_count * row_count,
    )
    grad_one, grad_two, grad_far = [exchange(grad, slot) for slot in (1, 2, 3)]
    grad_queries, acc = call(
        functools.partial(local_body, columns),
        (shape((columns, row_count), BF16), shape((2 * columns, row_count), F32)),
        (own, one, two, far, grad, tile, inverse),
        [VMEM] * 7,
        3 * LINKS * square,
        8 * message * row_count,
    )
    acc = call(
        functools.partial(middle_body, columns),
        shape((2 * columns, row_count), F32),
        (own, far, grad_far, acc),
        [VMEM] * 4,
        4 * square,
        6 * message * row_count,
        heads * row_count * row_count,
    )
    grad_keys, grad_values = call(
        functools.partial(last_body, columns),
        (shape(flat, BF16), shape(flat, BF16)),
        (own, one, two, grad_one, grad_two, acc),
        [VMEM] * 6,
        8 * square,
        8 * message * row_count,
        2 * heads * row_count * row_count,
    )
    return (stream_grad.T, grad_queries.T, grad_keys.T, grad_values.T)


def solution(mesh):
    in_specs = (
        P("head", "ctx"),
        P(None, "head", "ctx"),
        P(None, "head"),
        P(None, "head", None),
        P("head", "ctx"),
        P("head", None),
        P("ctx", "head"),
        P("ctx", "head"),
        P("ctx", "head"),
        P("ctx", None, None),
        P("ctx"),
    )
    out_specs = (P("ctx", "head"), P("ctx", "head"), P("ctx", "head"), P("ctx", "head"))
    return jax.shard_map(
        per_device, mesh=mesh, in_specs=in_specs, out_specs=out_specs, check_vma=False
    )
```

```python
import functools
import math

import jax
import jax.numpy as jnp
from jax import lax
from jax.experimental import pallas as pl
from jax.experimental.pallas import tpu as pltpu
from jax.sharding import PartitionSpec as P

HEAD_DIM = 64
KW = 31
LINKS = 4
HALF = 15
LANES = 128
META = 16
PAD = 16
NEG = -1e30
SCALE = 1.0 / math.sqrt(HEAD_DIM)
SCALE2 = SCALE * math.log2(math.e)
VMEM = pl.BlockSpec(memory_space=pltpu.VMEM)
F32 = jnp.float32
BF16 = jnp.bfloat16


def call(body, out_shapes, args, specs, flops, moved, exps=0, scratch=()):
    return pl.pallas_call(
        body,
        out_shape=out_shapes,
        in_specs=specs,
        out_specs=jax.tree.map(lambda _: VMEM, out_shapes),
        scratch_shapes=list(scratch),
        compiler_params=pltpu.CompilerParams(vmem_limit_bytes=24 * 1024 * 1024),
        cost_estimate=pl.CostEstimate(flops=flops, bytes_accessed=moved, transcendentals=exps),
    )(*args)


def dot_tn(a, b):
    return lax.dot_general(a, b, (((0,), (0,)), ((), ())), preferred_element_type=F32)


def dot_nt(a, b):
    return lax.dot_general(a, b, (((1,), (1,)), ((), ())), preferred_element_type=F32)


def dot_nn(a, b):
    return lax.dot_general(a, b, (((1,), (0,)), ((), ())), preferred_element_type=F32)


def own_body(
    odd_ref,
    mask_ref,
    count_ref,
    keys_ref,
    values_ref,
    queries_ref,
    g_ref,
    pre_ref,
    taps_ref,
    out_ref,
    sum_out,
    gate_out,
    slope_out,
    x_ref,
    moved_ref,
    sum_ref,
):
    columns, rows = g_ref.shape
    x_ref[0:PAD, :] = jnp.zeros((PAD, columns), F32)
    x_ref[PAD + rows :, :] = jnp.zeros((PAD, columns), F32)
    x_ref[PAD : PAD + rows, :] = g_ref[...].astype(F32).T
    for shift in range(8):
        moved_ref[shift] = x_ref[shift : shift + rows + 24, :]
    out_ref[0:columns, :] = keys_ref[...]
    out_ref[columns : 2 * columns, :] = values_ref[...]
    out_ref[2 * columns : 3 * columns, :] = queries_ref[...]
    row = lax.broadcasted_iota(jnp.int32, (META, rows), 0)
    first = lax.broadcasted_iota(jnp.int32, (META, rows), 1) < rows // 2
    odd = odd_ref[...] > 0
    meta = jnp.where(row == 0, count_ref[...].astype(F32).reshape(1, 1), 0.0)
    for kb in range(2):
        bits = []
        for qb in range(2):
            given = [
                (mask_ref[qb, kb : kb + 1, j : j + 1] > 0).astype(F32) for j in range(LINKS)
            ]
            own_bit = jnp.ones_like(given[0]) if qb == kb else given[0]
            bits.append(
                (
                    own_bit,
                    jnp.where(odd, given[1], given[2]),
                    jnp.where(odd, given[2], given[1]),
                    given[3],
                )
            )
        for slot in range(LINKS):
            meta = jnp.where(
                row == 1 + 2 * slot + kb, jnp.where(first, bits[0][slot], bits[1][slot]), meta
            )
    out_ref[3 * columns :, :] = meta.astype(BF16)
    step = 32

    def block(i, carry):
        at = pl.multiple_of(i * step, step)
        acc = jnp.zeros((step, columns), F32)
        for k in range(KW):
            a, shift = divmod(PAD + HALF - k, 8)
            acc = acc + taps_ref[k : k + 1, :] * moved_ref[shift, pl.ds(at + 8 * a, step), :]
        sum_ref[pl.ds(at, step), :] = acc
        return carry

    lax.fori_loop(0, rows // step, block, 0, unroll=4)
    sum_out[...] = sum_ref[...].T
    gate = jax.nn.sigmoid(pre_ref[1].astype(F32))
    gate_out[...] = gate
    slope_out[...] = pre_ref[0].astype(F32) * gate * (1.0 - gate)


def edge_body(
    odd_ref, two_ref, one_ref, taps_ref, sum_ref, gate_ref, slope_ref, w_ref, out_ref, head, tail
):
    columns, rows = sum_ref.shape
    odd = jnp.broadcast_to(odd_ref[...] > 0, (columns, LANES))
    before = jnp.where(odd, one_ref[:, rows - LANES :], two_ref[:, rows - LANES :]).astype(F32)
    after = jnp.where(odd, two_ref[:, :LANES], one_ref[:, :LANES]).astype(F32)
    blank = jnp.zeros((PAD, columns), F32)
    head[0:PAD, :] = before.T[LANES - PAD :, :]
    head[PAD:, :] = blank
    tail[0:PAD, :] = blank
    tail[PAD:, :] = after.T[:PAD, :]
    first, last = blank, blank
    for d in range(1, HALF + 1):
        first = first + taps_ref[HALF + d : HALF + d + 1, :] * head[PAD - d : 2 * PAD - d, :]
        last = last + taps_ref[HALF - d : HALF - d + 1, :] * tail[d : PAD + d, :]
    rest = jnp.zeros((LANES - PAD, columns), F32)
    left = jnp.concatenate([first, rest], axis=0).T
    right = jnp.concatenate([rest, last], axis=0).T
    grad = sum_ref[...] + jnp.concatenate([left, right], axis=1)
    low = jnp.concatenate(
        [(grad * gate_ref[...]).astype(BF16), (grad * slope_ref[...]).astype(BF16)], axis=0
    )
    model = w_ref.shape[0]
    chunk = 256 if model % 256 == 0 else LANES
    for at in range(0, model, chunk):
        out_ref[at : at + chunk, :] = dot_nn(w_ref[at : at + chunk, :], low).astype(BF16)


def meta_of(ref, columns):
    return ref[3 * columns : 3 * columns + META, :].astype(F32)


def limits(query_meta, key_count, slot):
    lane = lax.broadcasted_iota(jnp.int32, query_meta[0:1].shape, 1).astype(F32)
    valid = lane < query_meta[0:1]
    return [
        jnp.where(valid & (query_meta[1 + 2 * slot + kb : 2 + 2 * slot + kb] > 0.5), key_count, 0.0)
        for kb in range(2)
    ]


def masked(scores, limit_rows):
    rows = scores.shape[0]
    half = rows // 2
    parts = []
    for kb in range(2):
        index = lax.broadcasted_iota(jnp.int32, (half, scores.shape[1]), 0).astype(F32) + kb * half
        parts.append(
            jnp.where(index < limit_rows[kb], scores[kb * half : (kb + 1) * half], NEG)
        )
    return jnp.concatenate(parts, axis=0)


def pieces(value, count):
    found = []
    for _ in range(count):
        low = value.astype(BF16).astype(F32)
        found.append(low)
        value = value - low
    return found


def grad_body(
    columns, w_ref, stream_ref, own_ref, one_ref, far_ref, two_ref, out_ref, tile_out, inverse_out
):
    refs = (own_ref, one_ref, two_ref, far_ref)
    own_meta = meta_of(own_ref, columns)
    lane = lax.broadcasted_iota(jnp.int32, own_meta[0:1].shape, 1).astype(F32)
    valid = lane < own_meta[0:1]
    limit = [limits(own_meta, meta_of(refs[j], columns)[0:1], j) for j in range(LINKS)]
    low = jnp.where(valid, dot_nn(w_ref[...], stream_ref[...]), 0.0).astype(BF16)
    out_ref[0:columns, :] = low
    rows = []
    inverse_out[...] = jnp.zeros(inverse_out.shape, F32)
    for h in range(columns // HEAD_DIM):
        lo, hi = h * HEAD_DIM, (h + 1) * HEAD_DIM
        query = own_ref[2 * columns + lo : 2 * columns + hi, :]
        scores = [
            masked(dot_tn(refs[j][lo:hi, :], query) * SCALE2, limit[j]) for j in range(LINKS)
        ]
        top = functools.reduce(jnp.maximum, [jnp.max(s, axis=0, keepdims=True) for s in scores])
        total = jnp.zeros_like(top)
        mixed = jnp.zeros_like(top)
        for j in range(LINKS):
            expo = jnp.exp2(scores[j] - top)
            dprob = dot_tn(refs[j][columns + lo : columns + hi, :], low[lo:hi])
            tile_out[2 * (LINKS * h + j)] = expo
            tile_out[2 * (LINKS * h + j) + 1] = dprob
            total = total + jnp.sum(expo, axis=0, keepdims=True)
            mixed = mixed + jnp.sum(expo * dprob, axis=0, keepdims=True)
        inverse = jnp.where(valid, 1.0 / total, 0.0)
        inverse_out[h : h + 1, :] = inverse
        delta = mixed * inverse
        rows += pieces(jnp.where(valid, top + jnp.log2(total), -NEG), 3)
        rows += pieces(delta, 2)
    index = lax.broadcasted_iota(jnp.int32, (META, own_meta.shape[1]), 0)
    meta = jnp.zeros((META, own_meta.shape[1]), F32)
    for i, row in enumerate(rows):
        meta = jnp.where(index == i, row, meta)
    out_ref[columns:, :] = meta.astype(BF16)


def stats_of(ref, columns, h):
    meta = ref[columns : columns + META, :].astype(F32)
    at = 5 * h
    lse = (meta[at : at + 1] + meta[at + 1 : at + 2]) + meta[at + 2 : at + 3]
    delta = meta[at + 3 : at + 4] + meta[at + 4 : at + 5]
    return lse, delta


def tile(key, value, query, grad, lse, delta, limit):
    probs = jnp.exp2(masked(dot_tn(key, query) * SCALE2 - lse, limit))
    dscore = (probs * (dot_tn(value, grad) - delta)).astype(BF16)
    return probs.astype(BF16), dscore


def local_body(
    columns,
    own_ref,
    one_ref,
    two_ref,
    far_ref,
    grad_ref,
    tile_ref,
    inverse_ref,
    query_out,
    acc_out,
):
    refs = (own_ref, one_ref, two_ref, far_ref)
    for h in range(columns // HEAD_DIM):
        lo, hi = h * HEAD_DIM, (h + 1) * HEAD_DIM
        grad = grad_ref[lo:hi, :]
        inverse = inverse_ref[h : h + 1, :]
        _, delta = stats_of(grad_ref, columns, h)
        total = jnp.zeros((HEAD_DIM, own_ref.shape[1]), F32)
        for j in range(LINKS):
            probs = tile_ref[2 * (LINKS * h + j)] * inverse
            dscore = (probs * (tile_ref[2 * (LINKS * h + j) + 1] - delta)).astype(BF16)
            total = total + dot_nn(refs[j][lo:hi, :], dscore)
            if j == 0:
                query = own_ref[2 * columns + lo : 2 * columns + hi, :]
                acc_out[lo:hi, :] = dot_nt(query, dscore)
                acc_out[columns + lo : columns + hi, :] = dot_nt(grad, probs.astype(BF16))
        query_out[lo:hi, :] = (total * SCALE).astype(BF16)


def remote_terms(columns, slots, own_ref, span_refs, grad_refs, h):
    lo, hi = h * HEAD_DIM, (h + 1) * HEAD_DIM
    key = own_ref[lo:hi, :]
    value = own_ref[columns + lo : columns + hi, :]
    count = meta_of(own_ref, columns)[0:1]
    key_term = value_term = 0.0
    for slot, span_ref, grad_ref in zip(slots, span_refs, grad_refs):
        query = span_ref[2 * columns + lo : 2 * columns + hi, :]
        grad = grad_ref[lo:hi, :]
        lse, delta = stats_of(grad_ref, columns, h)
        limit = limits(meta_of(span_ref, columns), count, slot)
        probs, dscore = tile(key, value, query, grad, lse, delta, limit)
        key_term = key_term + dot_nt(query, dscore)
        value_term = value_term + dot_nt(grad, probs)
    return key_term, value_term


def middle_body(columns, own_ref, far_ref, grad_far_ref, acc_ref, acc_out):
    for h in range(columns // HEAD_DIM):
        lo, hi = h * HEAD_DIM, (h + 1) * HEAD_DIM
        key_term, value_term = remote_terms(
            columns, (3,), own_ref, (far_ref,), (grad_far_ref,), h
        )
        acc_out[lo:hi, :] = acc_ref[lo:hi, :] + key_term
        acc_out[columns + lo : columns + hi, :] = acc_ref[columns + lo : columns + hi, :] + value_term


def last_body(
    columns, own_ref, one_ref, two_ref, grad_one_ref, grad_two_ref, acc_ref, key_out, value_out
):
    for h in range(columns // HEAD_DIM):
        lo, hi = h * HEAD_DIM, (h + 1) * HEAD_DIM
        key_term, value_term = remote_terms(
            columns, (1, 2), own_ref, (one_ref, two_ref), (grad_one_ref, grad_two_ref), h
        )
        key_out[lo:hi, :] = ((acc_ref[lo:hi, :] + key_term) * SCALE).astype(BF16)
        value_out[lo:hi, :] = (acc_ref[columns + lo : columns + hi, :] + value_term).astype(BF16)


def exchange(value, slot, closed=True):
    count = lax.axis_size("ctx")
    if slot == 3:
        pairs = [(c, (c + count // 2) % count) for c in range(count)]
    else:
        pairs = [(c, (c + (1 if (c + slot) % 2 else -1)) % count) for c in range(count)]
    if not closed:
        pairs = [(i, j) for i, j in pairs if abs(i - j) == 1]
    return lax.ppermute(value, "ctx", pairs)


def per_device(
    g_conv, pre, kernel, w_point, g_out, w_out, queries, keys, values, block_mask, counts
):
    columns, row_count = g_conv.shape
    model = w_point.shape[2]
    groups = lax.axis_size("head")
    shape = jax.ShapeDtypeStruct
    queries, keys, values = (queries.T, keys.T, values.T)
    message = 3 * columns + META
    square = 2 * columns * row_count * row_count

    odd = (lax.axis_index("ctx") % 2).astype(jnp.int32).reshape(1, 1)
    near = [exchange(g_conv, slot, closed=False) for slot in (2, 1)]
    flat = (columns, row_count)
    own, conv, gate, slope = call(
        own_body,
        (shape((message, row_count), BF16),) + (shape(flat, F32),) * 3,
        (
            odd,
            block_mask.transpose(0, 2, 1),
            counts,
            keys,
            values,
            queries,
            g_conv,
            pre,
            kernel,
        ),
        [VMEM] * 9,
        2 * KW * columns * row_count,
        6 * message * row_count,
        columns * row_count,
        (
            pltpu.VMEM((row_count + 2 * PAD, columns), F32),
            pltpu.VMEM((8, row_count + 24, columns), F32),
            pltpu.VMEM((row_count, columns), F32),
        ),
    )
    w_turned = w_point.reshape(2 * columns, model).T
    point_grad = call(
        edge_body,
        shape((model, row_count), BF16),
        (odd, *near, kernel, conv, gate, slope, w_turned),
        [VMEM] * 8,
        4 * columns * model * row_count,
        4 * columns * model,
        0,
        (pltpu.VMEM((2 * PAD, columns), F32), pltpu.VMEM((2 * PAD, columns), F32)),
    )
    parts = lax.all_to_all(
        point_grad.reshape(groups, columns, row_count), "head", 0, 0, tiled=False
    )
    own, _ = lax.optimization_barrier((own, point_grad))
    two, one, far = [exchange(own, slot) for slot in (2, 1, 3)]
    piece = jnp.sum(parts.astype(F32), axis=0)
    stream_grad = (g_out.astype(F32) + piece).astype(BF16)
    stream_full = lax.all_gather(stream_grad, "head", axis=0, tiled=True)
    heads = columns // HEAD_DIM
    tiles = (2 * LINKS * columns // HEAD_DIM, row_count, row_count)
    grad, tile, inverse = call(
        functools.partial(grad_body, columns),
        (shape((columns + META, row_count), BF16), shape(tiles, F32), shape((8, row_count), F32)),
        (w_out, stream_full, own, one, far, two),
        [VMEM] * 6,
        2 * columns * model * row_count + 2 * LINKS * square,
        2 * model * (columns + row_count),
        LINKS * columns // HEAD_DIM * row_count * row_count,
    )
    grad_one, grad_two, grad_far = [exchange(grad, slot) for slot in (1, 2, 3)]
    grad_queries, acc = call(
        functools.partial(local_body, columns),
        (shape((columns, row_count), BF16), shape((2 * columns, row_count), F32)),
        (own, one, two, far, grad, tile, inverse),
        [VMEM] * 7,
        3 * LINKS * square,
        8 * message * row_count,
    )
    acc = call(
        functools.partial(middle_body, columns),
        shape((2 * columns, row_count), F32),
        (own, far, grad_far, acc),
        [VMEM] * 4,
        4 * square,
        6 * message * row_count,
        heads * row_count * row_count,
    )
    grad_keys, grad_values = call(
        functools.partial(last_body, columns),
        (shape(flat, BF16), shape(flat, BF16)),
        (own, one, two, grad_one, grad_two, acc),
        [VMEM] * 6,
        8 * square,
        8 * message * row_count,
        2 * heads * row_count * row_count,
    )
    return (stream_grad.T, grad_queries.T, grad_keys.T, grad_values.T)


def solution(mesh):
    in_specs = (
        P("head", "ctx"),
        P(None, "head", "ctx"),
        P(None, "head"),
        P(None, "head", None),
        P("head", "ctx"),
        P("head", None),
        P("ctx", "head"),
        P("ctx", "head"),
        P("ctx", "head"),
        P("ctx", None, None),
        P("ctx"),
    )
    out_specs = (P("ctx", "head"), P("ctx", "head"), P("ctx", "head"), P("ctx", "head"))
    return jax.shard_map(
        per_device, mesh=mesh, in_specs=in_specs, out_specs=out_specs, check_vma=False
    )
```
